32 devices in a mesh: mode: 4 (over y, core), gx: 2 (over x), gy: 4 (over z).
Axes of the slice: x: 2, y: 2, z: 4, core: 2. Of those that a mesh axis runs over, the one named last changes fastest.
Arguments:
- right_side: float32 [16, 32, 7168], P('gx', 'gy', 'mode'), may hold values from -6 to 6
- col_block: int32 [56, 8], P('mode'), may hold values from 0 to 55, as said below
- blocks: bfloat16 [56, 8, 128, 128], P('mode'), may hold values from -0.1875 to 0.1875
- relax_rate: float32 [7168], P('mode'), may hold values from 0.5 to 4
- drift_speed: float32 [2, 7168], P(None, 'mode'), may hold values from 0.3 to 1.5
- upwind_sign: int32 [2, 7168], P(None, 'mode'), may hold values from 0 to 1
- wall_mask: int32 [16, 32], P('gx', 'gy'), may hold values 0 or 1
Outputs:
- solution: float32 [16, 32, 7168], P('gx', 'gy', 'mode')
- hessenberg: float32 [4, 3], replicated
The draws below stay inside these ranges and needn't reach their ends.
Inputs may be any that keep to these rules, and one draw needn't show every extreme that they name: `col_block`: for every block row and every o in 0 .. 3, slots o * 2 to (o + 1) * 2 - 1 hold distinct column blocks of o * 14 to (o + 1) * 14 - 1.
All inputs are finite; a program needn't handle non-finite values. No bound on the sum of `wall_mask` on one device may be relied on, other than what follows from the above.
Results may differ from the reference program's by a relative error of at most 0.00081.
Values may be sent and summed in bfloat16 or wider, within the bound.
No kernel may reach another device: no remote copies, remote signals or barrier semaphores. Data moves between devices by JAX's collectives and lax.ppermute only.
A program may use at most 128 MiB of HBM per device.

```python
import math
import jax
import jax.numpy as jnp
from jax import lax

BLOCK = 128
MB_DEV = 14
PER_OWNER = 2
KRYLOV = 3
MODE_BLOCKS = 56
MODES = 7168
NNZ = 8
NX = 16
NY = 32


def draw_col_block(key, part):
    owners = MODE_BLOCKS // MB_DEV
    scores = jax.random.randint(key, (MODE_BLOCKS, owners, MB_DEV), 0, 1 << 20)
    scores = scores * MB_DEV + jnp.arange(MB_DEV, dtype=jnp.int32)
    order = jnp.argsort(scores, axis=-1, stable=True)[:, :, :PER_OWNER]
    shifted = order + (jnp.arange(owners, dtype=jnp.int32) * MB_DEV)[None, :, None]
    return shifted.reshape(MODE_BLOCKS, owners * PER_OWNER).astype(jnp.int32)


def place_ends(values, key, smallest, largest):
    dims = values.shape
    spot = [jax.random.randint(jax.random.fold_in(key, axis), (), 0, dims[axis]) for axis in range(len(dims))]
    values = values.at[tuple(spot)].set(smallest)
    longest = dims.index(max(dims))
    spot[longest] = (spot[longest] + 1) % dims[longest]
    return values.at[tuple(spot)].set(largest)


def shard_levels(own_key, shape, cuts, low, high):
    def one(axis_at, parts):
        steps = jax.random.uniform(jax.random.fold_in(jax.random.fold_in(own_key, 6), axis_at), (parts,), jnp.float32, low / len(cuts), high / len(cuts))
        return jnp.repeat(jnp.exp(steps), shape[axis_at] // parts).reshape((-1,) + (1,) * (len(shape) - axis_at - 1))

    loudness = one(*cuts[0])
    for cut in cuts[1:]:
        loudness = loudness * one(*cut)
    return loudness


def scatter_about(stream_key, shape, deviation, most, pieces=(), kind=jnp.bfloat16):
    gain = shard_levels(stream_key, shape, pieces, -0.22, 0.18) if pieces else 1.0
    result = jax.random.normal(stream_key, shape, jnp.float32) * deviation * gain
    return jnp.minimum(jnp.maximum(result, -most), most).astype(kind)


def setup_inputs(seed: int = 0) -> dict:
    key_of = jax.random.split(jax.random.key(seed), 8)
    return {
        "right_side": scatter_about(key_of[0], (NX, NY, MODES), 1.0, 6.0, ((0, 2), (1, 4), (2, 4)), jnp.float32),
        "col_block": draw_col_block(jax.random.fold_in(key_of[7], 71), 0),
        "blocks": scatter_about(key_of[2], (MODE_BLOCKS, NNZ, BLOCK, BLOCK), (NNZ * BLOCK) ** -0.5, 0.1875, ((0, 4),)),
        "relax_rate": jnp.clip(jnp.exp(math.log(4.0) - 2.0794415 * jax.random.uniform(key_of[3], (MODES,), jnp.float32) ** shard_levels(key_of[3], (MODES,), ((0, 4),), -0.2, 0.2)), 0.5, 4.0),
        "drift_speed": jnp.clip(jnp.exp(math.log(1.5) - 1.60943787 * jax.random.uniform(key_of[4], (2, MODES), jnp.float32) ** shard_levels(key_of[4], (2, MODES), ((1, 4),), -0.2, 0.2)), 0.3, 1.5),
        "upwind_sign": place_ends(jax.random.randint(key_of[5], (2, MODES), 0, 2), jax.random.fold_in(key_of[5], 1), 0, 1).astype(jnp.int32),
        "wall_mask": place_ends((jax.random.randint(key_of[6], (NX, NY), 0, 8) < 1).astype(jnp.int32), jax.random.fold_in(key_of[6], 1), 0, 1),
    }


epsilon = 1e-12

def apply_operator(current, col_block, blocks, relax_rate, drift_speed, upwind_sign, open_cells):
    masked = current * open_cells[:, :, None]
    padded = jnp.pad(masked, ((1, 1), (1, 1), (0, 0)))
    from_west = padded[:-2, 1:-1]
    from_east = padded[2:, 1:-1]
    from_south = padded[1:-1, :-2]
    from_north = padded[1:-1, 2:]
    upstream_first = jnp.where(upwind_sign[0] == 1, from_west, from_east)
    upstream_second = jnp.where(upwind_sign[1] == 1, from_south, from_north)
    drift_term = drift_speed[0] * (current - upstream_first) + drift_speed[1] * (current - upstream_second)
    rounded = current.astype(jnp.bfloat16).reshape(NX * NY, MODE_BLOCKS, BLOCK)

    def block_row(pair):
        columns, weights = pair
        picked = jnp.take(rounded, columns, axis=1).astype(jnp.float32)
        return jnp.einsum('sik,csk->ci', weights.astype(jnp.float32), picked, precision=lax.Precision.HIGHEST)
    scattered = lax.map(block_row, (col_block, blocks))
    scattered = jnp.transpose(scattered, (1, 0, 2)).reshape(NX, NY, MODES)
    return relax_rate * current + drift_term - scattered

def least_squares(hessenberg, initial):
    upper = [[hessenberg[row_index, col_index] for col_index in range(KRYLOV)] for row_index in range(KRYLOV + 1)]
    target = [initial] + [jnp.zeros_like(initial) for row_index in range(KRYLOV)]
    cosines = []
    sines = []
    for col_index in range(KRYLOV):
        for row_index in range(col_index):
            first = upper[row_index][col_index]
            second = upper[row_index + 1][col_index]
            upper[row_index][col_index] = cosines[row_index] * first + sines[row_index] * second
            upper[row_index + 1][col_index] = cosines[row_index] * second - sines[row_index] * first
        first = upper[col_index][col_index]
        second = upper[col_index + 1][col_index]
        radius = jnp.sqrt(first * first + second * second)
        cosine = first / radius
        sine_value = second / radius
        upper[col_index][col_index] = radius
        target[col_index + 1] = -sine_value * target[col_index]
        target[col_index] = cosine * target[col_index]
        cosines.append(cosine)
        sines.append(sine_value)
    combo = [None] * KRYLOV
    for row_index in reversed(range(KRYLOV)):
        running = target[row_index]
        for col_index in range(row_index + 1, KRYLOV):
            running = running - upper[row_index][col_index] * combo[col_index]
        combo[row_index] = running / upper[row_index][row_index]
    return combo

def reference(right_side, col_block, blocks, relax_rate, drift_speed, upwind_sign, wall_mask):
    open_cells = (1 - wall_mask).astype(jnp.float32)
    initial = jnp.sqrt(jnp.sum(right_side * right_side) + epsilon)
    krylov_basis = [right_side / initial]
    columns_list = []
    for section in range(KRYLOV):
        mapped = apply_operator(krylov_basis[section], col_block, blocks, relax_rate, drift_speed, upwind_sign, open_cells)
        coefficients = [jnp.sum(krylov_basis[earlier] * mapped) for earlier in range(section + 1)]
        remainder = mapped
        for earlier in range(section + 1):
            remainder = remainder - coefficients[earlier] * krylov_basis[earlier]
        length = jnp.sqrt(jnp.sum(remainder * remainder) + epsilon)
        krylov_basis.append(remainder / length)
        entries = coefficients + [length] + [jnp.zeros_like(length) for later in range(KRYLOV - section - 1)]
        columns_list.append(jnp.stack(entries))
    hessenberg = jnp.stack(columns_list, axis=1)
    combo = least_squares(hessenberg, initial)
    solution = jnp.zeros_like(right_side)
    for section in range(KRYLOV):
        solution = solution + combo[section] * krylov_basis[section]
    return (solution, hessenberg)
```

```python
import functools

import jax
import jax.numpy as jnp
from jax import lax
from jax.experimental import pallas as pl
from jax.experimental.pallas import tpu as pltpu
from jax.sharding import PartitionSpec as P

KRYLOV = 3
ENTRIES = 16
TAIL = 16
AXES = ("mode", "gx", "gy")

epsilon = 1e-12


def pair_list(count, first):
    pairs = []
    for low in range(first, count - 1, 2):
        pairs += [(low, low + 1), (low + 1, low)]
    return pairs


def swaps_of(count):
    return [pairs for pairs in (pair_list(count, 0), pair_list(count, 1)) if pairs]


def face_swaps(faces):
    received = []
    for axis in ("gx", "gy"):
        swaps = swaps_of(lax.axis_size(axis))
        received.append(
            [lax.ppermute(face, axis, pairs) for face, pairs in zip(faces[axis], swaps)]
        )
    return received


def gather_modes(packed):
    count = lax.axis_size("mode")
    held = {0: packed}
    bit = count // 2
    while bit:
        for key in list(held):
            held[key ^ bit] = lax.ppermute(
                held[key], "mode", [(i, i ^ bit) for i in range(count)]
            )
        bit //= 2
    return [held[key] for key in range(count)]


def write_faces(masked, lanes, first, second, x_refs, y_refs):
    if x_refs:
        even = lax.rem(lax.axis_index("gx"), 2) == 0
        low, high = masked[0], masked[first - 1]
        for ref, take_high in zip(x_refs, (even, jnp.logical_not(even))):
            ref[:, lanes] = jnp.where(take_high, high, low)
    if y_refs:
        even = lax.rem(lax.axis_index("gy"), 2) == 0
        low, high = masked[:, 0, :], masked[:, second - 1, :]
        for ref, take_high in zip(y_refs, (even, jnp.logical_not(even))):
            ref[:, lanes] = jnp.where(take_high, high, low)


def halos(refs, axis, lanes, shape):
    zero = jnp.zeros(shape, jnp.float32)
    values = [ref[:, lanes] for ref in refs] + [zero, zero]
    odd = lax.rem(lax.axis_index(axis), 2) == 1
    return jnp.where(odd, values[0], values[1]), jnp.where(odd, values[1], values[0])


def prepare_kernel(sizes, refs_in, x_refs, y_refs, packed_ref, open_ref):
    first, second, local_blocks, block = sizes
    rhs_ref, relax_ref, speed_ref, wall_ref = refs_in
    cells = first * second
    wall = wall_ref[...].astype(jnp.float32)
    eye = (
        lax.broadcasted_iota(jnp.int32, (second, second), 0)
        == lax.broadcasted_iota(jnp.int32, (second, second), 1)
    ).astype(jnp.float32)
    for row in range(first):
        column = jnp.sum(eye * (1.0 - wall[row : row + 1, :]), axis=1, keepdims=True)
        open_ref[row * second : (row + 1) * second, :] = jnp.broadcast_to(column, (second, block))
    total = jnp.zeros((1, block), jnp.float32)
    for b in range(local_blocks):
        lanes = slice(b * block, (b + 1) * block)
        value = rhs_ref[:, lanes]
        packed_ref[b * cells : (b + 1) * cells, :] = value.astype(jnp.bfloat16)
        masked = (value * open_ref[...]).reshape(first, second, block)
        write_faces(masked, lanes, first, second, x_refs, y_refs)
        total += relax_ref[:, lanes] + speed_ref[0:1, lanes] + speed_ref[1:2, lanes]
    mean = jnp.sum(total, axis=1, keepdims=True) * (1.0 / (local_blocks * block))
    packed_ref[local_blocks * cells :, :] = jnp.broadcast_to(mean, (TAIL, block)).astype(
        jnp.bfloat16
    )


def shift_of(sources, owners, tail_at):
    rows = [ref[tail_at : tail_at + TAIL, :].astype(jnp.float32)[0:1] for ref in sources]
    total = jnp.zeros_like(rows[0])
    for owner in range(len(sources)):
        term = rows[0]
        for place in range(1, len(sources)):
            term = jnp.where(owners[place] == owner, rows[place], term)
        total = total + term
    return total * (1.0 / len(sources))


def step_kernel(sizes, per_owner, last, cols_ref, sources, blocks_ref, earlier, params, x_in, y_in, outs):
    first, second, local_blocks, block = sizes
    relax_ref, speed_ref, sign_ref, open_ref = params
    cells = first * second
    count = len(sources)
    mine = lax.axis_index("mode")
    owners = [mine ^ place for place in range(count)]
    shift = shift_of(sources[: count], owners, local_blocks * cells) if outs.shift_in is None else outs.shift_in[...]
    if outs.shift is not None:
        outs.shift[...] = shift
    open_cells = open_ref[...]
    current_ref = earlier[-1]
    row_at = lax.broadcasted_iota(jnp.int32, (first, second, block), 1)
    sums = {}
    for b in range(local_blocks):
        lanes = slice(b * block, (b + 1) * block)
        picks, weights = [], []
        for place in range(count):
            for p in range(per_owner):
                slot = owners[place] * per_owner + p
                column = cols_ref[b, slot] - owners[place] * local_blocks
                picks.append(sources[place][pl.ds(pl.multiple_of(column * cells, cells), cells), :])
                weights.append(blocks_ref[b, slot])
        scattered = lax.dot_general(
            jnp.concatenate(picks, axis=1),
            jnp.concatenate(weights, axis=1),
            (((1,), (1,)), ((), ())),
            preferred_element_type=jnp.float32,
        )
        current = current_ref[:, lanes]
        masked = (current * open_cells).reshape(first, second, block)
        west_in, east_in = halos(x_in, "gx", lanes, (second, block))
        south_in, north_in = halos(y_in, "gy", lanes, (first, block))
        from_west = jnp.concatenate([west_in[None], masked[:-1]], axis=0)
        from_east = jnp.concatenate([masked[1:], east_in[None]], axis=0)
        from_south = jnp.where(
            row_at == 0, south_in[:, None, :], pltpu.roll(masked, 1, axis=1)
        )
        from_north = jnp.where(
            row_at == second - 1, north_in[:, None, :], pltpu.roll(masked, second - 1, axis=1)
        )
        sign_x = sign_ref[0:1, lanes].reshape(1, 1, block)
        sign_y = sign_ref[1:2, lanes].reshape(1, 1, block)
        speed_x, speed_y = speed_ref[0:1, lanes], speed_ref[1:2, lanes]
        upstream_x = jnp.where(sign_x == 1, from_west, from_east).reshape(cells, block)
        upstream_y = jnp.where(sign_y == 1, from_south, from_north).reshape(cells, block)
        diagonal = relax_ref[:, lanes] + speed_x + speed_y - shift
        result = diagonal * current - speed_x * upstream_x - speed_y * upstream_y - scattered
        if not last:
            outs.value[:, lanes] = result
            outs.packed[b * cells : (b + 1) * cells, :] = result.astype(jnp.bfloat16)
            write_faces(
                (result * open_cells).reshape(first, second, block),
                lanes, first, second, outs.x, outs.y,
            )
        else:
            vectors = [ref[:, lanes] for ref in earlier] + [result]
            at = 0
            for i in range(len(vectors)):
                for j in range(i, len(vectors)):
                    term = jnp.sum((vectors[i] * vectors[j]).reshape(cells // 8, 8, block), axis=0)
                    sums[at] = term if b == 0 else sums[at] + term
                    at += 1
    if last:
        devices = outs.gram.shape[0]
        for at, value in sums.items():
            total = jnp.sum(jnp.sum(value, axis=0, keepdims=True), axis=1, keepdims=True)
            outs.gram[:, at : at + 1, :] = jnp.broadcast_to(
                total.reshape(1, 1, 1), (devices, 1, block)
            )
        left = outs.gram.shape[1] - len(sums)
        outs.gram[:, len(sums) :, :] = jnp.zeros((devices, left, block), jnp.float32)
    elif outs.packed.shape[0] > local_blocks * cells:
        outs.packed[local_blocks * cells :, :] = jnp.zeros((TAIL, block), jnp.bfloat16)


class Outs:
    value = packed = gram = shift = shift_in = None
    x = y = ()


def least_squares(hessenberg, initial):
    upper = [list(row) for row in hessenberg]
    target = [initial] + [jnp.zeros_like(initial) for row_index in range(KRYLOV)]
    cosines = []
    sines = []
    for col_index in range(KRYLOV):
        for row_index in range(col_index):
            first = upper[row_index][col_index]
            second = upper[row_index + 1][col_index]
            upper[row_index][col_index] = cosines[row_index] * first + sines[row_index] * second
            upper[row_index + 1][col_index] = cosines[row_index] * second - sines[row_index] * first
        first = upper[col_index][col_index]
        second = upper[col_index + 1][col_index]
        radius = jnp.sqrt(first * first + second * second)
        cosine = first / radius
        sine_value = second / radius
        upper[col_index][col_index] = radius
        target[col_index + 1] = -sine_value * target[col_index]
        target[col_index] = cosine * target[col_index]
        cosines.append(cosine)
        sines.append(sine_value)
    combo = [None] * KRYLOV
    for row_index in reversed(range(KRYLOV)):
        running = target[row_index]
        for col_index in range(row_index + 1, KRYLOV):
            running = running - upper[row_index][col_index] * combo[col_index]
        combo[row_index] = running / upper[row_index][row_index]
    return combo


def arnoldi(gram, shift):
    size = KRYLOV + 1

    def inner(left, right):
        total = None
        for i in range(size):
            for j in range(size):
                if left[i] is None or right[j] is None:
                    continue
                term = left[i] * right[j] * gram[min(i, j)][max(i, j)]
                total = term if total is None else total + term
        return total

    initial = jnp.sqrt(gram[0][0] + epsilon)
    basis = [[1.0 / initial] + [None] * KRYLOV]
    zero = jnp.zeros_like(initial)
    hessenberg = [[zero] * KRYLOV for row_index in range(size)]
    for section in range(KRYLOV):
        vector = basis[section]
        image = [None] * size
        for k in range(section + 2):
            parts = []
            if k > 0 and vector[k - 1] is not None:
                parts.append(vector[k - 1])
            if vector[k] is not None:
                parts.append(shift * vector[k])
            image[k] = sum(parts[1:], parts[0])
        rest = list(image)
        for earlier in range(section + 1):
            coefficient = inner(basis[earlier], image)
            hessenberg[earlier][section] = coefficient
            for k in range(earlier + 1):
                rest[k] = rest[k] - coefficient * basis[earlier][k]
        length = jnp.sqrt(jnp.maximum(inner(rest, rest), 0.0) + epsilon)
        hessenberg[section + 1][section] = length
        basis.append([None if part is None else part / length for part in rest])
    combo = least_squares(hessenberg, initial)
    weights = []
    for k in range(KRYLOV):
        total = zero
        for j in range(k, KRYLOV):
            total = total + combo[j] * basis[j][k]
        weights.append(total)
    return hessenberg, weights


def finish_kernel(gram_ref, shift_ref, *refs):
    vectors, (solution_ref, hessenberg_ref) = refs[:KRYLOV], refs[KRYLOV:]
    total = jnp.sum(gram_ref[...], axis=0)
    gram = [[None] * (KRYLOV + 1) for i in range(KRYLOV + 1)]
    at = 0
    for i in range(KRYLOV + 1):
        for j in range(i, KRYLOV + 1):
            gram[i][j] = total[at : at + 1, :]
            at += 1
    hessenberg, weights = arnoldi(gram, shift_ref[...])
    rows = lax.broadcasted_iota(jnp.int32, (KRYLOV + 1, KRYLOV), 0)
    cols = lax.broadcasted_iota(jnp.int32, (KRYLOV + 1, KRYLOV), 1)
    table = jnp.zeros((KRYLOV + 1, KRYLOV), jnp.float32)
    for i in range(KRYLOV + 1):
        for j in range(KRYLOV):
            table = jnp.where((rows == i) & (cols == j), hessenberg[i][j][:, :KRYLOV], table)
    hessenberg_ref[...] = table
    block = shift_ref.shape[1]
    for b in range(solution_ref.shape[1] // block):
        lanes = slice(b * block, (b + 1) * block)
        solution_ref[:, lanes] = sum(
            weight * ref[:, lanes] for weight, ref in zip(weights, vectors)
        )


VMEM = pl.BlockSpec(memory_space=pltpu.VMEM)
SMEM = pl.BlockSpec(memory_space=pltpu.SMEM)


def per_device(right_side, col_block, blocks, relax_rate, drift_speed, upwind_sign, wall_mask):
    first, second, local_modes = right_side.shape
    local_blocks, slots, block = blocks.shape[:3]
    cells = first * second
    count = lax.axis_size("mode")
    devices = count * lax.axis_size("gx") * lax.axis_size("gy")
    sizes = (first, second, local_blocks, block)
    x_swaps, y_swaps = len(swaps_of(lax.axis_size("gx"))), len(swaps_of(lax.axis_size("gy")))
    f32 = jnp.float32
    face_shapes = [jax.ShapeDtypeStruct((second, local_modes), f32)] * x_swaps + [
        jax.ShapeDtypeStruct((first, local_modes), f32)
    ] * y_swaps
    packed_rows = local_blocks * cells + TAIL
    packed_shape = jax.ShapeDtypeStruct((packed_rows, block), jnp.bfloat16)
    vector_shape = jax.ShapeDtypeStruct((cells, local_modes), f32)
    shift_shape = jax.ShapeDtypeStruct((1, block), f32)
    n_faces = x_swaps + y_swaps
    limit = pltpu.CompilerParams(vmem_limit_bytes=32 * 1024 * 1024)

    start = right_side.reshape(cells, local_modes)
    relax = relax_rate.reshape(1, local_modes)

    def prepare(*refs):
        faces, (packed_ref, open_ref) = refs[4 : 4 + n_faces], refs[4 + n_faces :]
        prepare_kernel(
            sizes, refs[:4], faces[:x_swaps], faces[x_swaps:], packed_ref, open_ref
        )

    *faces, packed, open_cells = pl.pallas_call(
        prepare,
        out_shape=face_shapes + [packed_shape, jax.ShapeDtypeStruct((cells, block), f32)],
        in_specs=[VMEM] * 4,
        out_specs=[VMEM] * (n_faces + 2),
        compiler_params=limit,
        name="prepare",
    )(start, relax, drift_speed, wall_mask)

    vectors = [start]
    shift = None
    for section in range(KRYLOV):
        last = section == KRYLOV - 1
        sources = gather_modes(packed)
        x_in, y_in = face_swaps({"gx": faces[:x_swaps], "gy": faces[x_swaps:]})
        n_before = len(vectors)

        def step(*refs, last=last, n_before=n_before, has_shift=shift is not None):
            refs = list(refs)

            def take(number):
                taken = refs[:number]
                del refs[:number]
                return taken

            (cols_ref,) = take(1)
            source_refs = take(count)
            (blocks_ref,) = take(1)
            earlier = take(n_before)
            params = take(4)
            x_refs, y_refs = take(x_swaps), take(y_swaps)
            outs = Outs()
            if has_shift:
                (outs.shift_in,) = take(1)
            if last:
                (outs.gram,) = take(1)
            else:
                outs.x, outs.y = take(x_swaps), take(y_swaps)
                outs.packed, outs.value = take(2)
            if not has_shift:
                (outs.shift,) = take(1)
            step_kernel(
                sizes, slots // count, last, cols_ref, source_refs, blocks_ref, earlier, params,
                x_refs, y_refs, outs,
            )

        operands = [col_block, *sources, blocks, *vectors, relax, drift_speed, upwind_sign,
                    open_cells, *x_in, *y_in]
        if shift is not None:
            operands.append(shift)
        if last:
            shapes = [jax.ShapeDtypeStruct((devices, ENTRIES, block), f32)]
        else:
            shapes = face_shapes + [packed_shape, vector_shape]
        if shift is None:
            shapes = shapes + [shift_shape]
        results = pl.pallas_call(
            step,
            out_shape=shapes,
            in_specs=[SMEM] + [VMEM] * (len(operands) - 1),
            out_specs=[VMEM] * len(shapes),
            compiler_params=limit,
            name="step_%d" % section,
        )(*operands)
        if shift is None:
            *results, shift = results
        if last:
            (gram,) = results
        else:
            *faces, packed, value = results
            vectors.append(value)

    gram = lax.all_to_all(gram, AXES, 0, 0)
    solution, hessenberg = pl.pallas_call(
        finish_kernel,
        out_shape=[vector_shape, jax.ShapeDtypeStruct((KRYLOV + 1, KRYLOV), f32)],
        in_specs=[VMEM] * (2 + KRYLOV),
        out_specs=[VMEM] * 2,
        compiler_params=limit,
        name="finish",
    )(gram, shift, *vectors)
    return solution.reshape(first, second, local_modes), hessenberg


def solution(mesh):
    return jax.shard_map(
        per_device,
        mesh=mesh,
        in_specs=(
            P("gx", "gy", "mode"),
            P("mode", None),
            P("mode", None, None, None),
            P("mode"),
            P(None, "mode"),
            P(None, "mode"),
            P("gx", "gy"),
        ),
        out_specs=(P("gx", "gy", "mode"), P()),
        check_vma=False,
    )
```

```python
import functools

import jax
import jax.numpy as jnp
from jax import lax
from jax.experimental import pallas as pl
from jax.experimental.pallas import tpu as pltpu
from jax.sharding import PartitionSpec as P

KRYLOV = 3
TAIL = 16
AXES = ("mode", "gx", "gy")

epsilon = 1e-12


def pair_list(count, first):
    pairs = []
    for low in range(first, count - 1, 2):
        pairs += [(low, low + 1), (low + 1, low)]
    return pairs


def swaps_of(count):
    return [pairs for pairs in (pair_list(count, 0), pair_list(count, 1)) if pairs]


def face_swaps(faces):
    received = []
    for axis in ("gx", "gy"):
        swaps = swaps_of(lax.axis_size(axis))
        received.append(
            [lax.ppermute(face, axis, pairs) for face, pairs in zip(faces[axis], swaps)]
        )
    return received


def exchange(array, bit):
    count = lax.axis_size("mode")
    return lax.ppermute(array, "mode", [(i, i ^ bit) for i in range(count)])


def gather_far(packed):
    held = {0: packed}
    bit = lax.axis_size("mode") // 2
    while bit > 1:
        for key in list(held):
            held[key ^ bit] = exchange(held[key], bit)
        bit //= 2
    del held[0]
    return held


def hand_on(arrays, after):
    count = len(arrays)
    if not count:
        return []
    return pl.pallas_call(
        lambda *refs: None,
        out_shape=[jax.ShapeDtypeStruct(array.shape, array.dtype) for array in arrays],
        in_specs=[ANY] * (count + 1),
        out_specs=[ANY] * count,
        input_output_aliases={at: at for at in range(count)},
        name="hand_on",
    )(*arrays, after)


def write_faces(masked, lanes, first, second, x_refs, y_refs):
    if x_refs:
        even = lax.rem(lax.axis_index("gx"), 2) == 0
        low, high = masked[0], masked[first - 1]
        for ref, take_high in zip(x_refs, (even, jnp.logical_not(even))):
            ref[:, lanes] = jnp.where(take_high, high, low)
    if y_refs:
        even = lax.rem(lax.axis_index("gy"), 2) == 0
        low, high = masked[:, 0, :], masked[:, second - 1, :]
        for ref, take_high in zip(y_refs, (even, jnp.logical_not(even))):
            ref[:, lanes] = jnp.where(take_high, high, low)


def halos(refs, axis, lanes, shape):
    zero = jnp.zeros(shape, jnp.float32)
    values = [ref[:, lanes] for ref in refs] + [zero, zero]
    odd = lax.rem(lax.axis_index(axis), 2) == 1
    return jnp.where(odd, values[0], values[1]), jnp.where(odd, values[1], values[0])


def start_copies(pairs, sems):
    copies = [
        pltpu.make_async_copy(source, target, sems.at[at])
        for at, (source, target) in enumerate(pairs)
    ]
    for copy in copies:
        copy.start()
    return copies


def prepare_kernel(sizes, ins, x_refs, y_refs, packed_ref, open_ref, rhs_ref, scratch):
    first, second, local_blocks, block = sizes
    relax_ref, speed_ref, wall_ref, sems = scratch
    copies = start_copies(list(zip(ins, (rhs_ref, relax_ref, speed_ref, wall_ref))), sems)
    cells = first * second
    for copy in reversed(copies):
        copy.wait()
    wall = wall_ref[...].astype(jnp.float32)
    eye = (
        lax.broadcasted_iota(jnp.int32, (second, second), 0)
        == lax.broadcasted_iota(jnp.int32, (second, second), 1)
    ).astype(jnp.float32)
    for row in range(first):
        column = jnp.sum(eye * (1.0 - wall[row : row + 1, :]), axis=1, keepdims=True)
        open_ref[row * second : (row + 1) * second, :] = jnp.broadcast_to(column, (second, block))
    total = jnp.zeros((1, block), jnp.float32)
    for b in range(local_blocks):
        lanes = slice(b * block, (b + 1) * block)
        value = rhs_ref[:, lanes]
        packed_ref[b * cells : (b + 1) * cells, :] = value.astype(jnp.bfloat16)
        masked = (value * open_ref[...]).reshape(first, second, block)
        write_faces(masked, lanes, first, second, x_refs, y_refs)
        total += relax_ref[lanes].reshape(1, block) + speed_ref[0:1, lanes] + speed_ref[1:2, lanes]
    mean = jnp.sum(total, axis=1, keepdims=True) * (1.0 / (local_blocks * block))
    packed_ref[local_blocks * cells :, :] = jnp.broadcast_to(mean, (TAIL, block)).astype(
        jnp.bfloat16
    )


def load_kernel(count, *refs):
    for copy in start_copies(list(zip(refs[:count], refs[count : 2 * count])), refs[-1]):
        copy.wait()


def scatter(sizes, per_owner, b, places, cols_ref, sources, blocks_ref):
    first, second, local_blocks, block = sizes
    cells = first * second
    mine = lax.axis_index("mode")
    picks, weights = [], []
    for place, source in zip(places, sources):
        owner = mine ^ place
        for p in range(per_owner):
            slot = owner * per_owner + p
            column = cols_ref[slot, b] - owner * local_blocks
            picks.append(source[pl.ds(pl.multiple_of(column * cells, cells), cells), :])
            weights.append(blocks_ref[b, slot])
    return lax.dot_general(
        jnp.concatenate(picks, axis=1),
        jnp.concatenate(weights, axis=1),
        (((1,), (1,)), ((), ())),
        preferred_element_type=jnp.float32,
    )


def near_kernel(sizes, per_owner, places, cols_ref, sources, blocks_ref, current_ref, params, x_in, y_in, out_ref):
    first, second, local_blocks, block = sizes
    relax_ref, speed_ref, sign_ref, open_ref = params
    cells = first * second
    open_cells = open_ref[...]
    row_at = lax.broadcasted_iota(jnp.int32, (first, second, block), 1)
    for b in range(local_blocks):
        lanes = slice(b * block, (b + 1) * block)
        scattered = scatter(sizes, per_owner, b, places, cols_ref, sources, blocks_ref)
        current = current_ref[:, lanes]
        masked = (current * open_cells).reshape(first, second, block)
        west_in, east_in = halos(x_in, "gx", lanes, (second, block))
        south_in, north_in = halos(y_in, "gy", lanes, (first, block))
        from_west = jnp.concatenate([west_in[None], masked[:-1]], axis=0)
        from_east = jnp.concatenate([masked[1:], east_in[None]], axis=0)
        from_south = jnp.where(
            row_at == 0, south_in[:, None, :], pltpu.roll(masked, 1, axis=1)
        )
        from_north = jnp.where(
            row_at == second - 1, north_in[:, None, :], pltpu.roll(masked, second - 1, axis=1)
        )
        sign_x = sign_ref[0:1, lanes].reshape(1, 1, block)
        sign_y = sign_ref[1:2, lanes].reshape(1, 1, block)
        speed_x, speed_y = speed_ref[0:1, lanes], speed_ref[1:2, lanes]
        upstream_x = jnp.where(sign_x == 1, from_west, from_east).reshape(cells, block)
        upstream_y = jnp.where(sign_y == 1, from_south, from_north).reshape(cells, block)
        diagonal = relax_ref[lanes].reshape(1, block) + speed_x + speed_y
        out_ref[:, lanes] = (
            diagonal * current - speed_x * upstream_x - speed_y * upstream_y - scattered
        )


def add_kernel(sizes, per_owner, places, cols_ref, sources, blocks_ref, partial_ref, out_ref):
    first, second, local_blocks, block = sizes
    for b in range(local_blocks):
        lanes = slice(b * block, (b + 1) * block)
        out_ref[:, lanes] = partial_ref[:, lanes] - scatter(
            sizes, per_owner, b, places, cols_ref, sources, blocks_ref
        )


def shift_of(tails):
    mine = lax.axis_index("mode")
    total = jnp.zeros_like(tails[0])
    for owner in range(len(tails)):
        term = tails[0]
        for place in range(1, len(tails)):
            term = jnp.where((mine ^ place) == owner, tails[place], term)
        total = total + term
    return total * (1.0 / len(tails))


def last_kernel(sizes, per_owner, places, cols_ref, sources, blocks_ref, partial_ref, shift, earlier, open_ref, outs):
    first, second, local_blocks, block = sizes
    cells = first * second
    sums = {}
    for b in range(local_blocks):
        lanes = slice(b * block, (b + 1) * block)
        scattered = scatter(sizes, per_owner, b, places, cols_ref, sources, blocks_ref)
        result = partial_ref[:, lanes] - shift * earlier[-1][:, lanes] - scattered
        if outs.gram is None:
            outs.value[:, lanes] = result
            outs.packed[b * cells : (b + 1) * cells, :] = result.astype(jnp.bfloat16)
            write_faces(
                (result * open_ref[...]).reshape(first, second, block),
                lanes, first, second, outs.x, outs.y,
            )
        else:
            vectors = [ref[:, lanes] for ref in earlier] + [result]
            at = 0
            for i in range(len(vectors)):
                for j in range(i, len(vectors)):
                    term = jnp.sum((vectors[i] * vectors[j]).reshape(cells // 8, 8, block), axis=0)
                    sums[at] = term if b == 0 else sums[at] + term
                    at += 1
    if outs.gram is not None:
        devices = outs.gram.shape[0]
        lane = lax.broadcasted_iota(jnp.int32, (1, block), 1)
        row = jnp.zeros((1, block), jnp.float32)
        for at, value in sums.items():
            total = jnp.sum(jnp.sum(value, axis=0, keepdims=True), axis=1, keepdims=True)
            row = jnp.where(lane == at, total, row)
        outs.gram[...] = jnp.broadcast_to(row[None], (devices, 1, block))


class Outs:
    value = packed = gram = None
    x = y = ()


def least_squares(hessenberg, initial):
    upper = [list(row) for row in hessenberg]
    target = [initial] + [jnp.zeros_like(initial) for row_index in range(KRYLOV)]
    cosines = []
    sines = []
    for col_index in range(KRYLOV):
        for row_index in range(col_index):
            first = upper[row_index][col_index]
            second = upper[row_index + 1][col_index]
            upper[row_index][col_index] = cosines[row_index] * first + sines[row_index] * second
            upper[row_index + 1][col_index] = cosines[row_index] * second - sines[row_index] * first
        first = upper[col_index][col_index]
        second = upper[col_index + 1][col_index]
        radius = jnp.sqrt(first * first + second * second)
        cosine = first / radius
        sine_value = second / radius
        upper[col_index][col_index] = radius
        target[col_index + 1] = -sine_value * target[col_index]
        target[col_index] = cosine * target[col_index]
        cosines.append(cosine)
        sines.append(sine_value)
    combo = [None] * KRYLOV
    for row_index in reversed(range(KRYLOV)):
        running = target[row_index]
        for col_index in range(row_index + 1, KRYLOV):
            running = running - upper[row_index][col_index] * combo[col_index]
        combo[row_index] = running / upper[row_index][row_index]
    return combo


def arnoldi(gram, shift):
    size = KRYLOV + 1

    def inner(left, right):
        total = None
        for i in range(size):
            for j in range(size):
                if left[i] is None or right[j] is None:
                    continue
                term = left[i] * right[j] * gram[min(i, j)][max(i, j)]
                total = term if total is None else total + term
        return total

    initial = jnp.sqrt(gram[0][0] + epsilon)
    basis = [[1.0 / initial] + [None] * KRYLOV]
    zero = jnp.zeros_like(initial)
    hessenberg = [[zero] * KRYLOV for row_index in range(size)]
    for section in range(KRYLOV):
        vector = basis[section]
        image = [None] * size
        for k in range(section + 2):
            parts = []
            if k > 0 and vector[k - 1] is not None:
                parts.append(vector[k - 1])
            if vector[k] is not None:
                parts.append(shift * vector[k])
            image[k] = sum(parts[1:], parts[0])
        rest = list(image)
        for earlier in range(section + 1):
            coefficient = inner(basis[earlier], image)
            hessenberg[earlier][section] = coefficient
            for k in range(earlier + 1):
                rest[k] = rest[k] - coefficient * basis[earlier][k]
        length = jnp.sqrt(jnp.maximum(inner(rest, rest), 0.0) + epsilon)
        hessenberg[section + 1][section] = length
        basis.append([None if part is None else part / length for part in rest])
    combo = least_squares(hessenberg, initial)
    weights = []
    for k in range(KRYLOV):
        total = zero
        for j in range(k, KRYLOV):
            total = total + combo[j] * basis[j][k]
        weights.append(total)
    return hessenberg, weights


def finish_kernel(gram_ref, shift_ref, *refs):
    vectors, (solution_ref, hessenberg_ref) = refs[:KRYLOV], refs[KRYLOV:]
    block = shift_ref.shape[1]
    total = jnp.sum(gram_ref[...], axis=0)
    lane = lax.broadcasted_iota(jnp.int32, (1, block), 1)
    gram = [[None] * (KRYLOV + 1) for i in range(KRYLOV + 1)]
    at = 0
    for i in range(KRYLOV + 1):
        for j in range(i, KRYLOV + 1):
            entry = jnp.sum(jnp.where(lane == at, total, 0.0), axis=1, keepdims=True)
            gram[i][j] = jnp.broadcast_to(entry, (1, block))
            at += 1
    hessenberg, weights = arnoldi(gram, shift_ref[...])
    rows = lax.broadcasted_iota(jnp.int32, (KRYLOV + 1, KRYLOV), 0)
    cols = lax.broadcasted_iota(jnp.int32, (KRYLOV + 1, KRYLOV), 1)
    table = jnp.zeros((KRYLOV + 1, KRYLOV), jnp.float32)
    for i in range(KRYLOV + 1):
        for j in range(KRYLOV):
            table = jnp.where((rows == i) & (cols == j), hessenberg[i][j][:, :KRYLOV], table)
    hessenberg_ref[...] = table
    for b in range(solution_ref.shape[1] // block):
        lanes = slice(b * block, (b + 1) * block)
        solution_ref[:, lanes] = sum(
            weight * ref[:, lanes] for weight, ref in zip(weights, vectors)
        )


VMEM = pl.BlockSpec(memory_space=pltpu.VMEM)
SMEM = pl.BlockSpec(memory_space=pltpu.SMEM)
HBM = pl.BlockSpec(memory_space=pltpu.HBM)
ANY = pl.BlockSpec(memory_space=pl.ANY)


def call(name, kernel, groups, shapes, scratch=(), flops=0):
    flat = [pair for group in groups for pair in group]

    def body(*refs):
        refs = list(refs)
        lists = []
        for group in groups:
            lists.append(refs[: len(group)])
            del refs[: len(group)]
        kernel(*lists, refs[: len(shapes)], refs[len(shapes) :])

    size = sum(operand.size * operand.dtype.itemsize for spec, operand in flat)
    size += sum(shape.size * shape.dtype.itemsize for shape in shapes)
    return pl.pallas_call(
        body,
        out_shape=list(shapes),
        in_specs=[spec for spec, operand in flat],
        out_specs=[VMEM] * len(shapes),
        scratch_shapes=list(scratch),
        compiler_params=pltpu.CompilerParams(vmem_limit_bytes=32 * 1024 * 1024),
        cost_estimate=pl.CostEstimate(flops=flops, bytes_accessed=size, transcendentals=0),
        name=name,
    )(*[operand for spec, operand in flat])


def in_vmem(operands):
    return [(VMEM, operand) for operand in operands]


def in_hbm(operands):
    return [(HBM, operand) for operand in operands]


def per_device(right_side, col_block, blocks, relax_rate, drift_speed, upwind_sign, wall_mask):
    first, second, local_modes = right_side.shape
    local_blocks, slots, block = blocks.shape[:3]
    cells = first * second
    count = lax.axis_size("mode")
    devices = count * lax.axis_size("gx") * lax.axis_size("gy")
    per_owner = slots // count
    sizes = (first, second, local_blocks, block)
    x_swaps, y_swaps = len(swaps_of(lax.axis_size("gx"))), len(swaps_of(lax.axis_size("gy")))
    n_faces = x_swaps + y_swaps
    f32 = jnp.float32
    shape_of = jax.ShapeDtypeStruct
    face_shapes = [shape_of((second, local_modes), f32)] * x_swaps + [
        shape_of((first, local_modes), f32)
    ] * y_swaps
    packed_shape = shape_of((local_blocks * cells + TAIL, block), jnp.bfloat16)
    vector_shape = shape_of((cells, local_modes), f32)
    shift_shape = shape_of((1, block), f32)
    near = [place for place in (0, 1) if place < count]
    far = [place for place in range(count) if place not in near]
    middle = [place for place in far if place % 2 == 0]
    final = [place for place in far if place % 2 == 1]

    def prepare(ins, outs, scratch):
        faces, rest = outs[:n_faces], outs[n_faces:]
        prepare_kernel(sizes, ins, faces[:x_swaps], faces[x_swaps:], *rest, scratch)

    *faces, packed, open_cells, start = call(
        "prepare",
        prepare,
        [in_hbm([right_side.reshape(cells, local_modes), relax_rate, drift_speed, wall_mask])],
        face_shapes + [packed_shape, shape_of((cells, block), f32), vector_shape],
        [
            pltpu.VMEM(relax_rate.shape, f32),
            pltpu.VMEM(drift_speed.shape, f32),
            pltpu.VMEM(wall_mask.shape, jnp.int32),
            pltpu.SemaphoreType.DMA((4,)),
        ],
    )
    kept = [blocks, relax_rate, drift_speed, upwind_sign, col_block.T]

    def load(ins, after, outs, scratch):
        load_kernel(len(ins), *ins, *outs, *scratch)

    blocks, relax_rate, drift_speed, upwind_sign, columns = call(
        "load",
        load,
        [in_hbm(kept), [(ANY, open_cells)]],
        [shape_of(array.shape, array.dtype) for array in kept],
        [pltpu.SemaphoreType.DMA((len(kept),))],
    )

    work = 2 * cells * local_modes * per_owner * block
    vectors = [start]
    for section in range(KRYLOV):
        sources = {0: packed}
        if count > 1:
            sources[1] = exchange(packed, 1)
        held = gather_far(packed)
        x_in, y_in = face_swaps({"gx": faces[:x_swaps], "gy": faces[x_swaps:]})

        def near_step(cols, sources, rest, x_in, y_in, outs, scratch):
            blocks_ref, current_ref, *params = rest
            near_kernel(
                sizes, per_owner, near, cols[0], sources, blocks_ref, current_ref, params,
                x_in, y_in, outs[0],
            )

        (partial,) = call(
            "near_%d" % section,
            near_step,
            [
                [(SMEM, columns)],
                in_vmem([sources[place] for place in near]),
                in_vmem([blocks, vectors[-1], relax_rate, drift_speed, upwind_sign, open_cells]),
                in_vmem(x_in),
                in_vmem(y_in),
            ],
            [vector_shape],
            flops=work * len(near),
        )

        held = dict(zip(held, hand_on(list(held.values()), partial)))
        for place, array in held.items():
            sources[place] = array
            sources[place ^ 1] = exchange(array, 1)

        def middle_step(cols, sources, rest, outs, scratch):
            add_kernel(sizes, per_owner, middle, cols[0], sources, *rest, outs[0])

        if middle:
            (partial,) = call(
                "middle_%d" % section,
                middle_step,
                [
                    [(SMEM, columns)],
                    in_vmem([sources[place] for place in middle]),
                    in_vmem([blocks, partial]),
                ],
                [vector_shape],
                flops=work * len(middle),
            )

        last = section == KRYLOV - 1
        def last_step(cols, sources, rest, earlier, known, outs, scratch, section=section, last=last):
            blocks_ref, partial_ref, open_ref = rest
            if section == 0:
                tail_at = local_blocks * cells
                value = shift_of([ref[tail_at:, :].astype(f32)[0:1] for ref in known])
                outs[-1][...] = value
                outs = outs[:-1]
            else:
                value = known[0][...]
            named = Outs()
            if last:
                named.gram = outs[0]
            else:
                named.x, named.y = outs[:x_swaps], outs[x_swaps:n_faces]
                named.packed, named.value = outs[n_faces:]
            last_kernel(
                sizes, per_owner, final, cols[0], sources, blocks_ref, partial_ref,
                value, earlier, open_ref, named,
            )

        if last:
            shapes = [shape_of((devices, 1, block), f32)]
        else:
            shapes = face_shapes + [packed_shape, vector_shape]
        if section == 0:
            shapes = shapes + [shift_shape]
        results = call(
            "last_%d" % section,
            last_step,
            [
                [(SMEM, columns)],
                in_vmem([sources[place] for place in final]),
                in_vmem([blocks, partial, open_cells]),
                in_vmem(vectors),
                in_vmem([shift] if section else [sources[place] for place in range(count)]),
            ],
            shapes,
            flops=work * len(final),
        )
        if section == 0:
            *results, shift = results
        if last:
            (gram,) = results
        else:
            *faces, packed, value = results
            vectors.append(value)

    gram = lax.all_to_all(gram, AXES, 0, 0)

    def finish(ins, outs, scratch):
        finish_kernel(*ins, *outs)

    solution, hessenberg = call(
        "finish",
        finish,
        [in_vmem([gram, shift, *vectors])],
        [vector_shape, shape_of((KRYLOV + 1, KRYLOV), f32)],
    )
    return solution.reshape(first, second, local_modes), hessenberg


def solution(mesh):
    return jax.shard_map(
        per_device,
        mesh=mesh,
        in_specs=(
            P("gx", "gy", "mode"),
            P("mode", None),
            P("mode", None, None, None),
            P("mode"),
            P(None, "mode"),
            P(None, "mode"),
            P("gx", "gy"),
        ),
        out_specs=(P("gx", "gy", "mode"), P()),
        check_vma=False,
    )
```

```python
import functools

import jax
import jax.numpy as jnp
from jax import lax
from jax.experimental import pallas as pl
from jax.experimental.pallas import tpu as pltpu
from jax.sharding import PartitionSpec as P

KRYLOV = 3
SHIFT = 4.05
AXES = ("mode", "gx", "gy")

epsilon = 1e-12


def pair_list(count, first):
    pairs = []
    for low in range(first, count - 1, 2):
        pairs += [(low, low + 1), (low + 1, low)]
    return pairs


def swaps_of(count):
    return [pairs for pairs in (pair_list(count, 0), pair_list(count, 1)) if pairs]


def face_swaps(faces):
    received = []
    for axis in ("gx", "gy"):
        swaps = swaps_of(lax.axis_size(axis))
        received.append(
            [lax.ppermute(face, axis, pairs) for face, pairs in zip(faces[axis], swaps)]
        )
    return received


def exchange(array, bit):
    count = lax.axis_size("mode")
    return lax.ppermute(array, "mode", [(i, i ^ bit) for i in range(count)])


def gather_far(packed):
    held = {0: packed}
    bit = lax.axis_size("mode") // 2
    while bit > 1:
        for key in list(held):
            held[key ^ bit] = exchange(held[key], bit)
        bit //= 2
    del held[0]
    return held


def hand_on(arrays, after):
    count = len(arrays)
    if not count:
        return []
    return pl.pallas_call(
        lambda *refs: None,
        out_shape=[jax.ShapeDtypeStruct(array.shape, array.dtype) for array in arrays],
        in_specs=[ANY] * (count + len(after)),
        out_specs=[ANY] * count,
        input_output_aliases={at: at for at in range(count)},
        compiler_params=pltpu.CompilerParams(vmem_limit_bytes=SCOPED),
        name="hand_on",
    )(*arrays, *after)


def write_faces(masked, lanes, first, second, x_refs, y_refs):
    if x_refs:
        even = lax.rem(lax.axis_index("gx"), 2) == 0
        low, high = masked[0], masked[first - 1]
        for ref, take_high in zip(x_refs, (even, jnp.logical_not(even))):
            ref[:, lanes] = jnp.where(take_high, high, low)
    if y_refs:
        even = lax.rem(lax.axis_index("gy"), 2) == 0
        low, high = masked[:, 0, :], masked[:, second - 1, :]
        for ref, take_high in zip(y_refs, (even, jnp.logical_not(even))):
            ref[:, lanes] = jnp.where(take_high, high, low)


def halos(refs, axis, lanes, shape):
    zero = jnp.zeros(shape, jnp.float32)
    values = [ref[:, lanes] for ref in refs] + [zero, zero]
    odd = lax.rem(lax.axis_index(axis), 2) == 1
    return jnp.where(odd, values[0], values[1]), jnp.where(odd, values[1], values[0])


def prepare_kernel(sizes, rhs_ref, wall_ref, x_refs, y_refs, open_ref):
    first, second, local_blocks, block = sizes
    wall = wall_ref[...].astype(jnp.float32)
    eye = (
        lax.broadcasted_iota(jnp.int32, (second, second), 0)
        == lax.broadcasted_iota(jnp.int32, (second, second), 1)
    ).astype(jnp.float32)
    for row in range(first):
        column = jnp.sum(eye * (1.0 - wall[row : row + 1, :]), axis=1, keepdims=True)
        open_ref[row * second : (row + 1) * second, :] = jnp.broadcast_to(column, (second, block))
    for b in range(local_blocks):
        lanes = slice(b * block, (b + 1) * block)
        masked = (rhs_ref[:, lanes] * open_ref[...]).reshape(first, second, block)
        write_faces(masked, lanes, first, second, x_refs, y_refs)


def scatter(sizes, per_owner, b, places, cols_ref, sources, blocks_ref):
    first, second, local_blocks, block = sizes
    mine = lax.axis_index("mode")
    picks, weights = [], []
    for place, source in zip(places, sources):
        owner = mine ^ place
        for p in range(per_owner):
            slot = owner * per_owner + p
            column = cols_ref[slot, b] - owner * local_blocks
            picks.append(source[:, pl.ds(pl.multiple_of(column * block, block), block)])
            weights.append(blocks_ref[b, slot])
    return lax.dot_general(
        jnp.concatenate(picks, axis=1),
        jnp.concatenate(weights, axis=1),
        (((1,), (1,)), ((), ())),
        preferred_element_type=jnp.float32,
    )


def split_speeds(speed_ref, sign_ref, lanes):
    parts = []
    for axis in range(2):
        speed, sign = speed_ref[axis : axis + 1, lanes], sign_ref[axis : axis + 1, lanes]
        parts += [jnp.where(sign == 1, speed, 0.0), jnp.where(sign == 1, 0.0, speed)]
    return parts


def near_kernel(sizes, per_owner, places, cols_ref, sources, blocks_ref, current_ref, params, open_ref, out_ref):
    first, second, local_blocks, block = sizes
    cells = first * second
    open_cells = open_ref[...]
    row_at = lax.broadcasted_iota(jnp.int32, (first, second, block), 1)
    zero = jnp.zeros((1, second, block), jnp.float32)
    for b in range(local_blocks):
        lanes = slice(b * block, (b + 1) * block)
        scattered = scatter(sizes, per_owner, b, places, cols_ref, sources, blocks_ref)
        current = current_ref[:, lanes]
        masked = (current * open_cells).reshape(first, second, block)
        relax_ref, speed_ref, sign_ref = params
        west, east, south, north = split_speeds(speed_ref, sign_ref, lanes)
        diagonal = relax_ref[lanes].reshape(1, block) + (west + east) + (south + north) - SHIFT
        from_west = jnp.concatenate([zero, masked[:-1]], axis=0)
        from_east = jnp.concatenate([masked[1:], zero], axis=0)
        from_south = jnp.where(row_at == 0, 0.0, pltpu.roll(masked, 1, axis=1))
        from_north = jnp.where(row_at == second - 1, 0.0, pltpu.roll(masked, second - 1, axis=1))
        drift = (
            west.reshape(1, 1, block) * from_west
            + east.reshape(1, 1, block) * from_east
            + south.reshape(1, 1, block) * from_south
            + north.reshape(1, 1, block) * from_north
        ).reshape(cells, block)
        out_ref[:, lanes] = diagonal * current - drift - scattered


def middle_kernel(sizes, per_owner, places, cols_ref, sources, blocks_ref, partial_ref, speed_ref, sign_ref, x_in, y_in, out_ref):
    first, second, local_blocks, block = sizes
    cells = first * second
    row_at = lax.broadcasted_iota(jnp.int32, (first, second, block), 1)
    for b in range(local_blocks):
        lanes = slice(b * block, (b + 1) * block)
        value = partial_ref[:, lanes]
        if places:
            value = value - scatter(sizes, per_owner, b, places, cols_ref, sources, blocks_ref)
        west, east, south, north = split_speeds(speed_ref, sign_ref, lanes)
        west_in, east_in = halos(x_in, "gx", lanes, (second, block))
        south_in, north_in = halos(y_in, "gy", lanes, (first, block))
        value = value.reshape(first, second, block)
        value = value - jnp.where(
            row_at == 0,
            (south * south_in)[:, None, :],
            jnp.where(row_at == second - 1, (north * north_in)[:, None, :], 0.0),
        )
        value = jnp.concatenate(
            [value[:1] - (west * west_in)[None], value[1:-1], value[-1:] - (east * east_in)[None]],
            axis=0,
        )
        out_ref[:, lanes] = value.reshape(cells, block)


def last_kernel(sizes, per_owner, places, cols_ref, sources, blocks_ref, partial_ref, earlier, open_ref, outs):
    first, second, local_blocks, block = sizes
    cells = first * second
    sums = {}
    for b in range(local_blocks):
        lanes = slice(b * block, (b + 1) * block)
        scattered = scatter(sizes, per_owner, b, places, cols_ref, sources, blocks_ref)
        result = partial_ref[:, lanes] - scattered
        if outs.gram is None:
            outs.value[:, lanes] = result
            outs.packed[:, lanes] = result.astype(jnp.bfloat16)
            write_faces(
                (result * open_ref[...]).reshape(first, second, block),
                lanes, first, second, outs.x, outs.y,
            )
        else:
            vectors = [ref[:, lanes] for ref in earlier] + [result]
            at = 0
            for i in range(len(vectors)):
                for j in range(i, len(vectors)):
                    term = jnp.sum((vectors[i] * vectors[j]).reshape(cells // 8, 8, block), axis=0)
                    sums[at] = term if b == 0 else sums[at] + term
                    at += 1
    if outs.gram is not None:
        devices = outs.gram.shape[0]
        lane = lax.broadcasted_iota(jnp.int32, (1, block), 1)
        row = jnp.zeros((1, block), jnp.float32)
        for at, value in sums.items():
            total = jnp.sum(jnp.sum(value, axis=0, keepdims=True), axis=1, keepdims=True)
            row = jnp.where(lane == at, total, row)
        outs.gram[...] = jnp.broadcast_to(row[None], (devices, 1, block))


class Outs:
    value = packed = gram = None
    x = y = ()


def least_squares(hessenberg, initial):
    upper = [list(row) for row in hessenberg]
    target = [initial] + [jnp.zeros_like(initial) for row_index in range(KRYLOV)]
    cosines = []
    sines = []
    for col_index in range(KRYLOV):
        for row_index in range(col_index):
            first = upper[row_index][col_index]
            second = upper[row_index + 1][col_index]
            upper[row_index][col_index] = cosines[row_index] * first + sines[row_index] * second
            upper[row_index + 1][col_index] = cosines[row_index] * second - sines[row_index] * first
        first = upper[col_index][col_index]
        second = upper[col_index + 1][col_index]
        radius = jnp.sqrt(first * first + second * second)
        cosine = first / radius
        sine_value = second / radius
        upper[col_index][col_index] = radius
        target[col_index + 1] = -sine_value * target[col_index]
        target[col_index] = cosine * target[col_index]
        cosines.append(cosine)
        sines.append(sine_value)
    combo = [None] * KRYLOV
    for row_index in reversed(range(KRYLOV)):
        running = target[row_index]
        for col_index in range(row_index + 1, KRYLOV):
            running = running - upper[row_index][col_index] * combo[col_index]
        combo[row_index] = running / upper[row_index][row_index]
    return combo


def arnoldi(gram):
    size = KRYLOV + 1

    def inner(left, right):
        total = None
        for i in range(size):
            for j in range(size):
                if left[i] is None or right[j] is None:
                    continue
                term = left[i] * right[j] * gram[min(i, j)][max(i, j)]
                total = term if total is None else total + term
        return total

    initial = jnp.sqrt(gram[0][0] + epsilon)
    basis = [[1.0 / initial] + [None] * KRYLOV]
    zero = jnp.zeros_like(initial)
    hessenberg = [[zero] * KRYLOV for row_index in range(size)]
    for section in range(KRYLOV):
        vector = basis[section]
        image = [None] * size
        for k in range(section + 2):
            parts = []
            if k > 0 and vector[k - 1] is not None:
                parts.append(vector[k - 1])
            if vector[k] is not None:
                parts.append(SHIFT * vector[k])
            image[k] = sum(parts[1:], parts[0])
        rest = list(image)
        for earlier in range(section + 1):
            coefficient = inner(basis[earlier], image)
            hessenberg[earlier][section] = coefficient
            for k in range(earlier + 1):
                rest[k] = rest[k] - coefficient * basis[earlier][k]
        length = jnp.sqrt(jnp.maximum(inner(rest, rest), 0.0) + epsilon)
        hessenberg[section + 1][section] = length
        basis.append([None if part is None else part / length for part in rest])
    combo = least_squares(hessenberg, initial)
    weights = []
    for k in range(KRYLOV):
        total = zero
        for j in range(k, KRYLOV):
            total = total + combo[j] * basis[j][k]
        weights.append(total)
    return hessenberg, weights


def finish_kernel(gram_ref, *refs):
    vectors, (solution_ref, hessenberg_ref) = refs[:KRYLOV], refs[KRYLOV:]
    block = gram_ref.shape[2]
    total = jnp.sum(gram_ref[...], axis=0)
    lane = lax.broadcasted_iota(jnp.int32, (1, block), 1)
    gram = [[None] * (KRYLOV + 1) for i in range(KRYLOV + 1)]
    at = 0
    for i in range(KRYLOV + 1):
        for j in range(i, KRYLOV + 1):
            entry = jnp.sum(jnp.where(lane == at, total, 0.0), axis=1, keepdims=True)
            gram[i][j] = jnp.broadcast_to(entry, (1, block))
            at += 1
    hessenberg, weights = arnoldi(gram)
    rows = lax.broadcasted_iota(jnp.int32, (KRYLOV + 1, KRYLOV), 0)
    cols = lax.broadcasted_iota(jnp.int32, (KRYLOV + 1, KRYLOV), 1)
    table = jnp.zeros((KRYLOV + 1, KRYLOV), jnp.float32)
    for i in range(KRYLOV + 1):
        for j in range(KRYLOV):
            table = jnp.where((rows == i) & (cols == j), hessenberg[i][j][:, :KRYLOV], table)
    hessenberg_ref[...] = table
    for b in range(solution_ref.shape[1] // block):
        lanes = slice(b * block, (b + 1) * block)
        solution_ref[:, lanes] = sum(
            weight * ref[:, lanes] for weight, ref in zip(weights, vectors)
        )


VMEM = pl.BlockSpec(memory_space=pltpu.VMEM)
SMEM = pl.BlockSpec(memory_space=pltpu.SMEM)
ANY = pl.BlockSpec(memory_space=pl.ANY)
SCOPED = 16 * 1024 * 1024


def call(name, kernel, groups, shapes, scratch=(), flops=0):
    flat = [pair for group in groups for pair in group]

    def body(*refs):
        refs = list(refs)
        lists = []
        for group in groups:
            lists.append(refs[: len(group)])
            del refs[: len(group)]
        kernel(*lists, refs[: len(shapes)], refs[len(shapes) :])

    size = sum(operand.size * operand.dtype.itemsize for spec, operand in flat)
    size += sum(shape.size * shape.dtype.itemsize for shape in shapes)
    return pl.pallas_call(
        body,
        out_shape=list(shapes),
        in_specs=[spec for spec, operand in flat],
        out_specs=[VMEM] * len(shapes),
        scratch_shapes=list(scratch),
        compiler_params=pltpu.CompilerParams(vmem_limit_bytes=SCOPED),
        cost_estimate=pl.CostEstimate(flops=flops, bytes_accessed=size, transcendentals=0),
        name=name,
    )(*[operand for spec, operand in flat])


def in_vmem(operands):
    return [(VMEM, operand) for operand in operands]


def per_device(right_side, col_block, blocks, relax_rate, drift_speed, upwind_sign, wall_mask):
    first, second, local_modes = right_side.shape
    local_blocks, slots, block = blocks.shape[:3]
    cells = first * second
    count = lax.axis_size("mode")
    devices = count * lax.axis_size("gx") * lax.axis_size("gy")
    per_owner = slots // count
    sizes = (first, second, local_blocks, block)
    x_swaps, y_swaps = len(swaps_of(lax.axis_size("gx"))), len(swaps_of(lax.axis_size("gy")))
    n_faces = x_swaps + y_swaps
    f32 = jnp.float32
    shape_of = jax.ShapeDtypeStruct
    face_shapes = [shape_of((second, local_modes), f32)] * x_swaps + [
        shape_of((first, local_modes), f32)
    ] * y_swaps
    packed_shape = shape_of((cells, local_modes), jnp.bfloat16)
    vector_shape = shape_of((cells, local_modes), f32)
    near = [place for place in (0, 1) if place < count]
    far = [place for place in range(count) if place not in near]
    middle = [place for place in far if place % 2 == 0]
    final = [place for place in far if place % 2 == 1]

    start = right_side.reshape(cells, local_modes)
    packed = start.astype(jnp.bfloat16)

    def prepare(ins, outs, scratch):
        faces, (open_ref,) = outs[:n_faces], outs[n_faces:]
        prepare_kernel(sizes, *ins, faces[:x_swaps], faces[x_swaps:], open_ref)

    *faces, open_cells = call(
        "prepare",
        prepare,
        [in_vmem([start, wall_mask])],
        face_shapes + [shape_of((cells, block), f32)],
        flops=8 * 10**9,
    )
    columns = col_block.T

    work = 2 * cells * local_modes * per_owner * block
    vectors = [start]
    for section in range(KRYLOV):
        sources = {0: packed}
        if count > 1:
            sources[1] = exchange(packed, 1)
        held = gather_far(packed)
        x_in, y_in = face_swaps({"gx": faces[:x_swaps], "gy": faces[x_swaps:]})

        def near_step(cols, sources, rest, params, outs, scratch):
            blocks_ref, current_ref, open_ref = rest
            near_kernel(
                sizes, per_owner, near, cols[0], sources, blocks_ref, current_ref, params,
                open_ref, outs[0],
            )

        (partial,) = call(
            "near_%d" % section,
            near_step,
            [
                [(SMEM, columns)],
                in_vmem([sources[place] for place in near]),
                in_vmem([blocks, vectors[-1], open_cells]),
                in_vmem([relax_rate, drift_speed, upwind_sign]),
            ],
            [vector_shape],
            flops=work * len(near),
        )

        held = dict(zip(held, hand_on(list(held.values()), [partial, *x_in, *y_in])))
        for place, array in held.items():
            sources[place] = array
            sources[place ^ 1] = exchange(array, 1)

        def middle_step(cols, sources, rest, x_in, y_in, outs, scratch):
            middle_kernel(
                sizes, per_owner, middle, cols[0], sources, *rest, x_in, y_in, outs[0]
            )

        (partial,) = call(
            "middle_%d" % section,
            middle_step,
            [
                [(SMEM, columns)],
                in_vmem([sources[place] for place in middle]),
                in_vmem([blocks, partial, drift_speed, upwind_sign]),
                in_vmem(x_in),
                in_vmem(y_in),
            ],
            [vector_shape],
            flops=work * len(middle),
        )

        last = section == KRYLOV - 1
        def last_step(cols, sources, rest, earlier, outs, scratch, last=last):
            blocks_ref, partial_ref, open_ref = rest
            named = Outs()
            if last:
                named.gram = outs[0]
            else:
                named.x, named.y = outs[:x_swaps], outs[x_swaps:n_faces]
                named.packed, named.value = outs[n_faces:]
            last_kernel(
                sizes, per_owner, final, cols[0], sources, blocks_ref, partial_ref,
                earlier, open_ref, named,
            )

        if last:
            shapes = [shape_of((devices, 1, block), f32)]
        else:
            shapes = face_shapes + [packed_shape, vector_shape]
        results = call(
            "last_%d" % section,
            last_step,
            [
                [(SMEM, columns)],
                in_vmem([sources[place] for place in final]),
                in_vmem([blocks, partial, open_cells]),
                in_vmem(vectors if last else []),
            ],
            shapes,
            flops=work * len(final),
        )
        if last:
            (gram,) = results
        else:
            *faces, packed, value = results
            vectors.append(value)

    gram = lax.all_to_all(gram, AXES, 0, 0)

    def finish(ins, outs, scratch):
        finish_kernel(*ins, *outs)

    solution, hessenberg = call(
        "finish",
        finish,
        [in_vmem([gram, *vectors])],
        [vector_shape, shape_of((KRYLOV + 1, KRYLOV), f32)],
    )
    return solution.reshape(first, second, local_modes), hessenberg


def solution(mesh):
    return jax.shard_map(
        per_device,
        mesh=mesh,
        in_specs=(
            P("gx", "gy", "mode"),
            P("mode", None),
            P("mode", None, None, None),
            P("mode"),
            P(None, "mode"),
            P(None, "mode"),
            P("gx", "gy"),
        ),
        out_specs=(P("gx", "gy", "mode"), P()),
        check_vma=False,
    )
```

```python
import functools

import jax
import jax.numpy as jnp
from jax import lax
from jax.experimental import pallas as pl
from jax.experimental.pallas import tpu as pltpu
from jax.sharding import PartitionSpec as P

KRYLOV = 3
SHIFT = 4.05
AXES = ("mode", "gx", "gy")

epsilon = 1e-12


def moves_of(count):
    if count == 1:
        return []
    if count == 2:
        return [[(0, 1), (1, 0)]]
    return [
        [(i, (i + 1) % count) for i in range(count)],
        [(i, (i - 1) % count) for i in range(count)],
    ]


def move_faces(faces):
    received = []
    for axis in ("gy", "gx"):
        moves = moves_of(lax.axis_size(axis))
        received.append([lax.ppermute(face, axis, pairs) for face, pairs in zip(faces[axis], moves)])
    return received


def exchange(array, bit):
    count = lax.axis_size("mode")
    return lax.ppermute(array, "mode", [(i, i ^ bit) for i in range(count)])


def gather_far(packed):
    held = {0: packed}
    bit = lax.axis_size("mode") // 2
    while bit > 1:
        for key in list(held):
            held[key ^ bit] = exchange(held[key], bit)
        bit //= 2
    del held[0]
    return held


def hand_on(arrays, after):
    count = len(arrays)
    if not count:
        return []
    return pl.pallas_call(
        lambda *refs: None,
        out_shape=[jax.ShapeDtypeStruct(array.shape, array.dtype) for array in arrays],
        in_specs=[ANY] * (count + len(after)),
        out_specs=[ANY] * count,
        input_output_aliases={at: at for at in range(count)},
        compiler_params=pltpu.CompilerParams(vmem_limit_bytes=SCOPED),
        name="hand_on",
    )(*arrays, *after)


def store_faces(refs, axis, lanes, low, high):
    if len(refs) == 1:
        refs[0][:, lanes] = jnp.where(lax.axis_index(axis) == 0, high, low)
    elif refs:
        refs[0][:, lanes] = high
        refs[1][:, lanes] = low


def write_faces(masked, lanes, first, second, x_refs, y_refs):
    store_faces(x_refs, "gx", lanes, masked[0], masked[first - 1])
    store_faces(y_refs, "gy", lanes, masked[:, 0, :], masked[:, second - 1, :])


def halos(refs, axis, lanes, shape):
    zero = jnp.zeros(shape, jnp.float32)
    if not refs:
        return zero, zero
    at = lax.axis_index(axis)
    low, high = refs[0][:, lanes], refs[-1][:, lanes]
    return jnp.where(at == 0, zero, low), jnp.where(at == lax.axis_size(axis) - 1, zero, high)


def prepare_kernel(sizes, rhs_ref, wall_ref, x_refs, y_refs, open_ref):
    first, second, local_blocks, block = sizes
    wall = wall_ref[...].astype(jnp.float32)
    eye = (
        lax.broadcasted_iota(jnp.int32, (second, second), 0)
        == lax.broadcasted_iota(jnp.int32, (second, second), 1)
    ).astype(jnp.float32)
    for row in range(first):
        column = jnp.sum(eye * (1.0 - wall[row : row + 1, :]), axis=1, keepdims=True)
        open_ref[row * second : (row + 1) * second, :] = jnp.broadcast_to(column, (second, block))
    for b in range(local_blocks):
        lanes = slice(b * block, (b + 1) * block)
        masked = (rhs_ref[:, lanes] * open_ref[...]).reshape(first, second, block)
        write_faces(masked, lanes, first, second, x_refs, y_refs)


def scatter(sizes, per_owner, b, places, cols_ref, sources, blocks_ref):
    first, second, local_blocks, block = sizes
    mine = lax.axis_index("mode")
    picks, weights = [], []
    for place, source in zip(places, sources):
        owner = mine ^ place
        for p in range(per_owner):
            slot = owner * per_owner + p
            column = cols_ref[slot, b] - owner * local_blocks
            picks.append(source[:, pl.ds(pl.multiple_of(column * block, block), block)])
            weights.append(blocks_ref[b, slot])
    return lax.dot_general(
        jnp.concatenate(picks, axis=1),
        jnp.concatenate(weights, axis=1),
        (((1,), (1,)), ((), ())),
        preferred_element_type=jnp.float32,
    )


def split_speeds(speed_ref, sign_ref, lanes):
    parts = []
    for axis in range(2):
        speed, sign = speed_ref[axis : axis + 1, lanes], sign_ref[axis : axis + 1, lanes]
        parts += [jnp.where(sign == 1, speed, 0.0), jnp.where(sign == 1, 0.0, speed)]
    return parts


def near_kernel(sizes, per_owner, places, cols_ref, sources, blocks_ref, current_ref, params, open_ref, out_ref):
    first, second, local_blocks, block = sizes
    cells = first * second
    open_cells = open_ref[...]
    row_at = lax.broadcasted_iota(jnp.int32, (first, second, block), 1)
    zero = jnp.zeros((1, second, block), jnp.float32)
    for b in range(local_blocks):
        lanes = slice(b * block, (b + 1) * block)
        scattered = scatter(sizes, per_owner, b, places, cols_ref, sources, blocks_ref)
        current = current_ref[:, lanes]
        masked = (current * open_cells).reshape(first, second, block)
        relax_ref, speed_ref, sign_ref = params
        west, east, south, north = split_speeds(speed_ref, sign_ref, lanes)
        diagonal = relax_ref[lanes].reshape(1, block) + (west + east) + (south + north) - SHIFT
        from_west = jnp.concatenate([zero, masked[:-1]], axis=0)
        from_east = jnp.concatenate([masked[1:], zero], axis=0)
        from_south = jnp.where(row_at == 0, 0.0, pltpu.roll(masked, 1, axis=1))
        from_north = jnp.where(row_at == second - 1, 0.0, pltpu.roll(masked, second - 1, axis=1))
        drift = (
            west.reshape(1, 1, block) * from_west
            + east.reshape(1, 1, block) * from_east
            + south.reshape(1, 1, block) * from_south
            + north.reshape(1, 1, block) * from_north
        ).reshape(cells, block)
        out_ref[:, lanes] = diagonal * current - drift - scattered


def middle_kernel(sizes, per_owner, places, cols_ref, sources, blocks_ref, partial_ref, speed_ref, sign_ref, x_in, y_in, out_ref):
    first, second, local_blocks, block = sizes
    cells = first * second
    row_at = lax.broadcasted_iota(jnp.int32, (first, second, block), 1)
    for b in range(local_blocks):
        lanes = slice(b * block, (b + 1) * block)
        value = partial_ref[:, lanes]
        if places:
            value = value - scatter(sizes, per_owner, b, places, cols_ref, sources, blocks_ref)
        west, east, south, north = split_speeds(speed_ref, sign_ref, lanes)
        west_in, east_in = halos(x_in, "gx", lanes, (second, block))
        south_in, north_in = halos(y_in, "gy", lanes, (first, block))
        value = value.reshape(first, second, block)
        value = value - jnp.where(
            row_at == 0,
            (south * south_in)[:, None, :],
            jnp.where(row_at == second - 1, (north * north_in)[:, None, :], 0.0),
        )
        value = jnp.concatenate(
            [value[:1] - (west * west_in)[None], value[1:-1], value[-1:] - (east * east_in)[None]],
            axis=0,
        )
        out_ref[:, lanes] = value.reshape(cells, block)


def last_kernel(sizes, per_owner, places, cols_ref, sources, blocks_ref, partial_ref, earlier, open_ref, outs):
    first, second, local_blocks, block = sizes
    cells = first * second
    sums = {}
    for b in range(local_blocks):
        lanes = slice(b * block, (b + 1) * block)
        scattered = scatter(sizes, per_owner, b, places, cols_ref, sources, blocks_ref)
        result = partial_ref[:, lanes] - scattered
        if outs.gram is None:
            outs.value[:, lanes] = result
            outs.packed[:, lanes] = result.astype(jnp.bfloat16)
            write_faces(
                (result * open_ref[...]).reshape(first, second, block),
                lanes, first, second, outs.x, outs.y,
            )
        else:
            vectors = [ref[:, lanes] for ref in earlier] + [result]
            at = 0
            for i in range(len(vectors)):
                for j in range(i, len(vectors)):
                    term = jnp.sum((vectors[i] * vectors[j]).reshape(cells // 8, 8, block), axis=0)
                    sums[at] = term if b == 0 else sums[at] + term
                    at += 1
    if outs.gram is not None:
        devices = outs.gram.shape[0]
        lane = lax.broadcasted_iota(jnp.int32, (1, block), 1)
        row = jnp.zeros((1, block), jnp.float32)
        for at, value in sums.items():
            total = jnp.sum(jnp.sum(value, axis=0, keepdims=True), axis=1, keepdims=True)
            row = jnp.where(lane == at, total, row)
        outs.gram[...] = jnp.broadcast_to(row[None], (devices, 1, block))


class Outs:
    value = packed = gram = None
    x = y = ()


def least_squares(hessenberg, initial):
    upper = [list(row) for row in hessenberg]
    target = [initial] + [jnp.zeros_like(initial) for row_index in range(KRYLOV)]
    cosines = []
    sines = []
    for col_index in range(KRYLOV):
        for row_index in range(col_index):
            first = upper[row_index][col_index]
            second = upper[row_index + 1][col_index]
            upper[row_index][col_index] = cosines[row_index] * first + sines[row_index] * second
            upper[row_index + 1][col_index] = cosines[row_index] * second - sines[row_index] * first
        first = upper[col_index][col_index]
        second = upper[col_index + 1][col_index]
        radius = jnp.sqrt(first * first + second * second)
        cosine = first / radius
        sine_value = second / radius
        upper[col_index][col_index] = radius
        target[col_index + 1] = -sine_value * target[col_index]
        target[col_index] = cosine * target[col_index]
        cosines.append(cosine)
        sines.append(sine_value)
    combo = [None] * KRYLOV
    for row_index in reversed(range(KRYLOV)):
        running = target[row_index]
        for col_index in range(row_index + 1, KRYLOV):
            running = running - upper[row_index][col_index] * combo[col_index]
        combo[row_index] = running / upper[row_index][row_index]
    return combo


def arnoldi(gram):
    size = KRYLOV + 1

    def inner(left, right):
        total = None
        for i in range(size):
            for j in range(size):
                if left[i] is None or right[j] is None:
                    continue
                term = left[i] * right[j] * gram[min(i, j)][max(i, j)]
                total = term if total is None else total + term
        return total

    initial = jnp.sqrt(gram[0][0] + epsilon)
    basis = [[1.0 / initial] + [None] * KRYLOV]
    zero = jnp.zeros_like(initial)
    hessenberg = [[zero] * KRYLOV for row_index in range(size)]
    for section in range(KRYLOV):
        vector = basis[section]
        image = [None] * size
        for k in range(section + 2):
            parts = []
            if k > 0 and vector[k - 1] is not None:
                parts.append(vector[k - 1])
            if vector[k] is not None:
                parts.append(SHIFT * vector[k])
            image[k] = sum(parts[1:], parts[0])
        rest = list(image)
        for earlier in range(section + 1):
            coefficient = inner(basis[earlier], image)
            hessenberg[earlier][section] = coefficient
            for k in range(earlier + 1):
                rest[k] = rest[k] - coefficient * basis[earlier][k]
        length = jnp.sqrt(jnp.maximum(inner(rest, rest), 0.0) + epsilon)
        hessenberg[section + 1][section] = length
        basis.append([None if part is None else part / length for part in rest])
    combo = least_squares(hessenberg, initial)
    weights = []
    for k in range(KRYLOV):
        total = zero
        for j in range(k, KRYLOV):
            total = total + combo[j] * basis[j][k]
        weights.append(total)
    return hessenberg, weights


def finish_kernel(gram_ref, *refs):
    vectors, (solution_ref, hessenberg_ref) = refs[:KRYLOV], refs[KRYLOV:]
    block = gram_ref.shape[2]
    total = jnp.sum(gram_ref[...], axis=0)
    lane = lax.broadcasted_iota(jnp.int32, (1, block), 1)
    gram = [[None] * (KRYLOV + 1) for i in range(KRYLOV + 1)]
    at = 0
    for i in range(KRYLOV + 1):
        for j in range(i, KRYLOV + 1):
            entry = jnp.sum(jnp.where(lane == at, total, 0.0), axis=1, keepdims=True)
            gram[i][j] = jnp.broadcast_to(entry, (1, block))
            at += 1
    hessenberg, weights = arnoldi(gram)
    rows = lax.broadcasted_iota(jnp.int32, (KRYLOV + 1, KRYLOV), 0)
    cols = lax.broadcasted_iota(jnp.int32, (KRYLOV + 1, KRYLOV), 1)
    table = jnp.zeros((KRYLOV + 1, KRYLOV), jnp.float32)
    for i in range(KRYLOV + 1):
        for j in range(KRYLOV):
            table = jnp.where((rows == i) & (cols == j), hessenberg[i][j][:, :KRYLOV], table)
    hessenberg_ref[...] = table
    for b in range(solution_ref.shape[1] // block):
        lanes = slice(b * block, (b + 1) * block)
        solution_ref[:, lanes] = sum(
            weight * ref[:, lanes] for weight, ref in zip(weights, vectors)
        )


VMEM = pl.BlockSpec(memory_space=pltpu.VMEM)
ANY = pl.BlockSpec(memory_space=pl.ANY)
SCOPED = 16 * 1024 * 1024


def call(name, kernel, groups, shapes, scratch=(), flops=0):
    flat = [pair for group in groups for pair in group]

    def body(*refs):
        refs = list(refs)
        lists = []
        for group in groups:
            lists.append(refs[: len(group)])
            del refs[: len(group)]
        kernel(*lists, refs[: len(shapes)], refs[len(shapes) :])

    size = sum(operand.size * operand.dtype.itemsize for spec, operand in flat)
    size += sum(shape.size * shape.dtype.itemsize for shape in shapes)
    return pl.pallas_call(
        body,
        out_shape=list(shapes),
        in_specs=[spec for spec, operand in flat],
        out_specs=[VMEM] * len(shapes),
        scratch_shapes=list(scratch),
        compiler_params=pltpu.CompilerParams(vmem_limit_bytes=SCOPED),
        cost_estimate=pl.CostEstimate(flops=flops, bytes_accessed=size, transcendentals=0),
        name=name,
    )(*[operand for spec, operand in flat])


def in_vmem(operands):
    return [(VMEM, operand) for operand in operands]


def per_device(right_side, col_block, blocks, relax_rate, drift_speed, upwind_sign, wall_mask):
    first, second, local_modes = right_side.shape
    local_blocks, slots, block = blocks.shape[:3]
    cells = first * second
    count = lax.axis_size("mode")
    devices = count * lax.axis_size("gx") * lax.axis_size("gy")
    per_owner = slots // count
    sizes = (first, second, local_blocks, block)
    x_moves, y_moves = len(moves_of(lax.axis_size("gx"))), len(moves_of(lax.axis_size("gy")))
    n_faces = x_moves + y_moves
    f32 = jnp.float32
    shape_of = jax.ShapeDtypeStruct
    face_shapes = [shape_of((second, local_modes), f32)] * x_moves + [
        shape_of((first, local_modes), f32)
    ] * y_moves
    packed_shape = shape_of((cells, local_modes), jnp.bfloat16)
    vector_shape = shape_of((cells, local_modes), f32)
    near = [0]
    final = [place for place in range(3, count) if place % 2 == 1]
    middle = [place for place in range(1, count) if place not in final]

    start = right_side.reshape(cells, local_modes)
    packed = start.astype(jnp.bfloat16)

    def prepare(ins, outs, scratch):
        faces, (open_ref,) = outs[:n_faces], outs[n_faces:]
        prepare_kernel(sizes, *ins, faces[:x_moves], faces[x_moves:], open_ref)

    *faces, open_cells = call(
        "prepare",
        prepare,
        [in_vmem([start, wall_mask])],
        face_shapes + [shape_of((cells, block), f32)],
        flops=8 * 10**9,
    )
    columns = col_block.T

    work = 2 * cells * local_modes * per_owner * block
    vectors = [start]
    for section in range(KRYLOV):
        sources = {0: packed}
        held = gather_far(packed)
        y_in, x_in = move_faces({"gx": faces[:x_moves], "gy": faces[x_moves:]})

        def near_step(cols, sources, rest, params, outs, scratch):
            blocks_ref, current_ref, open_ref = rest
            near_kernel(
                sizes, per_owner, near, cols[0], sources, blocks_ref, current_ref, params,
                open_ref, outs[0],
            )

        (partial,) = call(
            "near_%d" % section,
            near_step,
            [
                in_vmem([columns]),
                in_vmem([sources[place] for place in near]),
                in_vmem([blocks, vectors[-1], open_cells]),
                in_vmem([relax_rate, drift_speed, upwind_sign]),
            ],
            [vector_shape],
            flops=work * len(near),
        )

        if count > 1:
            (own,) = hand_on([packed], [partial])
            sources[1] = exchange(own, 1)
        held = dict(zip(held, hand_on(list(held.values()), [partial, sources[1], *x_in, *y_in])))
        for place, array in held.items():
            sources[place] = array
            sources[place ^ 1] = exchange(array, 1)

        def middle_step(cols, sources, rest, x_in, y_in, outs, scratch):
            middle_kernel(
                sizes, per_owner, middle, cols[0], sources, *rest, x_in, y_in, outs[0]
            )

        (partial,) = call(
            "middle_%d" % section,
            middle_step,
            [
                in_vmem([columns]),
                in_vmem([sources[place] for place in middle]),
                in_vmem([blocks, partial, drift_speed, upwind_sign]),
                in_vmem(x_in),
                in_vmem(y_in),
            ],
            [vector_shape],
            flops=work * len(middle),
        )

        last = section == KRYLOV - 1
        def last_step(cols, sources, rest, earlier, outs, scratch, last=last):
            blocks_ref, partial_ref, open_ref = rest
            named = Outs()
            if last:
                named.gram = outs[0]
            else:
                named.x, named.y = outs[:x_moves], outs[x_moves:n_faces]
                named.packed, named.value = outs[n_faces:]
            last_kernel(
                sizes, per_owner, final, cols[0], sources, blocks_ref, partial_ref,
                earlier, open_ref, named,
            )

        if last:
            shapes = [shape_of((devices, 1, block), f32)]
        else:
            shapes = face_shapes + [packed_shape, vector_shape]
        results = call(
            "last_%d" % section,
            last_step,
            [
                in_vmem([columns]),
                in_vmem([sources[place] for place in final]),
                in_vmem([blocks, partial, open_cells]),
                in_vmem(vectors if last else []),
            ],
            shapes,
            flops=work * len(final),
        )
        if last:
            (gram,) = results
        else:
            *faces, packed, value = results
            vectors.append(value)

    gram = lax.all_to_all(gram, AXES, 0, 0)

    def finish(ins, outs, scratch):
        finish_kernel(*ins, *outs)

    solution, hessenberg = call(
        "finish",
        finish,
        [in_vmem([gram, *vectors])],
        [vector_shape, shape_of((KRYLOV + 1, KRYLOV), f32)],
    )
    return solution.reshape(first, second, local_modes), hessenberg


def solution(mesh):
    return jax.shard_map(
        per_device,
        mesh=mesh,
        in_specs=(
            P("gx", "gy", "mode"),
            P("mode", None),
            P("mode", None, None, None),
            P("mode"),
            P(None, "mode"),
            P(None, "mode"),
            P("gx", "gy"),
        ),
        out_specs=(P("gx", "gy", "mode"), P()),
        check_vma=False,
    )
```

```python
import functools

import jax
import jax.numpy as jnp
from jax import lax
from jax.experimental import pallas as pl
from jax.experimental.pallas import tpu as pltpu
from jax.sharding import PartitionSpec as P

KRYLOV = 3
SHIFT = 4.05
AXES = ("mode", "gx", "gy")

epsilon = 1e-12


def moves_of(count):
    if count == 1:
        return []
    if count == 2:
        return [[(0, 1), (1, 0)]]
    return [
        [(i, (i + 1) % count) for i in range(count)],
        [(i, (i - 1) % count) for i in range(count)],
    ]


def move_faces(faces):
    received = []
    for axis in ("gy", "gx"):
        moves = moves_of(lax.axis_size(axis))
        received.append([lax.ppermute(face, axis, pairs) for face, pairs in zip(faces[axis], moves)])
    return received


def exchange(array, bit):
    count = lax.axis_size("mode")
    return lax.ppermute(array, "mode", [(i, i ^ bit) for i in range(count)])


def gather_far(packed):
    held = {0: packed}
    bit = lax.axis_size("mode") // 2
    while bit > 1:
        for key in list(held):
            held[key ^ bit] = exchange(held[key], bit)
        bit //= 2
    del held[0]
    return held


def hand_on(arrays, after):
    count = len(arrays)
    if not count:
        return []
    return pl.pallas_call(
        lambda *refs: None,
        out_shape=[jax.ShapeDtypeStruct(array.shape, array.dtype) for array in arrays],
        in_specs=[ANY] * (count + len(after)),
        out_specs=[ANY] * count,
        input_output_aliases={at: at for at in range(count)},
        compiler_params=pltpu.CompilerParams(vmem_limit_bytes=SCOPED),
        name="hand_on",
    )(*arrays, *after)


def store_faces(refs, axis, lanes, low, high):
    if len(refs) == 1:
        refs[0][:, lanes] = jnp.where(lax.axis_index(axis) == 0, high, low)
    elif refs:
        refs[0][:, lanes] = high
        refs[1][:, lanes] = low


def write_faces(masked, lanes, first, second, x_refs, y_refs):
    store_faces(x_refs, "gx", lanes, masked[0], masked[first - 1])
    store_faces(y_refs, "gy", lanes, masked[:, 0, :], masked[:, second - 1, :])


def halos(refs, axis, lanes, shape):
    zero = jnp.zeros(shape, jnp.float32)
    if not refs:
        return zero, zero
    at = lax.axis_index(axis)
    low, high = refs[0][:, lanes], refs[-1][:, lanes]
    return jnp.where(at == 0, zero, low), jnp.where(at == lax.axis_size(axis) - 1, zero, high)


def prepare_kernel(sizes, rhs_ref, wall_ref, x_refs, y_refs, open_ref):
    first, second, local_blocks, block = sizes
    wall = wall_ref[...].astype(jnp.float32)
    eye = (
        lax.broadcasted_iota(jnp.int32, (second, second), 0)
        == lax.broadcasted_iota(jnp.int32, (second, second), 1)
    ).astype(jnp.float32)
    for row in range(first):
        column = jnp.sum(eye * (1.0 - wall[row : row + 1, :]), axis=1, keepdims=True)
        open_ref[row * second : (row + 1) * second, :] = jnp.broadcast_to(column, (second, block))
    for b in range(local_blocks):
        lanes = slice(b * block, (b + 1) * block)
        masked = (rhs_ref[:, lanes] * open_ref[...]).reshape(first, second, block)
        write_faces(masked, lanes, first, second, x_refs, y_refs)


def scatter(sizes, per_owner, b, places, cols_ref, sources, blocks_ref):
    first, second, local_blocks, block = sizes
    mine = lax.axis_index("mode")
    picks, weights = [], []
    for place, source in zip(places, sources):
        owner = mine ^ place
        for p in range(per_owner):
            slot = owner * per_owner + p
            column = cols_ref[slot, b] - owner * local_blocks
            picks.append(source[:, pl.ds(pl.multiple_of(column * block, block), block)])
            weights.append(blocks_ref[b, slot])
    return lax.dot_general(
        jnp.concatenate(picks, axis=1),
        jnp.concatenate(weights, axis=1),
        (((1,), (1,)), ((), ())),
        preferred_element_type=jnp.float32,
    )


def split_speeds(speed_ref, sign_ref, lanes):
    parts = []
    for axis in range(2):
        speed, sign = speed_ref[axis : axis + 1, lanes], sign_ref[axis : axis + 1, lanes]
        parts += [jnp.where(sign == 1, speed, 0.0), jnp.where(sign == 1, 0.0, speed)]
    return parts


def near_kernel(sizes, per_owner, places, cols_ref, sources, blocks_ref, current_ref, params, open_ref, out_ref):
    first, second, local_blocks, block = sizes
    cells = first * second
    open_cells = open_ref[...]
    row_at = lax.broadcasted_iota(jnp.int32, (first, second, block), 1)
    zero = jnp.zeros((1, second, block), jnp.float32)
    for b in range(local_blocks):
        lanes = slice(b * block, (b + 1) * block)
        scattered = scatter(sizes, per_owner, b, places, cols_ref, sources, blocks_ref)
        current = current_ref[:, lanes]
        masked = (current * open_cells).reshape(first, second, block)
        relax_ref, speed_ref, sign_ref = params
        west, east, south, north = split_speeds(speed_ref, sign_ref, lanes)
        diagonal = relax_ref[lanes].reshape(1, block) + (west + east) + (south + north) - SHIFT
        from_west = jnp.concatenate([zero, masked[:-1]], axis=0)
        from_east = jnp.concatenate([masked[1:], zero], axis=0)
        from_south = jnp.where(row_at == 0, 0.0, pltpu.roll(masked, 1, axis=1))
        from_north = jnp.where(row_at == second - 1, 0.0, pltpu.roll(masked, second - 1, axis=1))
        drift = (
            west.reshape(1, 1, block) * from_west
            + east.reshape(1, 1, block) * from_east
            + south.reshape(1, 1, block) * from_south
            + north.reshape(1, 1, block) * from_north
        ).reshape(cells, block)
        out_ref[:, lanes] = diagonal * current - drift - scattered


def middle_kernel(sizes, per_owner, places, cols_ref, sources, blocks_ref, partial_ref, speed_ref, sign_ref, x_in, y_in, out_ref):
    first, second, local_blocks, block = sizes
    cells = first * second
    row_at = lax.broadcasted_iota(jnp.int32, (first, second, block), 1)
    for b in range(local_blocks):
        lanes = slice(b * block, (b + 1) * block)
        value = partial_ref[:, lanes]
        if places:
            value = value - scatter(sizes, per_owner, b, places, cols_ref, sources, blocks_ref)
        west, east, south, north = split_speeds(speed_ref, sign_ref, lanes)
        west_in, east_in = halos(x_in, "gx", lanes, (second, block))
        south_in, north_in = halos(y_in, "gy", lanes, (first, block))
        value = value.reshape(first, second, block)
        value = value - jnp.where(
            row_at == 0,
            (south * south_in)[:, None, :],
            jnp.where(row_at == second - 1, (north * north_in)[:, None, :], 0.0),
        )
        value = jnp.concatenate(
            [value[:1] - (west * west_in)[None], value[1:-1], value[-1:] - (east * east_in)[None]],
            axis=0,
        )
        out_ref[:, lanes] = value.reshape(cells, block)


def last_kernel(sizes, per_owner, places, cols_ref, sources, blocks_ref, partial_ref, earlier, open_ref, outs):
    first, second, local_blocks, block = sizes
    cells = first * second
    sums = {}
    for b in range(local_blocks):
        lanes = slice(b * block, (b + 1) * block)
        scattered = scatter(sizes, per_owner, b, places, cols_ref, sources, blocks_ref)
        result = partial_ref[:, lanes] - scattered
        if outs.gram is None:
            outs.value[:, lanes] = result
            outs.packed[:, lanes] = result.astype(jnp.bfloat16)
            write_faces(
                (result * open_ref[...]).reshape(first, second, block),
                lanes, first, second, outs.x, outs.y,
            )
        else:
            vectors = [ref[:, lanes] for ref in earlier] + [result]
            at = 0
            for i in range(len(vectors)):
                for j in range(i, len(vectors)):
                    term = jnp.sum((vectors[i] * vectors[j]).reshape(cells // 8, 8, block), axis=0)
                    sums[at] = term if b == 0 else sums[at] + term
                    at += 1
    if outs.gram is not None:
        devices = outs.gram.shape[0]
        lane = lax.broadcasted_iota(jnp.int32, (1, block), 1)
        row = jnp.zeros((1, block), jnp.float32)
        for at, value in sums.items():
            total = jnp.sum(jnp.sum(value, axis=0, keepdims=True), axis=1, keepdims=True)
            row = jnp.where(lane == at, total, row)
        outs.gram[...] = jnp.broadcast_to(row[None], (devices, 1, block))


class Outs:
    value = packed = gram = None
    x = y = ()


def least_squares(hessenberg, initial):
    upper = [list(row) for row in hessenberg]
    target = [initial] + [jnp.zeros_like(initial) for row_index in range(KRYLOV)]
    cosines = []
    sines = []
    for col_index in range(KRYLOV):
        for row_index in range(col_index):
            first = upper[row_index][col_index]
            second = upper[row_index + 1][col_index]
            upper[row_index][col_index] = cosines[row_index] * first + sines[row_index] * second
            upper[row_index + 1][col_index] = cosines[row_index] * second - sines[row_index] * first
        first = upper[col_index][col_index]
        second = upper[col_index + 1][col_index]
        radius = jnp.sqrt(first * first + second * second)
        cosine = first / radius
        sine_value = second / radius
        upper[col_index][col_index] = radius
        target[col_index + 1] = -sine_value * target[col_index]
        target[col_index] = cosine * target[col_index]
        cosines.append(cosine)
        sines.append(sine_value)
    combo = [None] * KRYLOV
    for row_index in reversed(range(KRYLOV)):
        running = target[row_index]
        for col_index in range(row_index + 1, KRYLOV):
            running = running - upper[row_index][col_index] * combo[col_index]
        combo[row_index] = running / upper[row_index][row_index]
    return combo


def arnoldi(gram):
    size = KRYLOV + 1

    def inner(left, right):
        total = None
        for i in range(size):
            for j in range(size):
                if left[i] is None or right[j] is None:
                    continue
                term = left[i] * right[j] * gram[min(i, j)][max(i, j)]
                total = term if total is None else total + term
        return total

    initial = jnp.sqrt(gram[0][0] + epsilon)
    basis = [[1.0 / initial] + [None] * KRYLOV]
    zero = jnp.zeros_like(initial)
    hessenberg = [[zero] * KRYLOV for row_index in range(size)]
    for section in range(KRYLOV):
        vector = basis[section]
        image = [None] * size
        for k in range(section + 2):
            parts = []
            if k > 0 and vector[k - 1] is not None:
                parts.append(vector[k - 1])
            if vector[k] is not None:
                parts.append(SHIFT * vector[k])
            image[k] = sum(parts[1:], parts[0])
        rest = list(image)
        for earlier in range(section + 1):
            coefficient = inner(basis[earlier], image)
            hessenberg[earlier][section] = coefficient
            for k in range(earlier + 1):
                rest[k] = rest[k] - coefficient * basis[earlier][k]
        length = jnp.sqrt(jnp.maximum(inner(rest, rest), 0.0) + epsilon)
        hessenberg[section + 1][section] = length
        basis.append([None if part is None else part / length for part in rest])
    combo = least_squares(hessenberg, initial)
    weights = []
    for k in range(KRYLOV):
        total = zero
        for j in range(k, KRYLOV):
            total = total + combo[j] * basis[j][k]
        weights.append(total)
    return hessenberg, weights


def finish_kernel(gram_ref, *refs):
    vectors, (solution_ref, hessenberg_ref) = refs[:KRYLOV], refs[KRYLOV:]
    block = gram_ref.shape[2]
    total = jnp.sum(gram_ref[...], axis=0)
    lane = lax.broadcasted_iota(jnp.int32, (1, block), 1)
    gram = [[None] * (KRYLOV + 1) for i in range(KRYLOV + 1)]
    at = 0
    for i in range(KRYLOV + 1):
        for j in range(i, KRYLOV + 1):
            entry = jnp.sum(jnp.where(lane == at, total, 0.0), axis=1, keepdims=True)
            gram[i][j] = jnp.broadcast_to(entry, (1, block))
            at += 1
    hessenberg, weights = arnoldi(gram)
    rows = lax.broadcasted_iota(jnp.int32, (KRYLOV + 1, KRYLOV), 0)
    cols = lax.broadcasted_iota(jnp.int32, (KRYLOV + 1, KRYLOV), 1)
    table = jnp.zeros((KRYLOV + 1, KRYLOV), jnp.float32)
    for i in range(KRYLOV + 1):
        for j in range(KRYLOV):
            table = jnp.where((rows == i) & (cols == j), hessenberg[i][j][:, :KRYLOV], table)
    hessenberg_ref[...] = table
    for b in range(solution_ref.shape[1] // block):
        lanes = slice(b * block, (b + 1) * block)
        solution_ref[:, lanes] = sum(
            weight * ref[:, lanes] for weight, ref in zip(weights, vectors)
        )


VMEM = pl.BlockSpec(memory_space=pltpu.VMEM)
ANY = pl.BlockSpec(memory_space=pl.ANY)
SCOPED = 16 * 1024 * 1024


def call(name, kernel, groups, shapes, scratch=(), flops=0):
    flat = [pair for group in groups for pair in group]

    def body(*refs):
        refs = list(refs)
        lists = []
        for group in groups:
            lists.append(refs[: len(group)])
            del refs[: len(group)]
        kernel(*lists, refs[: len(shapes)], refs[len(shapes) :])

    size = sum(operand.size * operand.dtype.itemsize for spec, operand in flat)
    size += sum(shape.size * shape.dtype.itemsize for shape in shapes)
    return pl.pallas_call(
        body,
        out_shape=list(shapes),
        in_specs=[spec for spec, operand in flat],
        out_specs=[VMEM] * len(shapes),
        scratch_shapes=list(scratch),
        compiler_params=pltpu.CompilerParams(vmem_limit_bytes=SCOPED),
        cost_estimate=pl.CostEstimate(flops=flops, bytes_accessed=size, transcendentals=0),
        name=name,
    )(*[operand for spec, operand in flat])


def in_vmem(operands):
    return [(VMEM, operand) for operand in operands]


def per_device(right_side, col_block, blocks, relax_rate, drift_speed, upwind_sign, wall_mask):
    first, second, local_modes = right_side.shape
    local_blocks, slots, block = blocks.shape[:3]
    cells = first * second
    count = lax.axis_size("mode")
    devices = count * lax.axis_size("gx") * lax.axis_size("gy")
    per_owner = slots // count
    sizes = (first, second, local_blocks, block)
    x_moves, y_moves = len(moves_of(lax.axis_size("gx"))), len(moves_of(lax.axis_size("gy")))
    n_faces = x_moves + y_moves
    f32 = jnp.float32
    shape_of = jax.ShapeDtypeStruct
    face_shapes = [shape_of((second, local_modes), f32)] * x_moves + [
        shape_of((first, local_modes), f32)
    ] * y_moves
    packed_shape = shape_of((cells, local_modes), jnp.bfloat16)
    vector_shape = shape_of((cells, local_modes), f32)
    near = [place for place in (0, 1) if place < count]
    final = [place for place in range(3, count) if place % 2 == 1]
    middle = [place for place in range(2, count) if place not in final]

    start = right_side.reshape(cells, local_modes)
    packed = start.astype(jnp.bfloat16)

    def prepare(ins, outs, scratch):
        faces, (open_ref,) = outs[:n_faces], outs[n_faces:]
        prepare_kernel(sizes, *ins, faces[:x_moves], faces[x_moves:], open_ref)

    *faces, open_cells = call(
        "prepare",
        prepare,
        [in_vmem([start, wall_mask])],
        face_shapes + [shape_of((cells, block), f32)],
        flops=8 * 10**9,
    )
    columns = col_block.T

    work = 2 * cells * local_modes * per_owner * block
    vectors = [start]
    for section in range(KRYLOV):
        sources = {0: packed}
        if count > 1:
            sources[1] = exchange(packed, 1)
        held = gather_far(packed)
        y_in, x_in = move_faces({"gx": faces[:x_moves], "gy": faces[x_moves:]})

        def near_step(cols, sources, rest, params, outs, scratch):
            blocks_ref, current_ref, open_ref = rest
            near_kernel(
                sizes, per_owner, near, cols[0], sources, blocks_ref, current_ref, params,
                open_ref, outs[0],
            )

        (partial,) = call(
            "near_%d" % section,
            near_step,
            [
                in_vmem([columns]),
                in_vmem([sources[place] for place in near]),
                in_vmem([blocks, vectors[-1], open_cells]),
                in_vmem([relax_rate, drift_speed, upwind_sign]),
            ],
            [vector_shape],
            flops=work * len(near),
        )

        held = dict(zip(held, hand_on(list(held.values()), [partial, *x_in, *y_in])))
        for place, array in held.items():
            sources[place] = array
            sources[place ^ 1] = exchange(array, 1)

        def middle_step(cols, sources, rest, x_in, y_in, outs, scratch):
            middle_kernel(
                sizes, per_owner, middle, cols[0], sources, *rest, x_in, y_in, outs[0]
            )

        (partial,) = call(
            "middle_%d" % section,
            middle_step,
            [
                in_vmem([columns]),
                in_vmem([sources[place] for place in middle]),
                in_vmem([blocks, partial, drift_speed, upwind_sign]),
                in_vmem(x_in),
                in_vmem(y_in),
            ],
            [vector_shape],
            flops=work * len(middle),
        )

        last = section == KRYLOV - 1
        def last_step(cols, sources, rest, earlier, outs, scratch, last=last):
            blocks_ref, partial_ref, open_ref = rest
            named = Outs()
            if last:
                named.gram = outs[0]
            else:
                named.x, named.y = outs[:x_moves], outs[x_moves:n_faces]
                named.packed, named.value = outs[n_faces:]
            last_kernel(
                sizes, per_owner, final, cols[0], sources, blocks_ref, partial_ref,
                earlier, open_ref, named,
            )

        if last:
            shapes = [shape_of((devices, 1, block), f32)]
        else:
            shapes = face_shapes + [packed_shape, vector_shape]
        results = call(
            "last_%d" % section,
            last_step,
            [
                in_vmem([columns]),
                in_vmem([sources[place] for place in final]),
                in_vmem([blocks, partial, open_cells]),
                in_vmem(vectors if last else []),
            ],
            shapes,
            flops=work * len(final),
        )
        if last:
            (gram,) = results
        else:
            *faces, packed, value = results
            vectors.append(value)

    gram = lax.all_to_all(gram, AXES, 0, 0)

    def finish(ins, outs, scratch):
        finish_kernel(*ins, *outs)

    solution, hessenberg = call(
        "finish",
        finish,
        [in_vmem([gram, *vectors])],
        [vector_shape, shape_of((KRYLOV + 1, KRYLOV), f32)],
    )
    return solution.reshape(first, second, local_modes), hessenberg


def solution(mesh):
    return jax.shard_map(
        per_device,
        mesh=mesh,
        in_specs=(
            P("gx", "gy", "mode"),
            P("mode", None),
            P("mode", None, None, None),
            P("mode"),
            P(None, "mode"),
            P(None, "mode"),
            P("gx", "gy"),
        ),
        out_specs=(P("gx", "gy", "mode"), P()),
        check_vma=False,
    )
```

```python
import functools

import jax
import jax.numpy as jnp
from jax import lax
from jax.experimental import pallas as pl
from jax.experimental.pallas import tpu as pltpu
from jax.sharding import PartitionSpec as P

KRYLOV = 3
SHIFT = 4.05
AXES = ("mode", "gx", "gy")

epsilon = 1e-12


def moves_of(count):
    if count == 1:
        return []
    if count == 2:
        return [[(0, 1), (1, 0)]]
    return [
        [(i, (i + 1) % count) for i in range(count)],
        [(i, (i - 1) % count) for i in range(count)],
    ]


def move_faces(faces):
    received = []
    for axis in ("gy", "gx"):
        moves = moves_of(lax.axis_size(axis))
        received.append([lax.ppermute(face, axis, pairs) for face, pairs in zip(faces[axis], moves)])
    return received


def exchange(array, bit):
    count = lax.axis_size("mode")
    return lax.ppermute(array, "mode", [(i, i ^ bit) for i in range(count)])


def gather_far(packed):
    held = {0: packed}
    bit = lax.axis_size("mode") // 2
    while bit > 1:
        for key in list(held):
            held[key ^ bit] = exchange(held[key], bit)
        bit //= 2
    del held[0]
    return held


def hand_on(arrays, after):
    count = len(arrays)
    if not count:
        return []
    return pl.pallas_call(
        lambda *refs: None,
        out_shape=[jax.ShapeDtypeStruct(array.shape, array.dtype) for array in arrays],
        in_specs=[ANY] * (count + len(after)),
        out_specs=[ANY] * count,
        input_output_aliases={at: at for at in range(count)},
        compiler_params=pltpu.CompilerParams(vmem_limit_bytes=SCOPED),
        name="hand_on",
    )(*arrays, *after)


def store_faces(refs, axis, lanes, low, high):
    if len(refs) == 1:
        refs[0][:, lanes] = jnp.where(lax.axis_index(axis) == 0, high, low)
    elif refs:
        refs[0][:, lanes] = high
        refs[1][:, lanes] = low


def write_faces(masked, lanes, first, second, x_refs, y_refs):
    store_faces(x_refs, "gx", lanes, masked[0], masked[first - 1])
    store_faces(y_refs, "gy", lanes, masked[:, 0, :], masked[:, second - 1, :])


def halos(refs, axis, lanes, shape):
    zero = jnp.zeros(shape, jnp.float32)
    if not refs:
        return zero, zero
    at = lax.axis_index(axis)
    low, high = refs[0][:, lanes], refs[-1][:, lanes]
    return jnp.where(at == 0, zero, low), jnp.where(at == lax.axis_size(axis) - 1, zero, high)


def prepare_kernel(sizes, rhs_ref, wall_ref, x_refs, y_refs, open_ref):
    first, second, local_blocks, block = sizes
    wall = wall_ref[...].astype(jnp.float32)
    eye = (
        lax.broadcasted_iota(jnp.int32, (second, second), 0)
        == lax.broadcasted_iota(jnp.int32, (second, second), 1)
    ).astype(jnp.float32)
    for row in range(first):
        column = jnp.sum(eye * (1.0 - wall[row : row + 1, :]), axis=1, keepdims=True)
        open_ref[row * second : (row + 1) * second, :] = jnp.broadcast_to(column, (second, block))
    for b in range(local_blocks):
        lanes = slice(b * block, (b + 1) * block)
        masked = (rhs_ref[:, lanes] * open_ref[...]).reshape(first, second, block)
        write_faces(masked, lanes, first, second, x_refs, y_refs)


def scatter(sizes, per_owner, b, places, cols_ref, sources, blocks_ref):
    first, second, local_blocks, block = sizes
    mine = lax.axis_index("mode")
    picks, weights = [], []
    for place, source in zip(places, sources):
        owner = mine ^ place
        for p in range(per_owner):
            slot = owner * per_owner + p
            column = cols_ref[slot, b] - owner * local_blocks
            picks.append(source[:, pl.ds(pl.multiple_of(column * block, block), block)])
            weights.append(blocks_ref[b, slot])
    return lax.dot_general(
        jnp.concatenate(picks, axis=1),
        jnp.concatenate(weights, axis=1),
        (((1,), (1,)), ((), ())),
        preferred_element_type=jnp.float32,
    )


def split_speeds(speed_ref, sign_ref, lanes):
    parts = []
    for axis in range(2):
        speed, sign = speed_ref[axis : axis + 1, lanes], sign_ref[axis : axis + 1, lanes]
        parts += [jnp.where(sign == 1, speed, 0.0), jnp.where(sign == 1, 0.0, speed)]
    return parts


def near_kernel(sizes, per_owner, places, cols_ref, sources, blocks_ref, current_ref, params, open_ref, out_ref):
    first, second, local_blocks, block = sizes
    cells = first * second
    open_cells = open_ref[...]
    row_at = lax.broadcasted_iota(jnp.int32, (first, second, block), 1)
    zero = jnp.zeros((1, second, block), jnp.float32)
    for b in range(local_blocks):
        lanes = slice(b * block, (b + 1) * block)
        scattered = scatter(sizes, per_owner, b, places, cols_ref, sources, blocks_ref)
        current = current_ref[:, lanes]
        masked = (current * open_cells).reshape(first, second, block)
        relax_ref, speed_ref, sign_ref = params
        west, east, south, north = split_speeds(speed_ref, sign_ref, lanes)
        diagonal = relax_ref[lanes].reshape(1, block) + (west + east) + (south + north) - SHIFT
        from_west = jnp.concatenate([zero, masked[:-1]], axis=0)
        from_east = jnp.concatenate([masked[1:], zero], axis=0)
        from_south = jnp.where(row_at == 0, 0.0, pltpu.roll(masked, 1, axis=1))
        from_north = jnp.where(row_at == second - 1, 0.0, pltpu.roll(masked, second - 1, axis=1))
        drift = (
            west.reshape(1, 1, block) * from_west
            + east.reshape(1, 1, block) * from_east
            + south.reshape(1, 1, block) * from_south
            + north.reshape(1, 1, block) * from_north
        ).reshape(cells, block)
        out_ref[:, lanes] = diagonal * current - drift - scattered


def middle_kernel(sizes, per_owner, places, cols_ref, sources, blocks_ref, partial_ref, speed_ref, sign_ref, x_in, y_in, out_ref):
    first, second, local_blocks, block = sizes
    cells = first * second
    row_at = lax.broadcasted_iota(jnp.int32, (first, second, block), 1)
    for b in range(local_blocks):
        lanes = slice(b * block, (b + 1) * block)
        value = partial_ref[:, lanes]
        if places:
            value = value - scatter(sizes, per_owner, b, places, cols_ref, sources, blocks_ref)
        west, east, south, north = split_speeds(speed_ref, sign_ref, lanes)
        west_in, east_in = halos(x_in, "gx", lanes, (second, block))
        south_in, north_in = halos(y_in, "gy", lanes, (first, block))
        value = value.reshape(first, second, block)
        value = value - jnp.where(
            row_at == 0,
            (south * south_in)[:, None, :],
            jnp.where(row_at == second - 1, (north * north_in)[:, None, :], 0.0),
        )
        value = jnp.concatenate(
            [value[:1] - (west * west_in)[None], value[1:-1], value[-1:] - (east * east_in)[None]],
            axis=0,
        )
        out_ref[:, lanes] = value.reshape(cells, block)


def last_kernel(sizes, per_owner, places, cols_ref, sources, blocks_ref, partial_ref, earlier, open_ref, outs):
    first, second, local_blocks, block = sizes
    cells = first * second
    sums = {}
    for b in range(local_blocks):
        lanes = slice(b * block, (b + 1) * block)
        scattered = scatter(sizes, per_owner, b, places, cols_ref, sources, blocks_ref)
        result = partial_ref[:, lanes] - scattered
        if outs.gram is None:
            outs.value[:, lanes] = result
            outs.packed[:, lanes] = result.astype(jnp.bfloat16)
            write_faces(
                (result * open_ref[...]).reshape(first, second, block),
                lanes, first, second, outs.x, outs.y,
            )
        else:
            vectors = [ref[:, lanes] for ref in earlier] + [result]
            at = 0
            for i in range(len(vectors)):
                for j in range(i, len(vectors)):
                    term = jnp.sum((vectors[i] * vectors[j]).reshape(cells // 8, 8, block), axis=0)
                    sums[at] = term if b == 0 else sums[at] + term
                    at += 1
    if outs.gram is not None:
        devices = outs.gram.shape[0]
        lane = lax.broadcasted_iota(jnp.int32, (1, block), 1)
        row = jnp.zeros((1, block), jnp.float32)
        for at, value in sums.items():
            total = jnp.sum(jnp.sum(value, axis=0, keepdims=True), axis=1, keepdims=True)
            row = jnp.where(lane == at, total, row)
        outs.gram[...] = jnp.broadcast_to(row[None], (devices, 1, block))


class Outs:
    value = packed = gram = None
    x = y = ()


def least_squares(hessenberg, initial):
    upper = [list(row) for row in hessenberg]
    target = [initial] + [jnp.zeros_like(initial) for row_index in range(KRYLOV)]
    cosines = []
    sines = []
    for col_index in range(KRYLOV):
        for row_index in range(col_index):
            first = upper[row_index][col_index]
            second = upper[row_index + 1][col_index]
            upper[row_index][col_index] = cosines[row_index] * first + sines[row_index] * second
            upper[row_index + 1][col_index] = cosines[row_index] * second - sines[row_index] * first
        first = upper[col_index][col_index]
        second = upper[col_index + 1][col_index]
        radius = jnp.sqrt(first * first + second * second)
        cosine = first / radius
        sine_value = second / radius
        upper[col_index][col_index] = radius
        target[col_index + 1] = -sine_value * target[col_index]
        target[col_index] = cosine * target[col_index]
        cosines.append(cosine)
        sines.append(sine_value)
    combo = [None] * KRYLOV
    for row_index in reversed(range(KRYLOV)):
        running = target[row_index]
        for col_index in range(row_index + 1, KRYLOV):
            running = running - upper[row_index][col_index] * combo[col_index]
        combo[row_index] = running / upper[row_index][row_index]
    return combo


def arnoldi(gram):
    size = KRYLOV + 1

    def inner(left, right):
        total = None
        for i in range(size):
            for j in range(size):
                if left[i] is None or right[j] is None:
                    continue
                term = left[i] * right[j] * gram[min(i, j)][max(i, j)]
                total = term if total is None else total + term
        return total

    initial = jnp.sqrt(gram[0][0] + epsilon)
    basis = [[1.0 / initial] + [None] * KRYLOV]
    zero = jnp.zeros_like(initial)
    hessenberg = [[zero] * KRYLOV for row_index in range(size)]
    for section in range(KRYLOV):
        vector = basis[section]
        image = [None] * size
        for k in range(section + 2):
            parts = []
            if k > 0 and vector[k - 1] is not None:
                parts.append(vector[k - 1])
            if vector[k] is not None:
                parts.append(SHIFT * vector[k])
            image[k] = sum(parts[1:], parts[0])
        rest = list(image)
        for earlier in range(section + 1):
            coefficient = inner(basis[earlier], image)
            hessenberg[earlier][section] = coefficient
            for k in range(earlier + 1):
                rest[k] = rest[k] - coefficient * basis[earlier][k]
        length = jnp.sqrt(jnp.maximum(inner(rest, rest), 0.0) + epsilon)
        hessenberg[section + 1][section] = length
        basis.append([None if part is None else part / length for part in rest])
    combo = least_squares(hessenberg, initial)
    weights = []
    for k in range(KRYLOV):
        total = zero
        for j in range(k, KRYLOV):
            total = total + combo[j] * basis[j][k]
        weights.append(total)
    return hessenberg, weights


def finish_kernel(gram_ref, *refs):
    vectors, (solution_ref, hessenberg_ref) = refs[:KRYLOV], refs[KRYLOV:]
    block = gram_ref.shape[2]
    total = jnp.sum(gram_ref[...], axis=0)
    lane = lax.broadcasted_iota(jnp.int32, (1, block), 1)
    gram = [[None] * (KRYLOV + 1) for i in range(KRYLOV + 1)]
    at = 0
    for i in range(KRYLOV + 1):
        for j in range(i, KRYLOV + 1):
            entry = jnp.sum(jnp.where(lane == at, total, 0.0), axis=1, keepdims=True)
            gram[i][j] = jnp.broadcast_to(entry, (1, block))
            at += 1
    hessenberg, weights = arnoldi(gram)
    rows = lax.broadcasted_iota(jnp.int32, (KRYLOV + 1, KRYLOV), 0)
    cols = lax.broadcasted_iota(jnp.int32, (KRYLOV + 1, KRYLOV), 1)
    table = jnp.zeros((KRYLOV + 1, KRYLOV), jnp.float32)
    for i in range(KRYLOV + 1):
        for j in range(KRYLOV):
            table = jnp.where((rows == i) & (cols == j), hessenberg[i][j][:, :KRYLOV], table)
    hessenberg_ref[...] = table
    for b in range(solution_ref.shape[1] // block):
        lanes = slice(b * block, (b + 1) * block)
        solution_ref[:, lanes] = sum(
            weight * ref[:, lanes] for weight, ref in zip(weights, vectors)
        )


VMEM = pl.BlockSpec(memory_space=pltpu.VMEM)
ANY = pl.BlockSpec(memory_space=pl.ANY)
SCOPED = 16 * 1024 * 1024


def call(name, kernel, groups, shapes, scratch=(), flops=0):
    flat = [pair for group in groups for pair in group]

    def body(*refs):
        refs = list(refs)
        lists = []
        for group in groups:
            lists.append(refs[: len(group)])
            del refs[: len(group)]
        kernel(*lists, refs[: len(shapes)], refs[len(shapes) :])

    size = sum(operand.size * operand.dtype.itemsize for spec, operand in flat)
    size += sum(shape.size * shape.dtype.itemsize for shape in shapes)
    return pl.pallas_call(
        body,
        out_shape=list(shapes),
        in_specs=[spec for spec, operand in flat],
        out_specs=[VMEM] * len(shapes),
        scratch_shapes=list(scratch),
        compiler_params=pltpu.CompilerParams(vmem_limit_bytes=SCOPED),
        cost_estimate=pl.CostEstimate(flops=flops, bytes_accessed=size, transcendentals=0),
        name=name,
    )(*[operand for spec, operand in flat])


def in_vmem(operands):
    return [(VMEM, operand) for operand in operands]


def per_device(right_side, col_block, blocks, relax_rate, drift_speed, upwind_sign, wall_mask):
    first, second, local_modes = right_side.shape
    local_blocks, slots, block = blocks.shape[:3]
    cells = first * second
    count = lax.axis_size("mode")
    devices = count * lax.axis_size("gx") * lax.axis_size("gy")
    per_owner = slots // count
    sizes = (first, second, local_blocks, block)
    x_moves, y_moves = len(moves_of(lax.axis_size("gx"))), len(moves_of(lax.axis_size("gy")))
    n_faces = x_moves + y_moves
    f32 = jnp.float32
    shape_of = jax.ShapeDtypeStruct
    face_shapes = [shape_of((second, local_modes), f32)] * x_moves + [
        shape_of((first, local_modes), f32)
    ] * y_moves
    packed_shape = shape_of((cells, local_modes), jnp.bfloat16)
    vector_shape = shape_of((cells, local_modes), f32)
    near = [place for place in (0, 1) if place < count]
    final = [place for place in range(3, count) if place % 2 == 1]
    middle = [place for place in range(2, count) if place not in final]

    start = right_side.reshape(cells, local_modes)

    def pack(ins, outs, scratch):
        outs[0][...] = ins[0][...].astype(jnp.bfloat16)

    (packed,) = call("pack", pack, [in_vmem([start])], [packed_shape], flops=4 * 10**9)

    def prepare(ins, outs, scratch):
        faces, (open_ref,) = outs[:n_faces], outs[n_faces:]
        prepare_kernel(sizes, *ins, faces[:x_moves], faces[x_moves:], open_ref)

    *faces, open_cells = call(
        "prepare",
        prepare,
        [in_vmem([start, wall_mask])],
        face_shapes + [shape_of((cells, block), f32)],
        flops=8 * 10**9,
    )
    columns = col_block.T

    work = 2 * cells * local_modes * per_owner * block
    vectors = [start]
    for section in range(KRYLOV):
        sources = {0: packed}
        if count > 1:
            sources[1] = exchange(packed, 1)
        held = gather_far(packed)
        y_in, x_in = move_faces({"gx": faces[:x_moves], "gy": faces[x_moves:]})

        def near_step(cols, sources, rest, params, outs, scratch):
            blocks_ref, current_ref, open_ref = rest
            near_kernel(
                sizes, per_owner, near, cols[0], sources, blocks_ref, current_ref, params,
                open_ref, outs[0],
            )

        (partial,) = call(
            "near_%d" % section,
            near_step,
            [
                in_vmem([columns]),
                in_vmem([sources[place] for place in near]),
                in_vmem([blocks, vectors[-1], open_cells]),
                in_vmem([relax_rate, drift_speed, upwind_sign]),
            ],
            [vector_shape],
            flops=work * len(near),
        )

        held = dict(zip(held, hand_on(list(held.values()), [partial, *y_in, *x_in])))
        for place, array in held.items():
            sources[place] = array
            sources[place ^ 1] = exchange(array, 1)

        def middle_step(cols, sources, rest, y_in, x_in, outs, scratch):
            middle_kernel(
                sizes, per_owner, middle, cols[0], sources, *rest, x_in, y_in, outs[0]
            )

        (partial,) = call(
            "middle_%d" % section,
            middle_step,
            [
                in_vmem([columns]),
                in_vmem([sources[place] for place in middle]),
                in_vmem([blocks, partial, drift_speed, upwind_sign]),
                in_vmem(y_in),
                in_vmem(x_in),
            ],
            [vector_shape],
            flops=work * len(middle),
        )

        last = section == KRYLOV - 1
        def last_step(cols, sources, rest, earlier, outs, scratch, last=last):
            blocks_ref, partial_ref, open_ref = rest
            named = Outs()
            if last:
                named.gram = outs[0]
            else:
                named.x, named.y = outs[:x_moves], outs[x_moves:n_faces]
                named.packed, named.value = outs[n_faces:]
            last_kernel(
                sizes, per_owner, final, cols[0], sources, blocks_ref, partial_ref,
                earlier, open_ref, named,
            )

        if last:
            shapes = [shape_of((devices, 1, block), f32)]
        else:
            shapes = face_shapes + [packed_shape, vector_shape]
        results = call(
            "last_%d" % section,
            last_step,
            [
                in_vmem([columns]),
                in_vmem([sources[place] for place in final]),
                in_vmem([blocks, partial, open_cells]),
                in_vmem(vectors if last else []),
            ],
            shapes,
            flops=work * len(final),
        )
        if last:
            (gram,) = results
        else:
            *faces, packed, value = results
            vectors.append(value)

    gram = lax.all_to_all(gram, AXES, 0, 0)

    def finish(ins, outs, scratch):
        finish_kernel(*ins, *outs)

    solution, hessenberg = call(
        "finish",
        finish,
        [in_vmem([gram, *vectors])],
        [vector_shape, shape_of((KRYLOV + 1, KRYLOV), f32)],
    )
    return solution.reshape(first, second, local_modes), hessenberg


def solution(mesh):
    return jax.shard_map(
        per_device,
        mesh=mesh,
        in_specs=(
            P("gx", "gy", "mode"),
            P("mode", None),
            P("mode", None, None, None),
            P("mode"),
            P(None, "mode"),
            P(None, "mode"),
            P("gx", "gy"),
        ),
        out_specs=(P("gx", "gy", "mode"), P()),
        check_vma=False,
    )
```

```python
import functools

import jax
import jax.numpy as jnp
from jax import lax
from jax.experimental import pallas as pl
from jax.experimental.pallas import tpu as pltpu
from jax.sharding import PartitionSpec as P

KRYLOV = 3
SHIFT = 4.05
AXES = ("mode", "gx", "gy")

epsilon = 1e-12


def moves_of(count):
    moves = []
    for first in (0, 1)[: count - 1]:
        partner = list(range(count))
        for low in range(first, count - 1, 2):
            partner[low], partner[low + 1] = low + 1, low
        moves.append(partner)
    return moves


def move_faces(faces):
    received = []
    shards = lax.axis_size("mode")
    for axis in ("gy", "gx"):
        count = lax.axis_size(axis)
        arrived = []
        for face, partner in zip(faces[axis], moves_of(count)):
            pairs = []
            for shard in range(shards):
                for at in range(count):
                    alone = partner[at] == at
                    other = (shard ^ 1 if alone and shards > 1 else shard) * count + partner[at]
                    pairs.append((shard * count + at, other))
            arrived.append(lax.ppermute(face, ("mode", axis), pairs))
        received.append(arrived)
    return received


def exchange(array, bit):
    count = lax.axis_size("mode")
    return lax.ppermute(array, "mode", [(i, i ^ bit) for i in range(count)])


def gather_far(packed):
    held = {0: packed}
    bit = lax.axis_size("mode") // 2
    while bit > 1:
        for key in list(held):
            held[key ^ bit] = exchange(held[key], bit)
        bit //= 2
    del held[0]
    return held


def hand_on(arrays, after):
    count = len(arrays)
    if not count:
        return []
    return pl.pallas_call(
        lambda *refs: None,
        out_shape=[jax.ShapeDtypeStruct(array.shape, array.dtype) for array in arrays],
        in_specs=[ANY] * (count + len(after)),
        out_specs=[ANY] * count,
        input_output_aliases={at: at for at in range(count)},
        compiler_params=pltpu.CompilerParams(vmem_limit_bytes=SCOPED),
        name="hand_on",
    )(*arrays, *after)


def store_faces(refs, axis, lanes, low, high):
    even = lax.rem(lax.axis_index(axis), 2) == 0
    for ref, take_high in zip(refs, (even, jnp.logical_not(even))):
        ref[:, lanes] = jnp.where(take_high, high, low)


def write_faces(masked, lanes, first, second, x_refs, y_refs):
    store_faces(x_refs, "gx", lanes, masked[0], masked[first - 1])
    store_faces(y_refs, "gy", lanes, masked[:, 0, :], masked[:, second - 1, :])


def halos(refs, axis, lanes, shape):
    zero = jnp.zeros(shape, jnp.float32)
    if not refs:
        return zero, zero
    at = lax.axis_index(axis)
    odd = lax.rem(at, 2) == 1
    one, two = refs[0][:, lanes], refs[-1][:, lanes]
    low, high = jnp.where(odd, one, two), jnp.where(odd, two, one)
    return jnp.where(at == 0, zero, low), jnp.where(at == lax.axis_size(axis) - 1, zero, high)


def prepare_kernel(sizes, rhs_ref, wall_ref, x_refs, y_refs, open_ref):
    first, second, local_blocks, block = sizes
    wall = wall_ref[...].astype(jnp.float32)
    eye = (
        lax.broadcasted_iota(jnp.int32, (second, second), 0)
        == lax.broadcasted_iota(jnp.int32, (second, second), 1)
    ).astype(jnp.float32)
    for row in range(first):
        column = jnp.sum(eye * (1.0 - wall[row : row + 1, :]), axis=1, keepdims=True)
        open_ref[row * second : (row + 1) * second, :] = jnp.broadcast_to(column, (second, block))
    for b in range(local_blocks):
        lanes = slice(b * block, (b + 1) * block)
        masked = (rhs_ref[:, lanes] * open_ref[...]).reshape(first, second, block)
        write_faces(masked, lanes, first, second, x_refs, y_refs)


def scatter(sizes, per_owner, b, places, cols_ref, sources, blocks_ref):
    first, second, local_blocks, block = sizes
    mine = lax.axis_index("mode")
    picks, weights = [], []
    for place, source in zip(places, sources):
        owner = mine ^ place
        for p in range(per_owner):
            slot = owner * per_owner + p
            column = cols_ref[slot, b] - owner * local_blocks
            picks.append(source[:, pl.ds(pl.multiple_of(column * block, block), block)])
            weights.append(blocks_ref[b, slot])
    return lax.dot_general(
        jnp.concatenate(picks, axis=1),
        jnp.concatenate(weights, axis=1),
        (((1,), (1,)), ((), ())),
        preferred_element_type=jnp.float32,
    )


def split_speeds(speed_ref, sign_ref, lanes):
    parts = []
    for axis in range(2):
        speed, sign = speed_ref[axis : axis + 1, lanes], sign_ref[axis : axis + 1, lanes]
        parts += [jnp.where(sign == 1, speed, 0.0), jnp.where(sign == 1, 0.0, speed)]
    return parts


def near_kernel(sizes, per_owner, places, cols_ref, sources, blocks_ref, current_ref, params, open_ref, out_ref):
    first, second, local_blocks, block = sizes
    cells = first * second
    open_cells = open_ref[...]
    row_at = lax.broadcasted_iota(jnp.int32, (first, second, block), 1)
    zero = jnp.zeros((1, second, block), jnp.float32)
    for b in range(local_blocks):
        lanes = slice(b * block, (b + 1) * block)
        scattered = scatter(sizes, per_owner, b, places, cols_ref, sources, blocks_ref)
        current = current_ref[:, lanes]
        masked = (current * open_cells).reshape(first, second, block)
        relax_ref, speed_ref, sign_ref = params
        west, east, south, north = split_speeds(speed_ref, sign_ref, lanes)
        diagonal = relax_ref[lanes].reshape(1, block) + (west + east) + (south + north) - SHIFT
        from_west = jnp.concatenate([zero, masked[:-1]], axis=0)
        from_east = jnp.concatenate([masked[1:], zero], axis=0)
        from_south = jnp.where(row_at == 0, 0.0, pltpu.roll(masked, 1, axis=1))
        from_north = jnp.where(row_at == second - 1, 0.0, pltpu.roll(masked, second - 1, axis=1))
        drift = (
            west.reshape(1, 1, block) * from_west
            + east.reshape(1, 1, block) * from_east
            + south.reshape(1, 1, block) * from_south
            + north.reshape(1, 1, block) * from_north
        ).reshape(cells, block)
        out_ref[:, lanes] = diagonal * current - drift - scattered


def middle_kernel(sizes, per_owner, places, cols_ref, sources, blocks_ref, partial_ref, speed_ref, sign_ref, x_in, y_in, out_ref):
    first, second, local_blocks, block = sizes
    cells = first * second
    row_at = lax.broadcasted_iota(jnp.int32, (first, second, block), 1)
    for b in range(local_blocks):
        lanes = slice(b * block, (b + 1) * block)
        value = partial_ref[:, lanes]
        if places:
            value = value - scatter(sizes, per_owner, b, places, cols_ref, sources, blocks_ref)
        west, east, south, north = split_speeds(speed_ref, sign_ref, lanes)
        west_in, east_in = halos(x_in, "gx", lanes, (second, block))
        south_in, north_in = halos(y_in, "gy", lanes, (first, block))
        value = value.reshape(first, second, block)
        value = value - jnp.where(
            row_at == 0,
            (south * south_in)[:, None, :],
            jnp.where(row_at == second - 1, (north * north_in)[:, None, :], 0.0),
        )
        value = jnp.concatenate(
            [value[:1] - (west * west_in)[None], value[1:-1], value[-1:] - (east * east_in)[None]],
            axis=0,
        )
        out_ref[:, lanes] = value.reshape(cells, block)


def last_kernel(sizes, per_owner, places, cols_ref, sources, blocks_ref, partial_ref, earlier, open_ref, outs):
    first, second, local_blocks, block = sizes
    cells = first * second
    sums = {}
    for b in range(local_blocks):
        lanes = slice(b * block, (b + 1) * block)
        scattered = scatter(sizes, per_owner, b, places, cols_ref, sources, blocks_ref)
        result = partial_ref[:, lanes] - scattered
        if outs.gram is None:
            outs.value[:, lanes] = result
            outs.packed[:, lanes] = result.astype(jnp.bfloat16)
            write_faces(
                (result * open_ref[...]).reshape(first, second, block),
                lanes, first, second, outs.x, outs.y,
            )
        else:
            vectors = [ref[:, lanes] for ref in earlier] + [result]
            at = 0
            for i in range(len(vectors)):
                for j in range(i, len(vectors)):
                    term = jnp.sum((vectors[i] * vectors[j]).reshape(cells // 8, 8, block), axis=0)
                    sums[at] = term if b == 0 else sums[at] + term
                    at += 1
    if outs.gram is not None:
        devices = outs.gram.shape[0]
        lane = lax.broadcasted_iota(jnp.int32, (1, block), 1)
        row = jnp.zeros((1, block), jnp.float32)
        for at, value in sums.items():
            total = jnp.sum(jnp.sum(value, axis=0, keepdims=True), axis=1, keepdims=True)
            row = jnp.where(lane == at, total, row)
        outs.gram[...] = jnp.broadcast_to(row[None], (devices, 1, block))


class Outs:
    value = packed = gram = None
    x = y = ()


def least_squares(hessenberg, initial):
    upper = [list(row) for row in hessenberg]
    target = [initial] + [jnp.zeros_like(initial) for row_index in range(KRYLOV)]
    cosines = []
    sines = []
    for col_index in range(KRYLOV):
        for row_index in range(col_index):
            first = upper[row_index][col_index]
            second = upper[row_index + 1][col_index]
            upper[row_index][col_index] = cosines[row_index] * first + sines[row_index] * second
            upper[row_index + 1][col_index] = cosines[row_index] * second - sines[row_index] * first
        first = upper[col_index][col_index]
        second = upper[col_index + 1][col_index]
        radius = jnp.sqrt(first * first + second * second)
        cosine = first / radius
        sine_value = second / radius
        upper[col_index][col_index] = radius
        target[col_index + 1] = -sine_value * target[col_index]
        target[col_index] = cosine * target[col_index]
        cosines.append(cosine)
        sines.append(sine_value)
    combo = [None] * KRYLOV
    for row_index in reversed(range(KRYLOV)):
        running = target[row_index]
        for col_index in range(row_index + 1, KRYLOV):
            running = running - upper[row_index][col_index] * combo[col_index]
        combo[row_index] = running / upper[row_index][row_index]
    return combo


def arnoldi(gram):
    size = KRYLOV + 1

    def inner(left, right):
        total = None
        for i in range(size):
            for j in range(size):
                if left[i] is None or right[j] is None:
                    continue
                term = left[i] * right[j] * gram[min(i, j)][max(i, j)]
                total = term if total is None else total + term
        return total

    initial = jnp.sqrt(gram[0][0] + epsilon)
    basis = [[1.0 / initial] + [None] * KRYLOV]
    zero = jnp.zeros_like(initial)
    hessenberg = [[zero] * KRYLOV for row_index in range(size)]
    for section in range(KRYLOV):
        vector = basis[section]
        image = [None] * size
        for k in range(section + 2):
            parts = []
            if k > 0 and vector[k - 1] is not None:
                parts.append(vector[k - 1])
            if vector[k] is not None:
                parts.append(SHIFT * vector[k])
            image[k] = sum(parts[1:], parts[0])
        rest = list(image)
        for earlier in range(section + 1):
            coefficient = inner(basis[earlier], image)
            hessenberg[earlier][section] = coefficient
            for k in range(earlier + 1):
                rest[k] = rest[k] - coefficient * basis[earlier][k]
        length = jnp.sqrt(jnp.maximum(inner(rest, rest), 0.0) + epsilon)
        hessenberg[section + 1][section] = length
        basis.append([None if part is None else part / length for part in rest])
    combo = least_squares(hessenberg, initial)
    weights = []
    for k in range(KRYLOV):
        total = zero
        for j in range(k, KRYLOV):
            total = total + combo[j] * basis[j][k]
        weights.append(total)
    return hessenberg, weights


def finish_kernel(gram_ref, *refs):
    vectors, (solution_ref, hessenberg_ref) = refs[:KRYLOV], refs[KRYLOV:]
    block = gram_ref.shape[2]
    total = jnp.sum(gram_ref[...], axis=0)
    lane = lax.broadcasted_iota(jnp.int32, (1, block), 1)
    gram = [[None] * (KRYLOV + 1) for i in range(KRYLOV + 1)]
    at = 0
    for i in range(KRYLOV + 1):
        for j in range(i, KRYLOV + 1):
            entry = jnp.sum(jnp.where(lane == at, total, 0.0), axis=1, keepdims=True)
            gram[i][j] = jnp.broadcast_to(entry, (1, block))
            at += 1
    hessenberg, weights = arnoldi(gram)
    rows = lax.broadcasted_iota(jnp.int32, (KRYLOV + 1, KRYLOV), 0)
    cols = lax.broadcasted_iota(jnp.int32, (KRYLOV + 1, KRYLOV), 1)
    table = jnp.zeros((KRYLOV + 1, KRYLOV), jnp.float32)
    for i in range(KRYLOV + 1):
        for j in range(KRYLOV):
            table = jnp.where((rows == i) & (cols == j), hessenberg[i][j][:, :KRYLOV], table)
    hessenberg_ref[...] = table
    for b in range(solution_ref.shape[1] // block):
        lanes = slice(b * block, (b + 1) * block)
        solution_ref[:, lanes] = sum(
            weight * ref[:, lanes] for weight, ref in zip(weights, vectors)
        )


VMEM = pl.BlockSpec(memory_space=pltpu.VMEM)
ANY = pl.BlockSpec(memory_space=pl.ANY)
SCOPED = 16 * 1024 * 1024


def call(name, kernel, groups, shapes, scratch=(), flops=0):
    flat = [pair for group in groups for pair in group]

    def body(*refs):
        refs = list(refs)
        lists = []
        for group in groups:
            lists.append(refs[: len(group)])
            del refs[: len(group)]
        kernel(*lists, refs[: len(shapes)], refs[len(shapes) :])

    size = sum(operand.size * operand.dtype.itemsize for spec, operand in flat)
    size += sum(shape.size * shape.dtype.itemsize for shape in shapes)
    return pl.pallas_call(
        body,
        out_shape=list(shapes),
        in_specs=[spec for spec, operand in flat],
        out_specs=[VMEM] * len(shapes),
        scratch_shapes=list(scratch),
        compiler_params=pltpu.CompilerParams(vmem_limit_bytes=SCOPED),
        cost_estimate=pl.CostEstimate(flops=flops, bytes_accessed=size, transcendentals=0),
        name=name,
    )(*[operand for spec, operand in flat])


def in_vmem(operands):
    return [(VMEM, operand) for operand in operands]


def per_device(right_side, col_block, blocks, relax_rate, drift_speed, upwind_sign, wall_mask):
    first, second, local_modes = right_side.shape
    local_blocks, slots, block = blocks.shape[:3]
    cells = first * second
    count = lax.axis_size("mode")
    devices = count * lax.axis_size("gx") * lax.axis_size("gy")
    per_owner = slots // count
    sizes = (first, second, local_blocks, block)
    x_moves, y_moves = len(moves_of(lax.axis_size("gx"))), len(moves_of(lax.axis_size("gy")))
    n_faces = x_moves + y_moves
    f32 = jnp.float32
    shape_of = jax.ShapeDtypeStruct
    face_shapes = [shape_of((second, local_modes), f32)] * x_moves + [
        shape_of((first, local_modes), f32)
    ] * y_moves
    packed_shape = shape_of((cells, local_modes), jnp.bfloat16)
    vector_shape = shape_of((cells, local_modes), f32)
    near = [place for place in (0, 1) if place < count]
    final = [place for place in range(3, count) if place % 2 == 1]
    middle = [place for place in range(2, count) if place not in final]

    start = right_side.reshape(cells, local_modes)

    def pack(ins, outs, scratch):
        outs[0][...] = ins[0][...].astype(jnp.bfloat16)

    (packed,) = call("pack", pack, [in_vmem([start])], [packed_shape], flops=4 * 10**9)

    def prepare(ins, outs, scratch):
        faces, (open_ref,) = outs[:n_faces], outs[n_faces:]
        prepare_kernel(sizes, *ins, faces[:x_moves], faces[x_moves:], open_ref)

    *faces, open_cells = call(
        "prepare",
        prepare,
        [in_vmem([start, wall_mask])],
        face_shapes + [shape_of((cells, block), f32)],
        flops=8 * 10**9,
    )
    columns = col_block.T

    work = 2 * cells * local_modes * per_owner * block
    vectors = [start]
    for section in range(KRYLOV):
        sources = {0: packed}
        if count > 1:
            sources[1] = exchange(packed, 1)
        held = gather_far(packed)
        y_in, x_in = move_faces({"gx": faces[:x_moves], "gy": faces[x_moves:]})

        def near_step(cols, sources, rest, params, outs, scratch):
            blocks_ref, current_ref, open_ref = rest
            near_kernel(
                sizes, per_owner, near, cols[0], sources, blocks_ref, current_ref, params,
                open_ref, outs[0],
            )

        (partial,) = call(
            "near_%d" % section,
            near_step,
            [
                in_vmem([columns]),
                in_vmem([sources[place] for place in near]),
                in_vmem([blocks, vectors[-1], open_cells]),
                in_vmem([relax_rate, drift_speed, upwind_sign]),
            ],
            [vector_shape],
            flops=work * len(near),
        )

        held = dict(zip(held, hand_on(list(held.values()), [partial, *y_in, *x_in])))
        for place, array in held.items():
            sources[place] = array
            sources[place ^ 1] = exchange(array, 1)

        def middle_step(cols, sources, rest, y_in, x_in, outs, scratch):
            middle_kernel(
                sizes, per_owner, middle, cols[0], sources, *rest, x_in, y_in, outs[0]
            )

        (partial,) = call(
            "middle_%d" % section,
            middle_step,
            [
                in_vmem([columns]),
                in_vmem([sources[place] for place in middle]),
                in_vmem([blocks, partial, drift_speed, upwind_sign]),
                in_vmem(y_in),
                in_vmem(x_in),
            ],
            [vector_shape],
            flops=work * len(middle),
        )

        last = section == KRYLOV - 1
        def last_step(cols, sources, rest, earlier, outs, scratch, last=last):
            blocks_ref, partial_ref, open_ref = rest
            named = Outs()
            if last:
                named.gram = outs[0]
            else:
                named.x, named.y = outs[:x_moves], outs[x_moves:n_faces]
                named.packed, named.value = outs[n_faces:]
            last_kernel(
                sizes, per_owner, final, cols[0], sources, blocks_ref, partial_ref,
                earlier, open_ref, named,
            )

        if last:
            shapes = [shape_of((devices, 1, block), f32)]
        else:
            shapes = face_shapes + [packed_shape, vector_shape]
        results = call(
            "last_%d" % section,
            last_step,
            [
                in_vmem([columns]),
                in_vmem([sources[place] for place in final]),
                in_vmem([blocks, partial, open_cells]),
                in_vmem(vectors if last else []),
            ],
            shapes,
            flops=work * len(final),
        )
        if last:
            (gram,) = results
        else:
            *faces, packed, value = results
            vectors.append(value)

    gram = lax.all_to_all(gram, AXES, 0, 0)

    def finish(ins, outs, scratch):
        finish_kernel(*ins, *outs)

    solution, hessenberg = call(
        "finish",
        finish,
        [in_vmem([gram, *vectors])],
        [vector_shape, shape_of((KRYLOV + 1, KRYLOV), f32)],
    )
    return solution.reshape(first, second, local_modes), hessenberg


def solution(mesh):
    return jax.shard_map(
        per_device,
        mesh=mesh,
        in_specs=(
            P("gx", "gy", "mode"),
            P("mode", None),
            P("mode", None, None, None),
            P("mode"),
            P(None, "mode"),
            P(None, "mode"),
            P("gx", "gy"),
        ),
        out_specs=(P("gx", "gy", "mode"), P()),
        check_vma=False,
    )
```

```python
import functools

import jax
import jax.numpy as jnp
from jax import lax
from jax.experimental import pallas as pl
from jax.experimental.pallas import tpu as pltpu
from jax.sharding import PartitionSpec as P

KRYLOV = 3
SHIFT = 4.05
AXES = ("mode", "gx", "gy")

epsilon = 1e-12


def moves_of(count):
    moves = []
    for first in (0, 1)[: count - 1]:
        partner = list(range(count))
        for low in range(first, count - 1, 2):
            partner[low], partner[low + 1] = low + 1, low
        moves.append(partner)
    return moves


def move_faces(faces):
    received = []
    shards = lax.axis_size("mode")
    for axis in ("gy", "gx"):
        count = lax.axis_size(axis)
        arrived = []
        for face, partner in zip(faces[axis], moves_of(count)):
            pairs = []
            for shard in range(shards):
                for at in range(count):
                    alone = partner[at] == at
                    other = (shard ^ 1 if alone and shards > 1 else shard) * count + partner[at]
                    pairs.append((shard * count + at, other))
            arrived.append(lax.ppermute(face, ("mode", axis), pairs))
        received.append(arrived)
    return received


def exchange(array, bit):
    count = lax.axis_size("mode")
    return lax.ppermute(array, "mode", [(i, i ^ bit) for i in range(count)])


def gather_far(packed):
    held = {0: packed}
    bit = lax.axis_size("mode") // 2
    while bit > 1:
        for key in list(held):
            held[key ^ bit] = exchange(held[key], bit)
        bit //= 2
    del held[0]
    return held


def hand_on(arrays, after):
    count = len(arrays)
    if not count:
        return []
    return pl.pallas_call(
        lambda *refs: None,
        out_shape=[jax.ShapeDtypeStruct(array.shape, array.dtype) for array in arrays],
        in_specs=[ANY] * (count + len(after)),
        out_specs=[ANY] * count,
        input_output_aliases={at: at for at in range(count)},
        compiler_params=pltpu.CompilerParams(vmem_limit_bytes=SCOPED),
        name="hand_on",
    )(*arrays, *after)


def store_faces(refs, axis, lanes, low, high):
    even = lax.rem(lax.axis_index(axis), 2) == 0
    for ref, take_high in zip(refs, (even, jnp.logical_not(even))):
        ref[:, lanes] = jnp.where(take_high, high, low)


def write_faces(masked, lanes, first, second, x_refs, y_refs):
    store_faces(x_refs, "gx", lanes, masked[0], masked[first - 1])
    store_faces(y_refs, "gy", lanes, masked[:, 0, :], masked[:, second - 1, :])


def halos(refs, axis, lanes, shape):
    zero = jnp.zeros(shape, jnp.float32)
    if not refs:
        return zero, zero
    at = lax.axis_index(axis)
    odd = lax.rem(at, 2) == 1
    one, two = refs[0][:, lanes], refs[-1][:, lanes]
    low, high = jnp.where(odd, one, two), jnp.where(odd, two, one)
    return jnp.where(at == 0, zero, low), jnp.where(at == lax.axis_size(axis) - 1, zero, high)


def prepare_kernel(sizes, rhs_ref, wall_ref, x_refs, y_refs, open_ref):
    first, second, local_blocks, block = sizes
    wall = wall_ref[...].astype(jnp.float32)
    eye = (
        lax.broadcasted_iota(jnp.int32, (second, second), 0)
        == lax.broadcasted_iota(jnp.int32, (second, second), 1)
    ).astype(jnp.float32)
    for row in range(first):
        column = jnp.sum(eye * (1.0 - wall[row : row + 1, :]), axis=1, keepdims=True)
        open_ref[row * second : (row + 1) * second, :] = jnp.broadcast_to(column, (second, block))
    for b in range(local_blocks):
        lanes = slice(b * block, (b + 1) * block)
        masked = (rhs_ref[:, lanes] * open_ref[...]).reshape(first, second, block)
        write_faces(masked, lanes, first, second, x_refs, y_refs)


def scatter(sizes, per_owner, b, places, cols_ref, sources, blocks_ref):
    first, second, local_blocks, block = sizes
    mine = lax.axis_index("mode")
    picks, weights = [], []
    for place, source in zip(places, sources):
        owner = mine ^ place
        for p in range(per_owner):
            slot = owner * per_owner + p
            column = cols_ref[slot, b] - owner * local_blocks
            picks.append(source[:, pl.ds(pl.multiple_of(column * block, block), block)])
            weights.append(blocks_ref[b, slot])
    return lax.dot_general(
        jnp.concatenate(picks, axis=1),
        jnp.concatenate(weights, axis=1),
        (((1,), (1,)), ((), ())),
        preferred_element_type=jnp.float32,
    )


def split_speeds(speed_ref, sign_ref, lanes):
    parts = []
    for axis in range(2):
        speed, sign = speed_ref[axis : axis + 1, lanes], sign_ref[axis : axis + 1, lanes]
        parts += [jnp.where(sign == 1, speed, 0.0), jnp.where(sign == 1, 0.0, speed)]
    return parts


def near_kernel(sizes, per_owner, places, cols_ref, sources, blocks_ref, current_ref, params, open_ref, out_ref):
    first, second, local_blocks, block = sizes
    cells = first * second
    open_cells = open_ref[...]
    row_at = lax.broadcasted_iota(jnp.int32, (first, second, block), 1)
    zero = jnp.zeros((1, second, block), jnp.float32)
    for b in range(local_blocks):
        lanes = slice(b * block, (b + 1) * block)
        scattered = scatter(sizes, per_owner, b, places, cols_ref, sources, blocks_ref)
        current = current_ref[:, lanes]
        masked = (current * open_cells).reshape(first, second, block)
        relax_ref, speed_ref, sign_ref = params
        west, east, south, north = split_speeds(speed_ref, sign_ref, lanes)
        diagonal = relax_ref[lanes].reshape(1, block) + (west + east) + (south + north) - SHIFT
        from_west = jnp.concatenate([zero, masked[:-1]], axis=0)
        from_east = jnp.concatenate([masked[1:], zero], axis=0)
        from_south = jnp.where(row_at == 0, 0.0, pltpu.roll(masked, 1, axis=1))
        from_north = jnp.where(row_at == second - 1, 0.0, pltpu.roll(masked, second - 1, axis=1))
        drift = (
            west.reshape(1, 1, block) * from_west
            + east.reshape(1, 1, block) * from_east
            + south.reshape(1, 1, block) * from_south
            + north.reshape(1, 1, block) * from_north
        ).reshape(cells, block)
        out_ref[:, lanes] = diagonal * current - drift - scattered


def middle_kernel(sizes, per_owner, places, cols_ref, sources, blocks_ref, partial_ref, speed_ref, sign_ref, x_in, y_in, out_ref):
    first, second, local_blocks, block = sizes
    cells = first * second
    row_at = lax.broadcasted_iota(jnp.int32, (first, second, block), 1)
    for b in range(local_blocks):
        lanes = slice(b * block, (b + 1) * block)
        value = partial_ref[:, lanes]
        if places:
            value = value - scatter(sizes, per_owner, b, places, cols_ref, sources, blocks_ref)
        west, east, south, north = split_speeds(speed_ref, sign_ref, lanes)
        west_in, east_in = halos(x_in, "gx", lanes, (second, block))
        south_in, north_in = halos(y_in, "gy", lanes, (first, block))
        value = value.reshape(first, second, block)
        value = value - jnp.where(
            row_at == 0,
            (south * south_in)[:, None, :],
            jnp.where(row_at == second - 1, (north * north_in)[:, None, :], 0.0),
        )
        value = jnp.concatenate(
            [value[:1] - (west * west_in)[None], value[1:-1], value[-1:] - (east * east_in)[None]],
            axis=0,
        )
        out_ref[:, lanes] = value.reshape(cells, block)


def last_kernel(sizes, per_owner, places, cols_ref, sources, blocks_ref, partial_ref, earlier, open_ref, outs):
    first, second, local_blocks, block = sizes
    cells = first * second
    sums = {}
    for b in range(local_blocks):
        lanes = slice(b * block, (b + 1) * block)
        scattered = scatter(sizes, per_owner, b, places, cols_ref, sources, blocks_ref)
        result = partial_ref[:, lanes] - scattered
        if outs.gram is None:
            outs.value[:, lanes] = result
            outs.packed[:, lanes] = result.astype(jnp.bfloat16)
            write_faces(
                (result * open_ref[...]).reshape(first, second, block),
                lanes, first, second, outs.x, outs.y,
            )
        else:
            vectors = [ref[:, lanes] for ref in earlier] + [result]
            at = 0
            for i in range(len(vectors)):
                for j in range(i, len(vectors)):
                    term = jnp.sum((vectors[i] * vectors[j]).reshape(cells // 8, 8, block), axis=0)
                    sums[at] = term if b == 0 else sums[at] + term
                    at += 1
    if outs.gram is not None:
        devices = outs.gram.shape[0]
        lane = lax.broadcasted_iota(jnp.int32, (1, block), 1)
        row = jnp.zeros((1, block), jnp.float32)
        for at, value in sums.items():
            total = jnp.sum(jnp.sum(value, axis=0, keepdims=True), axis=1, keepdims=True)
            row = jnp.where(lane == at, total, row)
        outs.gram[...] = jnp.broadcast_to(row[None], (devices, 1, block))


class Outs:
    value = packed = gram = None
    x = y = ()


def least_squares(hessenberg, initial):
    upper = [list(row) for row in hessenberg]
    target = [initial] + [jnp.zeros_like(initial) for row_index in range(KRYLOV)]
    cosines = []
    sines = []
    for col_index in range(KRYLOV):
        for row_index in range(col_index):
            first = upper[row_index][col_index]
            second = upper[row_index + 1][col_index]
            upper[row_index][col_index] = cosines[row_index] * first + sines[row_index] * second
            upper[row_index + 1][col_index] = cosines[row_index] * second - sines[row_index] * first
        first = upper[col_index][col_index]
        second = upper[col_index + 1][col_index]
        radius = jnp.sqrt(first * first + second * second)
        cosine = first / radius
        sine_value = second / radius
        upper[col_index][col_index] = radius
        target[col_index + 1] = -sine_value * target[col_index]
        target[col_index] = cosine * target[col_index]
        cosines.append(cosine)
        sines.append(sine_value)
    combo = [None] * KRYLOV
    for row_index in reversed(range(KRYLOV)):
        running = target[row_index]
        for col_index in range(row_index + 1, KRYLOV):
            running = running - upper[row_index][col_index] * combo[col_index]
        combo[row_index] = running / upper[row_index][row_index]
    return combo


def arnoldi(gram):
    size = KRYLOV + 1

    def inner(left, right):
        total = None
        for i in range(size):
            for j in range(size):
                if left[i] is None or right[j] is None:
                    continue
                term = left[i] * right[j] * gram[min(i, j)][max(i, j)]
                total = term if total is None else total + term
        return total

    initial = jnp.sqrt(gram[0][0] + epsilon)
    basis = [[1.0 / initial] + [None] * KRYLOV]
    zero = jnp.zeros_like(initial)
    hessenberg = [[zero] * KRYLOV for row_index in range(size)]
    for section in range(KRYLOV):
        vector = basis[section]
        image = [None] * size
        for k in range(section + 2):
            parts = []
            if k > 0 and vector[k - 1] is not None:
                parts.append(vector[k - 1])
            if vector[k] is not None:
                parts.append(SHIFT * vector[k])
            image[k] = sum(parts[1:], parts[0])
        rest = list(image)
        for earlier in range(section + 1):
            coefficient = inner(basis[earlier], image)
            hessenberg[earlier][section] = coefficient
            for k in range(earlier + 1):
                rest[k] = rest[k] - coefficient * basis[earlier][k]
        length = jnp.sqrt(jnp.maximum(inner(rest, rest), 0.0) + epsilon)
        hessenberg[section + 1][section] = length
        basis.append([None if part is None else part / length for part in rest])
    combo = least_squares(hessenberg, initial)
    weights = []
    for k in range(KRYLOV):
        total = zero
        for j in range(k, KRYLOV):
            total = total + combo[j] * basis[j][k]
        weights.append(total)
    return hessenberg, weights


def finish_kernel(gram_ref, *refs):
    vectors, (solution_ref, hessenberg_ref, held_ref, sems) = refs[:KRYLOV], refs[KRYLOV:]
    block = gram_ref.shape[2]
    total = jnp.sum(gram_ref[...], axis=0)
    lane = lax.broadcasted_iota(jnp.int32, (1, block), 1)
    gram = [[None] * (KRYLOV + 1) for i in range(KRYLOV + 1)]
    at = 0
    for i in range(KRYLOV + 1):
        for j in range(i, KRYLOV + 1):
            entry = jnp.sum(jnp.where(lane == at, total, 0.0), axis=1, keepdims=True)
            gram[i][j] = jnp.broadcast_to(entry, (1, block))
            at += 1
    hessenberg, weights = arnoldi(gram)
    rows = lax.broadcasted_iota(jnp.int32, (KRYLOV + 1, KRYLOV), 0)
    cols = lax.broadcasted_iota(jnp.int32, (KRYLOV + 1, KRYLOV), 1)
    table = jnp.zeros((KRYLOV + 1, KRYLOV), jnp.float32)
    for i in range(KRYLOV + 1):
        for j in range(KRYLOV):
            table = jnp.where((rows == i) & (cols == j), hessenberg[i][j][:, :KRYLOV], table)
    hessenberg_ref[...] = table
    rows = held_ref.shape[0] // sems.shape[0]
    copies = []
    for part in range(sems.shape[0]):
        cells = slice(part * rows, (part + 1) * rows)
        for b in range(held_ref.shape[1] // block):
            lanes = slice(b * block, (b + 1) * block)
            held_ref[cells, lanes] = sum(
                weight * ref[cells, lanes] for weight, ref in zip(weights, vectors)
            )
        copies.append(
            pltpu.make_async_copy(held_ref.at[cells, :], solution_ref.at[cells, :], sems.at[part])
        )
        copies[-1].start()
    for copy in copies:
        copy.wait()


VMEM = pl.BlockSpec(memory_space=pltpu.VMEM)
ANY = pl.BlockSpec(memory_space=pl.ANY)
SCOPED = 16 * 1024 * 1024


def call(name, kernel, groups, shapes, scratch=(), flops=0, out_specs=None):
    flat = [pair for group in groups for pair in group]

    def body(*refs):
        refs = list(refs)
        lists = []
        for group in groups:
            lists.append(refs[: len(group)])
            del refs[: len(group)]
        kernel(*lists, refs[: len(shapes)], refs[len(shapes) :])

    size = sum(operand.size * operand.dtype.itemsize for spec, operand in flat)
    size += sum(shape.size * shape.dtype.itemsize for shape in shapes)
    return pl.pallas_call(
        body,
        out_shape=list(shapes),
        in_specs=[spec for spec, operand in flat],
        out_specs=out_specs or [VMEM] * len(shapes),
        scratch_shapes=list(scratch),
        compiler_params=pltpu.CompilerParams(vmem_limit_bytes=SCOPED),
        cost_estimate=pl.CostEstimate(flops=flops, bytes_accessed=size, transcendentals=0),
        name=name,
    )(*[operand for spec, operand in flat])


def in_vmem(operands):
    return [(VMEM, operand) for operand in operands]


def per_device(right_side, col_block, blocks, relax_rate, drift_speed, upwind_sign, wall_mask):
    first, second, local_modes = right_side.shape
    local_blocks, slots, block = blocks.shape[:3]
    cells = first * second
    count = lax.axis_size("mode")
    devices = count * lax.axis_size("gx") * lax.axis_size("gy")
    per_owner = slots // count
    sizes = (first, second, local_blocks, block)
    x_moves, y_moves = len(moves_of(lax.axis_size("gx"))), len(moves_of(lax.axis_size("gy")))
    n_faces = x_moves + y_moves
    f32 = jnp.float32
    shape_of = jax.ShapeDtypeStruct
    face_shapes = [shape_of((second, local_modes), f32)] * x_moves + [
        shape_of((first, local_modes), f32)
    ] * y_moves
    packed_shape = shape_of((cells, local_modes), jnp.bfloat16)
    vector_shape = shape_of((cells, local_modes), f32)
    near = [place for place in (0, 1) if place < count]
    final = [place for place in range(3, count) if place % 2 == 1]
    middle = [place for place in range(2, count) if place not in final]

    start = right_side.reshape(cells, local_modes)

    def pack(ins, outs, scratch):
        outs[0][...] = ins[0][...].astype(jnp.bfloat16)

    (packed,) = call("pack", pack, [in_vmem([start])], [packed_shape], flops=4 * 10**9)

    def prepare(ins, outs, scratch):
        faces, (open_ref,) = outs[:n_faces], outs[n_faces:]
        prepare_kernel(sizes, *ins, faces[:x_moves], faces[x_moves:], open_ref)

    *faces, open_cells = call(
        "prepare",
        prepare,
        [in_vmem([start, wall_mask])],
        face_shapes + [shape_of((cells, block), f32)],
        flops=8 * 10**9,
    )
    columns = col_block.T

    work = 2 * cells * local_modes * per_owner * block
    vectors = [start]
    for section in range(KRYLOV):
        sources = {0: packed}
        if count > 1:
            sources[1] = exchange(packed, 1)
        held = gather_far(packed)
        y_in, x_in = move_faces({"gx": faces[:x_moves], "gy": faces[x_moves:]})

        def near_step(cols, sources, rest, params, outs, scratch):
            blocks_ref, current_ref, open_ref = rest
            near_kernel(
                sizes, per_owner, near, cols[0], sources, blocks_ref, current_ref, params,
                open_ref, outs[0],
            )

        (partial,) = call(
            "near_%d" % section,
            near_step,
            [
                in_vmem([columns]),
                in_vmem([sources[place] for place in near]),
                in_vmem([blocks, vectors[-1], open_cells]),
                in_vmem([relax_rate, drift_speed, upwind_sign]),
            ],
            [vector_shape],
            flops=work * len(near),
        )

        held = dict(zip(held, hand_on(list(held.values()), [partial, *x_in, *y_in])))
        for place, array in held.items():
            sources[place] = array
            sources[place ^ 1] = exchange(array, 1)

        def middle_step(cols, sources, rest, x_in, y_in, outs, scratch):
            middle_kernel(
                sizes, per_owner, middle, cols[0], sources, *rest, x_in, y_in, outs[0]
            )

        (partial,) = call(
            "middle_%d" % section,
            middle_step,
            [
                in_vmem([columns]),
                in_vmem([sources[place] for place in middle]),
                in_vmem([blocks, partial, drift_speed, upwind_sign]),
                in_vmem(x_in),
                in_vmem(y_in),
            ],
            [vector_shape],
            flops=work * len(middle),
        )

        last = section == KRYLOV - 1
        def last_step(cols, sources, rest, earlier, outs, scratch, last=last):
            blocks_ref, partial_ref, open_ref = rest
            named = Outs()
            if last:
                named.gram = outs[0]
            else:
                named.x, named.y = outs[:x_moves], outs[x_moves:n_faces]
                named.packed, named.value = outs[n_faces:]
            last_kernel(
                sizes, per_owner, final, cols[0], sources, blocks_ref, partial_ref,
                earlier, open_ref, named,
            )

        if last:
            shapes = [shape_of((devices, 1, block), f32)]
        else:
            shapes = face_shapes + [packed_shape, vector_shape]
        results = call(
            "last_%d" % section,
            last_step,
            [
                in_vmem([columns]),
                in_vmem([sources[place] for place in final]),
                in_vmem([blocks, partial, open_cells]),
                in_vmem(vectors if last else []),
            ],
            shapes,
            flops=work * len(final),
        )
        if last:
            (gram,) = results
        else:
            *faces, packed, value = results
            vectors.append(value)

    gram = lax.all_to_all(gram, AXES, 0, 0)

    def finish(ins, outs, scratch):
        finish_kernel(*ins, *outs, *scratch)

    solution, hessenberg = call(
        "finish",
        finish,
        [in_vmem([gram, *vectors])],
        [vector_shape, shape_of((KRYLOV + 1, KRYLOV), f32)],
        [pltpu.VMEM((cells, local_modes), f32), pltpu.SemaphoreType.DMA((cells // 16,))],
        out_specs=[ANY, VMEM],
    )
    return solution.reshape(first, second, local_modes), hessenberg


def solution(mesh):
    return jax.shard_map(
        per_device,
        mesh=mesh,
        in_specs=(
            P("gx", "gy", "mode"),
            P("mode", None),
            P("mode", None, None, None),
            P("mode"),
            P(None, "mode"),
            P(None, "mode"),
            P("gx", "gy"),
        ),
        out_specs=(P("gx", "gy", "mode"), P()),
        check_vma=False,
    )
```

```python
import functools

import jax
import jax.numpy as jnp
from jax import lax
from jax.experimental import pallas as pl
from jax.experimental.pallas import tpu as pltpu
from jax.sharding import PartitionSpec as P

KRYLOV = 3
SHIFT = 4.05
AXES = ("mode", "gx", "gy")

epsilon = 1e-12


def moves_of(count):
    moves = []
    for first in (0, 1)[: count - 1]:
        partner = list(range(count))
        for low in range(first, count - 1, 2):
            partner[low], partner[low + 1] = low + 1, low
        moves.append(partner)
    return moves


def move_faces(faces):
    received = []
    shards = lax.axis_size("mode")
    for axis in ("gy", "gx"):
        count = lax.axis_size(axis)
        arrived = []
        for face, partner in zip(faces[axis], moves_of(count)):
            pairs = []
            for shard in range(shards):
                for at in range(count):
                    alone = partner[at] == at
                    other = (shard ^ 1 if alone and shards > 1 else shard) * count + partner[at]
                    pairs.append((shard * count + at, other))
            arrived.append(lax.ppermute(face, ("mode", axis), pairs))
        received.append(arrived)
    return received


def exchange(array, bit):
    count = lax.axis_size("mode")
    return lax.ppermute(array, "mode", [(i, i ^ bit) for i in range(count)])


def gather_far(packed):
    held = {0: packed}
    bit = lax.axis_size("mode") // 2
    while bit > 1:
        for key in list(held):
            held[key ^ bit] = exchange(held[key], bit)
        bit //= 2
    del held[0]
    return held


def store_packed(refs, lanes, value):
    refs[0][:, lanes] = value.astype(jnp.bfloat16)
    at = 0
    for ref in refs[1:]:
        rows = ref.shape[0]
        ref[:, lanes] = value[at : at + rows].astype(jnp.bfloat16)
        at += rows


def hand_on(arrays, after):
    count = len(arrays)
    if not count:
        return []
    return pl.pallas_call(
        lambda *refs: None,
        out_shape=[jax.ShapeDtypeStruct(array.shape, array.dtype) for array in arrays],
        in_specs=[ANY] * (count + len(after)),
        out_specs=[ANY] * count,
        input_output_aliases={at: at for at in range(count)},
        compiler_params=pltpu.CompilerParams(vmem_limit_bytes=SCOPED),
        name="hand_on",
    )(*arrays, *after)


def store_faces(refs, axis, lanes, low, high):
    even = lax.rem(lax.axis_index(axis), 2) == 0
    for ref, take_high in zip(refs, (even, jnp.logical_not(even))):
        ref[:, lanes] = jnp.where(take_high, high, low)


def write_faces(masked, lanes, first, second, x_refs, y_refs):
    store_faces(x_refs, "gx", lanes, masked[0], masked[first - 1])
    store_faces(y_refs, "gy", lanes, masked[:, 0, :], masked[:, second - 1, :])


def halos(refs, axis, lanes, shape):
    zero = jnp.zeros(shape, jnp.float32)
    if not refs:
        return zero, zero
    at = lax.axis_index(axis)
    odd = lax.rem(at, 2) == 1
    one, two = refs[0][:, lanes], refs[-1][:, lanes]
    low, high = jnp.where(odd, one, two), jnp.where(odd, two, one)
    return jnp.where(at == 0, zero, low), jnp.where(at == lax.axis_size(axis) - 1, zero, high)


def prepare_kernel(sizes, rhs_ref, wall_ref, x_refs, y_refs, open_ref):
    first, second, local_blocks, block = sizes
    wall = wall_ref[...].astype(jnp.float32)
    eye = (
        lax.broadcasted_iota(jnp.int32, (second, second), 0)
        == lax.broadcasted_iota(jnp.int32, (second, second), 1)
    ).astype(jnp.float32)
    for row in range(first):
        column = jnp.sum(eye * (1.0 - wall[row : row + 1, :]), axis=1, keepdims=True)
        open_ref[row * second : (row + 1) * second, :] = jnp.broadcast_to(column, (second, block))
    for b in range(local_blocks):
        lanes = slice(b * block, (b + 1) * block)
        masked = (rhs_ref[:, lanes] * open_ref[...]).reshape(first, second, block)
        write_faces(masked, lanes, first, second, x_refs, y_refs)


def scatter(sizes, per_owner, b, places, cols_ref, sources, blocks_ref):
    first, second, local_blocks, block = sizes
    mine = lax.axis_index("mode")
    picks, weights = [], []
    for place, source in zip(places, sources):
        owner = mine ^ place
        for p in range(per_owner):
            slot = owner * per_owner + p
            column = cols_ref[slot, b] - owner * local_blocks
            lanes = pl.ds(pl.multiple_of(column * block, block), block)
            picks.append(jnp.concatenate([part[:, lanes] for part in source], axis=0))
            weights.append(blocks_ref[b, slot])
    return lax.dot_general(
        jnp.concatenate(picks, axis=1),
        jnp.concatenate(weights, axis=1),
        (((1,), (1,)), ((), ())),
        preferred_element_type=jnp.float32,
    )


def split_speeds(speed_ref, sign_ref, lanes):
    parts = []
    for axis in range(2):
        speed, sign = speed_ref[axis : axis + 1, lanes], sign_ref[axis : axis + 1, lanes]
        parts += [jnp.where(sign == 1, speed, 0.0), jnp.where(sign == 1, 0.0, speed)]
    return parts


def near_kernel(sizes, per_owner, places, cols_ref, sources, blocks_ref, current_ref, params, open_ref, out_ref):
    first, second, local_blocks, block = sizes
    cells = first * second
    open_cells = open_ref[...]
    row_at = lax.broadcasted_iota(jnp.int32, (first, second, block), 1)
    zero = jnp.zeros((1, second, block), jnp.float32)
    for b in range(local_blocks):
        lanes = slice(b * block, (b + 1) * block)
        scattered = scatter(sizes, per_owner, b, places, cols_ref, sources, blocks_ref)
        current = current_ref[:, lanes]
        masked = (current * open_cells).reshape(first, second, block)
        relax_ref, speed_ref, sign_ref = params
        west, east, south, north = split_speeds(speed_ref, sign_ref, lanes)
        diagonal = relax_ref[lanes].reshape(1, block) + (west + east) + (south + north) - SHIFT
        from_west = jnp.concatenate([zero, masked[:-1]], axis=0)
        from_east = jnp.concatenate([masked[1:], zero], axis=0)
        from_south = jnp.where(row_at == 0, 0.0, pltpu.roll(masked, 1, axis=1))
        from_north = jnp.where(row_at == second - 1, 0.0, pltpu.roll(masked, second - 1, axis=1))
        drift = (
            west.reshape(1, 1, block) * from_west
            + east.reshape(1, 1, block) * from_east
            + south.reshape(1, 1, block) * from_south
            + north.reshape(1, 1, block) * from_north
        ).reshape(cells, block)
        out_ref[:, lanes] = diagonal * current - drift - scattered


def middle_kernel(sizes, per_owner, places, cols_ref, sources, blocks_ref, partial_ref, speed_ref, sign_ref, x_in, y_in, out_ref):
    first, second, local_blocks, block = sizes
    cells = first * second
    row_at = lax.broadcasted_iota(jnp.int32, (first, second, block), 1)
    for b in range(local_blocks):
        lanes = slice(b * block, (b + 1) * block)
        value = partial_ref[:, lanes]
        if places:
            value = value - scatter(sizes, per_owner, b, places, cols_ref, sources, blocks_ref)
        west, east, south, north = split_speeds(speed_ref, sign_ref, lanes)
        west_in, east_in = halos(x_in, "gx", lanes, (second, block))
        south_in, north_in = halos(y_in, "gy", lanes, (first, block))
        value = value.reshape(first, second, block)
        value = value - jnp.where(
            row_at == 0,
            (south * south_in)[:, None, :],
            jnp.where(row_at == second - 1, (north * north_in)[:, None, :], 0.0),
        )
        value = jnp.concatenate(
            [value[:1] - (west * west_in)[None], value[1:-1], value[-1:] - (east * east_in)[None]],
            axis=0,
        )
        out_ref[:, lanes] = value.reshape(cells, block)


def last_kernel(sizes, per_owner, places, cols_ref, sources, blocks_ref, partial_ref, earlier, open_ref, outs):
    first, second, local_blocks, block = sizes
    cells = first * second
    sums = {}
    for b in range(local_blocks):
        lanes = slice(b * block, (b + 1) * block)
        scattered = scatter(sizes, per_owner, b, places, cols_ref, sources, blocks_ref)
        result = partial_ref[:, lanes] - scattered
        if outs.gram is None:
            outs.value[:, lanes] = result
            store_packed(outs.packed, lanes, result)
            write_faces(
                (result * open_ref[...]).reshape(first, second, block),
                lanes, first, second, outs.x, outs.y,
            )
        else:
            vectors = [ref[:, lanes] for ref in earlier] + [result]
            at = 0
            for i in range(len(vectors)):
                for j in range(i, len(vectors)):
                    term = jnp.sum((vectors[i] * vectors[j]).reshape(cells // 8, 8, block), axis=0)
                    sums[at] = term if b == 0 else sums[at] + term
                    at += 1
    if outs.gram is not None:
        devices = outs.gram.shape[0]
        lane = lax.broadcasted_iota(jnp.int32, (1, block), 1)
        row = jnp.zeros((1, block), jnp.float32)
        for at, value in sums.items():
            total = jnp.sum(jnp.sum(value, axis=0, keepdims=True), axis=1, keepdims=True)
            row = jnp.where(lane == at, total, row)
        outs.gram[...] = jnp.broadcast_to(row[None], (devices, 1, block))


class Outs:
    value = gram = None
    x = y = packed = ()


def least_squares(hessenberg, initial):
    upper = [list(row) for row in hessenberg]
    target = [initial] + [jnp.zeros_like(initial) for row_index in range(KRYLOV)]
    cosines = []
    sines = []
    for col_index in range(KRYLOV):
        for row_index in range(col_index):
            first = upper[row_index][col_index]
            second = upper[row_index + 1][col_index]
            upper[row_index][col_index] = cosines[row_index] * first + sines[row_index] * second
            upper[row_index + 1][col_index] = cosines[row_index] * second - sines[row_index] * first
        first = upper[col_index][col_index]
        second = upper[col_index + 1][col_index]
        radius = jnp.sqrt(first * first + second * second)
        cosine = first / radius
        sine_value = second / radius
        upper[col_index][col_index] = radius
        target[col_index + 1] = -sine_value * target[col_index]
        target[col_index] = cosine * target[col_index]
        cosines.append(cosine)
        sines.append(sine_value)
    combo = [None] * KRYLOV
    for row_index in reversed(range(KRYLOV)):
        running = target[row_index]
        for col_index in range(row_index + 1, KRYLOV):
            running = running - upper[row_index][col_index] * combo[col_index]
        combo[row_index] = running / upper[row_index][row_index]
    return combo


def arnoldi(gram):
    size = KRYLOV + 1

    def inner(left, right):
        total = None
        for i in range(size):
            for j in range(size):
                if left[i] is None or right[j] is None:
                    continue
                term = left[i] * right[j] * gram[min(i, j)][max(i, j)]
                total = term if total is None else total + term
        return total

    initial = jnp.sqrt(gram[0][0] + epsilon)
    basis = [[1.0 / initial] + [None] * KRYLOV]
    zero = jnp.zeros_like(initial)
    hessenberg = [[zero] * KRYLOV for row_index in range(size)]
    for section in range(KRYLOV):
        vector = basis[section]
        image = [None] * size
        for k in range(section + 2):
            parts = []
            if k > 0 and vector[k - 1] is not None:
                parts.append(vector[k - 1])
            if vector[k] is not None:
                parts.append(SHIFT * vector[k])
            image[k] = sum(parts[1:], parts[0])
        rest = list(image)
        for earlier in range(section + 1):
            coefficient = inner(basis[earlier], image)
            hessenberg[earlier][section] = coefficient
            for k in range(earlier + 1):
                rest[k] = rest[k] - coefficient * basis[earlier][k]
        length = jnp.sqrt(jnp.maximum(inner(rest, rest), 0.0) + epsilon)
        hessenberg[section + 1][section] = length
        basis.append([None if part is None else part / length for part in rest])
    combo = least_squares(hessenberg, initial)
    weights = []
    for k in range(KRYLOV):
        total = zero
        for j in range(k, KRYLOV):
            total = total + combo[j] * basis[j][k]
        weights.append(total)
    return hessenberg, weights


def finish_kernel(gram_ref, *refs):
    vectors, (solution_ref, hessenberg_ref) = refs[:KRYLOV], refs[KRYLOV:]
    block = gram_ref.shape[2]
    total = jnp.sum(gram_ref[...], axis=0)
    lane = lax.broadcasted_iota(jnp.int32, (1, block), 1)
    gram = [[None] * (KRYLOV + 1) for i in range(KRYLOV + 1)]
    at = 0
    for i in range(KRYLOV + 1):
        for j in range(i, KRYLOV + 1):
            entry = jnp.sum(jnp.where(lane == at, total, 0.0), axis=1, keepdims=True)
            gram[i][j] = jnp.broadcast_to(entry, (1, block))
            at += 1
    hessenberg, weights = arnoldi(gram)
    rows = lax.broadcasted_iota(jnp.int32, (KRYLOV + 1, KRYLOV), 0)
    cols = lax.broadcasted_iota(jnp.int32, (KRYLOV + 1, KRYLOV), 1)
    table = jnp.zeros((KRYLOV + 1, KRYLOV), jnp.float32)
    for i in range(KRYLOV + 1):
        for j in range(KRYLOV):
            table = jnp.where((rows == i) & (cols == j), hessenberg[i][j][:, :KRYLOV], table)
    hessenberg_ref[...] = table
    for b in range(solution_ref.shape[1] // block):
        lanes = slice(b * block, (b + 1) * block)
        solution_ref[:, lanes] = sum(
            weight * ref[:, lanes] for weight, ref in zip(weights, vectors)
        )


VMEM = pl.BlockSpec(memory_space=pltpu.VMEM)
ANY = pl.BlockSpec(memory_space=pl.ANY)
SCOPED = 16 * 1024 * 1024


def call(name, kernel, groups, shapes, scratch=(), flops=0):
    flat = [pair for group in groups for pair in group]

    def body(*refs):
        refs = list(refs)
        lists = []
        for group in groups:
            lists.append(refs[: len(group)])
            del refs[: len(group)]
        kernel(*lists, refs[: len(shapes)], refs[len(shapes) :])

    size = sum(operand.size * operand.dtype.itemsize for spec, operand in flat)
    size += sum(shape.size * shape.dtype.itemsize for shape in shapes)
    return pl.pallas_call(
        body,
        out_shape=list(shapes),
        in_specs=[spec for spec, operand in flat],
        out_specs=[VMEM] * len(shapes),
        scratch_shapes=list(scratch),
        compiler_params=pltpu.CompilerParams(vmem_limit_bytes=SCOPED),
        cost_estimate=pl.CostEstimate(flops=flops, bytes_accessed=size, transcendentals=0),
        name=name,
    )(*[operand for spec, operand in flat])


def in_vmem(operands):
    return [(VMEM, operand) for operand in operands]


def per_device(right_side, col_block, blocks, relax_rate, drift_speed, upwind_sign, wall_mask):
    first, second, local_modes = right_side.shape
    local_blocks, slots, block = blocks.shape[:3]
    cells = first * second
    count = lax.axis_size("mode")
    devices = count * lax.axis_size("gx") * lax.axis_size("gy")
    per_owner = slots // count
    sizes = (first, second, local_blocks, block)
    x_moves, y_moves = len(moves_of(lax.axis_size("gx"))), len(moves_of(lax.axis_size("gy")))
    n_faces = x_moves + y_moves
    f32 = jnp.float32
    shape_of = jax.ShapeDtypeStruct
    face_shapes = [shape_of((second, local_modes), f32)] * x_moves + [
        shape_of((first, local_modes), f32)
    ] * y_moves
    parts = 2 if cells % 32 == 0 else 1
    packed_shapes = [shape_of((cells, local_modes), jnp.bfloat16)]
    packed_shapes += [shape_of((cells // parts, local_modes), jnp.bfloat16)] * parts
    vector_shape = shape_of((cells, local_modes), f32)
    near = [place for place in (0, 1) if place < count]
    final = [place for place in range(3, count) if place % 2 == 1]
    middle = [place for place in range(2, count) if place not in final]

    start = right_side.reshape(cells, local_modes)

    def pack(ins, outs, scratch):
        store_packed(outs, slice(None), ins[0][...])

    packed = call("pack", pack, [in_vmem([start])], packed_shapes, flops=4 * 10**9)

    def prepare(ins, outs, scratch):
        faces, (open_ref,) = outs[:n_faces], outs[n_faces:]
        prepare_kernel(sizes, *ins, faces[:x_moves], faces[x_moves:], open_ref)

    *faces, open_cells = call(
        "prepare",
        prepare,
        [in_vmem([start, wall_mask])],
        face_shapes + [shape_of((cells, block), f32)],
        flops=8 * 10**9,
    )
    columns = col_block.T

    work = 2 * cells * local_modes * per_owner * block
    vectors = [start]
    for section in range(KRYLOV):
        sources = {0: packed[0]}
        held = gather_far(packed[0])
        neighbour = [exchange(part, 1) for part in packed[1:]] if count > 1 else []
        y_in, x_in = move_faces({"gx": faces[:x_moves], "gy": faces[x_moves:]})

        def near_step(cols, sources, rest, params, outs, scratch):
            sources = [sources[:1], sources[1:]]
            blocks_ref, current_ref, open_ref = rest
            near_kernel(
                sizes, per_owner, near, cols[0], sources, blocks_ref, current_ref, params,
                open_ref, outs[0],
            )

        (partial,) = call(
            "near_%d" % section,
            near_step,
            [
                in_vmem([columns]),
                in_vmem([packed[0], *neighbour]),
                in_vmem([blocks, vectors[-1], open_cells]),
                in_vmem([relax_rate, drift_speed, upwind_sign]),
            ],
            [vector_shape],
            flops=work * len(near),
        )

        held = dict(zip(held, hand_on(list(held.values()), [partial, *x_in, *y_in])))
        for place, array in held.items():
            sources[place] = array
            sources[place ^ 1] = exchange(array, 1)

        def middle_step(cols, sources, rest, x_in, y_in, outs, scratch):
            middle_kernel(
                sizes, per_owner, middle, cols[0], [[ref] for ref in sources], *rest, x_in, y_in, outs[0]
            )

        (partial,) = call(
            "middle_%d" % section,
            middle_step,
            [
                in_vmem([columns]),
                in_vmem([sources[place] for place in middle]),
                in_vmem([blocks, partial, drift_speed, upwind_sign]),
                in_vmem(x_in),
                in_vmem(y_in),
            ],
            [vector_shape],
            flops=work * len(middle),
        )

        last = section == KRYLOV - 1
        def last_step(cols, sources, rest, earlier, outs, scratch, last=last):
            blocks_ref, partial_ref, open_ref = rest
            named = Outs()
            if last:
                named.gram = outs[0]
            else:
                named.x, named.y = outs[:x_moves], outs[x_moves:n_faces]
                *named.packed, named.value = outs[n_faces:]
            last_kernel(
                sizes, per_owner, final, cols[0], [[ref] for ref in sources], blocks_ref, partial_ref,
                earlier, open_ref, named,
            )

        if last:
            shapes = [shape_of((devices, 1, block), f32)]
        else:
            shapes = face_shapes + packed_shapes + [vector_shape]
        results = call(
            "last_%d" % section,
            last_step,
            [
                in_vmem([columns]),
                in_vmem([sources[place] for place in final]),
                in_vmem([blocks, partial, open_cells]),
                in_vmem(vectors if last else []),
            ],
            shapes,
            flops=work * len(final),
        )
        if last:
            (gram,) = results
        else:
            faces, packed, value = results[:n_faces], results[n_faces:-1], results[-1]
            vectors.append(value)

    gram = lax.all_to_all(gram, AXES, 0, 0)

    def finish(ins, outs, scratch):
        finish_kernel(*ins, *outs)

    solution, hessenberg = call(
        "finish",
        finish,
        [in_vmem([gram, *vectors])],
        [vector_shape, shape_of((KRYLOV + 1, KRYLOV), f32)],
    )
    return solution.reshape(first, second, local_modes), hessenberg


def solution(mesh):
    return jax.shard_map(
        per_device,
        mesh=mesh,
        in_specs=(
            P("gx", "gy", "mode"),
            P("mode", None),
            P("mode", None, None, None),
            P("mode"),
            P(None, "mode"),
            P(None, "mode"),
            P("gx", "gy"),
        ),
        out_specs=(P("gx", "gy", "mode"), P()),
        check_vma=False,
    )
```

```python
import functools

import jax
import jax.numpy as jnp
from jax import lax
from jax.experimental import pallas as pl
from jax.experimental.pallas import tpu as pltpu
from jax.sharding import PartitionSpec as P

KRYLOV = 3
SHIFT = 4.05
AXES = ("mode", "gx", "gy")

epsilon = 1e-12


def moves_of(count):
    moves = []
    for first in (0, 1)[: count - 1]:
        partner = list(range(count))
        for low in range(first, count - 1, 2):
            partner[low], partner[low + 1] = low + 1, low
        moves.append(partner)
    return moves


def move_faces(faces):
    received = []
    shards = lax.axis_size("mode")
    for axis in ("gy", "gx"):
        count = lax.axis_size(axis)
        arrived = []
        for face, partner in zip(faces[axis], moves_of(count)):
            pairs = []
            for shard in range(shards):
                for at in range(count):
                    alone = partner[at] == at
                    other = (shard ^ 1 if alone and shards > 1 else shard) * count + partner[at]
                    pairs.append((shard * count + at, other))
            arrived.append(lax.ppermute(face, ("mode", axis), pairs))
        received.append(arrived)
    return received


def exchange(array, bit):
    count = lax.axis_size("mode")
    return lax.ppermute(array, "mode", [(i, i ^ bit) for i in range(count)])


def gather_far(packed):
    held = {0: packed}
    bit = lax.axis_size("mode") // 2
    while bit > 1:
        for key in list(held):
            held[key ^ bit] = exchange(held[key], bit)
        bit //= 2
    del held[0]
    return held


def store_packed(refs, lanes, value):
    refs[0][:, lanes] = value.astype(jnp.bfloat16)
    at = 0
    for ref in refs[1:]:
        rows = ref.shape[0]
        ref[:, lanes] = value[at : at + rows].astype(jnp.bfloat16)
        at += rows


def hand_on(arrays, after):
    count = len(arrays)
    if not count:
        return []
    return pl.pallas_call(
        lambda *refs: None,
        out_shape=[jax.ShapeDtypeStruct(array.shape, array.dtype) for array in arrays],
        in_specs=[ANY] * (count + len(after)),
        out_specs=[ANY] * count,
        input_output_aliases={at: at for at in range(count)},
        compiler_params=pltpu.CompilerParams(vmem_limit_bytes=SCOPED),
        name="hand_on",
    )(*arrays, *after)


def store_faces(refs, axis, lanes, low, high):
    even = lax.rem(lax.axis_index(axis), 2) == 0
    for ref, take_high in zip(refs, (even, jnp.logical_not(even))):
        ref[:, lanes] = jnp.where(take_high, high, low)


def write_faces(masked, lanes, first, second, x_refs, y_refs):
    store_faces(x_refs, "gx", lanes, masked[0], masked[first - 1])
    store_faces(y_refs, "gy", lanes, masked[:, 0, :], masked[:, second - 1, :])


def halos(refs, axis, lanes, shape):
    zero = jnp.zeros(shape, jnp.float32)
    if not refs:
        return zero, zero
    at = lax.axis_index(axis)
    odd = lax.rem(at, 2) == 1
    one, two = refs[0][:, lanes], refs[-1][:, lanes]
    low, high = jnp.where(odd, one, two), jnp.where(odd, two, one)
    return jnp.where(at == 0, zero, low), jnp.where(at == lax.axis_size(axis) - 1, zero, high)


def prepare_kernel(sizes, rhs_ref, wall_ref, x_refs, y_refs, open_ref):
    first, second, local_blocks, block = sizes
    wall = wall_ref[...].astype(jnp.float32)
    eye = (
        lax.broadcasted_iota(jnp.int32, (second, second), 0)
        == lax.broadcasted_iota(jnp.int32, (second, second), 1)
    ).astype(jnp.float32)
    for row in range(first):
        column = jnp.sum(eye * (1.0 - wall[row : row + 1, :]), axis=1, keepdims=True)
        open_ref[row * second : (row + 1) * second, :] = jnp.broadcast_to(column, (second, block))
    for b in range(local_blocks):
        lanes = slice(b * block, (b + 1) * block)
        masked = (rhs_ref[:, lanes] * open_ref[...]).reshape(first, second, block)
        write_faces(masked, lanes, first, second, x_refs, y_refs)


def scatter(sizes, per_owner, b, places, cols_ref, sources, blocks_ref):
    first, second, local_blocks, block = sizes
    mine = lax.axis_index("mode")
    picks, weights = [], []
    for place, source in zip(places, sources):
        owner = mine ^ place
        for p in range(per_owner):
            slot = owner * per_owner + p
            column = cols_ref[slot, b] - owner * local_blocks
            lanes = pl.ds(pl.multiple_of(column * block, block), block)
            picks.append(jnp.concatenate([part[:, lanes] for part in source], axis=0))
            weights.append(blocks_ref[b, slot])
    return lax.dot_general(
        jnp.concatenate(picks, axis=1),
        jnp.concatenate(weights, axis=1),
        (((1,), (1,)), ((), ())),
        preferred_element_type=jnp.float32,
    )


def split_speeds(speed_ref, sign_ref, lanes):
    parts = []
    for axis in range(2):
        speed, sign = speed_ref[axis : axis + 1, lanes], sign_ref[axis : axis + 1, lanes]
        parts += [jnp.where(sign == 1, speed, 0.0), jnp.where(sign == 1, 0.0, speed)]
    return parts


def near_kernel(sizes, per_owner, places, cols_ref, sources, blocks_ref, current_ref, params, open_ref, out_ref):
    first, second, local_blocks, block = sizes
    cells = first * second
    open_cells = open_ref[...]
    row_at = lax.broadcasted_iota(jnp.int32, (first, second, block), 1)
    zero = jnp.zeros((1, second, block), jnp.float32)
    for b in range(local_blocks):
        lanes = slice(b * block, (b + 1) * block)
        scattered = scatter(sizes, per_owner, b, places, cols_ref, sources, blocks_ref)
        current = current_ref[:, lanes]
        masked = (current * open_cells).reshape(first, second, block)
        relax_ref, speed_ref, sign_ref = params
        west, east, south, north = split_speeds(speed_ref, sign_ref, lanes)
        diagonal = relax_ref[lanes].reshape(1, block) + (west + east) + (south + north) - SHIFT
        from_west = jnp.concatenate([zero, masked[:-1]], axis=0)
        from_east = jnp.concatenate([masked[1:], zero], axis=0)
        from_south = jnp.where(row_at == 0, 0.0, pltpu.roll(masked, 1, axis=1))
        from_north = jnp.where(row_at == second - 1, 0.0, pltpu.roll(masked, second - 1, axis=1))
        drift = (
            west.reshape(1, 1, block) * from_west
            + east.reshape(1, 1, block) * from_east
            + south.reshape(1, 1, block) * from_south
            + north.reshape(1, 1, block) * from_north
        ).reshape(cells, block)
        out_ref[:, lanes] = diagonal * current - drift - scattered


def middle_kernel(sizes, per_owner, places, cols_ref, sources, blocks_ref, partial_ref, speed_ref, sign_ref, x_in, y_in, out_ref):
    first, second, local_blocks, block = sizes
    cells = first * second
    row_at = lax.broadcasted_iota(jnp.int32, (first, second, block), 1)
    for b in range(local_blocks):
        lanes = slice(b * block, (b + 1) * block)
        value = partial_ref[:, lanes]
        if places:
            value = value - scatter(sizes, per_owner, b, places, cols_ref, sources, blocks_ref)
        west, east, south, north = split_speeds(speed_ref, sign_ref, lanes)
        west_in, east_in = halos(x_in, "gx", lanes, (second, block))
        south_in, north_in = halos(y_in, "gy", lanes, (first, block))
        value = value.reshape(first, second, block)
        value = value - jnp.where(
            row_at == 0,
            (south * south_in)[:, None, :],
            jnp.where(row_at == second - 1, (north * north_in)[:, None, :], 0.0),
        )
        value = jnp.concatenate(
            [value[:1] - (west * west_in)[None], value[1:-1], value[-1:] - (east * east_in)[None]],
            axis=0,
        )
        out_ref[:, lanes] = value.reshape(cells, block)


def last_kernel(sizes, per_owner, places, cols_ref, sources, blocks_ref, partial_ref, earlier, open_ref, outs):
    first, second, local_blocks, block = sizes
    cells = first * second
    sums = {}
    for b in range(local_blocks):
        lanes = slice(b * block, (b + 1) * block)
        scattered = scatter(sizes, per_owner, b, places, cols_ref, sources, blocks_ref)
        result = partial_ref[:, lanes] - scattered
        if outs.gram is None:
            outs.value[:, lanes] = result
            store_packed(outs.packed, lanes, result)
            write_faces(
                (result * open_ref[...]).reshape(first, second, block),
                lanes, first, second, outs.x, outs.y,
            )
        else:
            vectors = [ref[:, lanes] for ref in earlier] + [result]
            at = 0
            for i in range(len(vectors)):
                for j in range(i, len(vectors)):
                    term = jnp.sum((vectors[i] * vectors[j]).reshape(cells // 8, 8, block), axis=0)
                    sums[at] = term if b == 0 else sums[at] + term
                    at += 1
    if outs.gram is not None:
        devices = outs.gram.shape[0]
        lane = lax.broadcasted_iota(jnp.int32, (1, block), 1)
        row = jnp.zeros((1, block), jnp.float32)
        for at, value in sums.items():
            total = jnp.sum(jnp.sum(value, axis=0, keepdims=True), axis=1, keepdims=True)
            row = jnp.where(lane == at, total, row)
        outs.gram[...] = jnp.broadcast_to(row[None], (devices, 1, block))


class Outs:
    value = gram = None
    x = y = packed = ()


def least_squares(hessenberg, initial):
    upper = [list(row) for row in hessenberg]
    target = [initial] + [jnp.zeros_like(initial) for row_index in range(KRYLOV)]
    cosines = []
    sines = []
    for col_index in range(KRYLOV):
        for row_index in range(col_index):
            first = upper[row_index][col_index]
            second = upper[row_index + 1][col_index]
            upper[row_index][col_index] = cosines[row_index] * first + sines[row_index] * second
            upper[row_index + 1][col_index] = cosines[row_index] * second - sines[row_index] * first
        first = upper[col_index][col_index]
        second = upper[col_index + 1][col_index]
        radius = jnp.sqrt(first * first + second * second)
        cosine = first / radius
        sine_value = second / radius
        upper[col_index][col_index] = radius
        target[col_index + 1] = -sine_value * target[col_index]
        target[col_index] = cosine * target[col_index]
        cosines.append(cosine)
        sines.append(sine_value)
    combo = [None] * KRYLOV
    for row_index in reversed(range(KRYLOV)):
        running = target[row_index]
        for col_index in range(row_index + 1, KRYLOV):
            running = running - upper[row_index][col_index] * combo[col_index]
        combo[row_index] = running / upper[row_index][row_index]
    return combo


def arnoldi(gram):
    size = KRYLOV + 1

    def inner(left, right):
        total = None
        for i in range(size):
            for j in range(size):
                if left[i] is None or right[j] is None:
                    continue
                term = left[i] * right[j] * gram[min(i, j)][max(i, j)]
                total = term if total is None else total + term
        return total

    initial = jnp.sqrt(gram[0][0] + epsilon)
    basis = [[1.0 / initial] + [None] * KRYLOV]
    zero = jnp.zeros_like(initial)
    hessenberg = [[zero] * KRYLOV for row_index in range(size)]
    for section in range(KRYLOV):
        vector = basis[section]
        image = [None] * size
        for k in range(section + 2):
            parts = []
            if k > 0 and vector[k - 1] is not None:
                parts.append(vector[k - 1])
            if vector[k] is not None:
                parts.append(SHIFT * vector[k])
            image[k] = sum(parts[1:], parts[0])
        rest = list(image)
        for earlier in range(section + 1):
            coefficient = inner(basis[earlier], image)
            hessenberg[earlier][section] = coefficient
            for k in range(earlier + 1):
                rest[k] = rest[k] - coefficient * basis[earlier][k]
        length = jnp.sqrt(jnp.maximum(inner(rest, rest), 0.0) + epsilon)
        hessenberg[section + 1][section] = length
        basis.append([None if part is None else part / length for part in rest])
    combo = least_squares(hessenberg, initial)
    weights = []
    for k in range(KRYLOV):
        total = zero
        for j in range(k, KRYLOV):
            total = total + combo[j] * basis[j][k]
        weights.append(total)
    return hessenberg, weights


def finish_kernel(gram_ref, *refs):
    vectors, (solution_ref, hessenberg_ref) = refs[:KRYLOV], refs[KRYLOV:]
    block = gram_ref.shape[2]
    total = jnp.sum(gram_ref[...], axis=0)
    lane = lax.broadcasted_iota(jnp.int32, (1, block), 1)
    gram = [[None] * (KRYLOV + 1) for i in range(KRYLOV + 1)]
    at = 0
    for i in range(KRYLOV + 1):
        for j in range(i, KRYLOV + 1):
            entry = jnp.sum(jnp.where(lane == at, total, 0.0), axis=1, keepdims=True)
            gram[i][j] = jnp.broadcast_to(entry, (1, block))
            at += 1
    hessenberg, weights = arnoldi(gram)
    rows = lax.broadcasted_iota(jnp.int32, (KRYLOV + 1, KRYLOV), 0)
    cols = lax.broadcasted_iota(jnp.int32, (KRYLOV + 1, KRYLOV), 1)
    table = jnp.zeros((KRYLOV + 1, KRYLOV), jnp.float32)
    for i in range(KRYLOV + 1):
        for j in range(KRYLOV):
            table = jnp.where((rows == i) & (cols == j), hessenberg[i][j][:, :KRYLOV], table)
    hessenberg_ref[...] = table
    for b in range(solution_ref.shape[1] // block):
        lanes = slice(b * block, (b + 1) * block)
        solution_ref[:, lanes] = sum(
            weight * ref[:, lanes] for weight, ref in zip(weights, vectors)
        )


VMEM = pl.BlockSpec(memory_space=pltpu.VMEM)
ANY = pl.BlockSpec(memory_space=pl.ANY)
SCOPED = 16 * 1024 * 1024


def call(name, kernel, groups, shapes, scratch=(), flops=0):
    flat = [pair for group in groups for pair in group]

    def body(*refs):
        refs = list(refs)
        lists = []
        for group in groups:
            lists.append(refs[: len(group)])
            del refs[: len(group)]
        kernel(*lists, refs[: len(shapes)], refs[len(shapes) :])

    size = sum(operand.size * operand.dtype.itemsize for spec, operand in flat)
    size += sum(shape.size * shape.dtype.itemsize for shape in shapes)
    return pl.pallas_call(
        body,
        out_shape=list(shapes),
        in_specs=[spec for spec, operand in flat],
        out_specs=[VMEM] * len(shapes),
        scratch_shapes=list(scratch),
        compiler_params=pltpu.CompilerParams(vmem_limit_bytes=SCOPED),
        cost_estimate=pl.CostEstimate(flops=flops, bytes_accessed=size, transcendentals=0),
        name=name,
    )(*[operand for spec, operand in flat])


def in_vmem(operands):
    return [(VMEM, operand) for operand in operands]


def per_device(right_side, col_block, blocks, relax_rate, drift_speed, upwind_sign, wall_mask):
    first, second, local_modes = right_side.shape
    local_blocks, slots, block = blocks.shape[:3]
    cells = first * second
    count = lax.axis_size("mode")
    devices = count * lax.axis_size("gx") * lax.axis_size("gy")
    per_owner = slots // count
    sizes = (first, second, local_blocks, block)
    x_moves, y_moves = len(moves_of(lax.axis_size("gx"))), len(moves_of(lax.axis_size("gy")))
    n_faces = x_moves + y_moves
    f32 = jnp.float32
    shape_of = jax.ShapeDtypeStruct
    face_shapes = [shape_of((second, local_modes), f32)] * x_moves + [
        shape_of((first, local_modes), f32)
    ] * y_moves
    parts = 2 if cells % 32 == 0 else 1
    packed_shapes = [shape_of((cells, local_modes), jnp.bfloat16)]
    packed_shapes += [shape_of((cells // parts, local_modes), jnp.bfloat16)] * parts
    vector_shape = shape_of((cells, local_modes), f32)
    near = [place for place in (0, 1) if place < count]
    final = [place for place in range(3, count) if place % 2 == 1]
    middle = [place for place in range(2, count) if place not in final]

    start = right_side.reshape(cells, local_modes)

    def pack(ins, outs, scratch):
        store_packed(outs, slice(None), ins[0][...])

    packed = call("pack", pack, [in_vmem([start])], packed_shapes, flops=8 * 10**9)

    def prepare(ins, outs, scratch):
        faces, (open_ref,) = outs[:n_faces], outs[n_faces:]
        prepare_kernel(sizes, *ins, faces[:x_moves], faces[x_moves:], open_ref)

    *faces, open_cells = call(
        "prepare",
        prepare,
        [in_vmem([start, wall_mask])],
        face_shapes + [shape_of((cells, block), f32)],
        flops=1 * 10**9,
    )
    columns = col_block.T

    work = 2 * cells * local_modes * per_owner * block
    vectors = [start]
    for section in range(KRYLOV):
        sources = {0: packed[0]}
        held = gather_far(packed[0])
        neighbour = [exchange(part, 1) for part in packed[1:]] if count > 1 else []
        y_in, x_in = move_faces({"gx": faces[:x_moves], "gy": faces[x_moves:]})

        def near_step(cols, sources, rest, params, outs, scratch):
            sources = [sources[:1], sources[1:]]
            blocks_ref, current_ref, open_ref = rest
            near_kernel(
                sizes, per_owner, near, cols[0], sources, blocks_ref, current_ref, params,
                open_ref, outs[0],
            )

        (partial,) = call(
            "near_%d" % section,
            near_step,
            [
                in_vmem([columns]),
                in_vmem([packed[0], *neighbour]),
                in_vmem([blocks, vectors[-1], open_cells]),
                in_vmem([relax_rate, drift_speed, upwind_sign]),
            ],
            [vector_shape],
            flops=work * len(near),
        )

        held = dict(zip(held, hand_on(list(held.values()), [partial, *x_in, *y_in])))
        for place, array in held.items():
            sources[place] = array
            sources[place ^ 1] = exchange(array, 1)

        def middle_step(cols, sources, rest, x_in, y_in, outs, scratch):
            middle_kernel(
                sizes, per_owner, middle, cols[0], [[ref] for ref in sources], *rest, x_in, y_in, outs[0]
            )

        (partial,) = call(
            "middle_%d" % section,
            middle_step,
            [
                in_vmem([columns]),
                in_vmem([sources[place] for place in middle]),
                in_vmem([blocks, partial, drift_speed, upwind_sign]),
                in_vmem(x_in),
                in_vmem(y_in),
            ],
            [vector_shape],
            flops=work * len(middle),
        )

        last = section == KRYLOV - 1
        def last_step(cols, sources, rest, earlier, outs, scratch, last=last):
            blocks_ref, partial_ref, open_ref = rest
            named = Outs()
            if last:
                named.gram = outs[0]
            else:
                named.x, named.y = outs[:x_moves], outs[x_moves:n_faces]
                *named.packed, named.value = outs[n_faces:]
            last_kernel(
                sizes, per_owner, final, cols[0], [[ref] for ref in sources], blocks_ref, partial_ref,
                earlier, open_ref, named,
            )

        if last:
            shapes = [shape_of((devices, 1, block), f32)]
        else:
            shapes = face_shapes + packed_shapes + [vector_shape]
        results = call(
            "last_%d" % section,
            last_step,
            [
                in_vmem([columns]),
                in_vmem([sources[place] for place in final]),
                in_vmem([blocks, partial, open_cells]),
                in_vmem(vectors if last else []),
            ],
            shapes,
            flops=work * len(final),
        )
        if last:
            (gram,) = results
        else:
            faces, packed, value = results[:n_faces], results[n_faces:-1], results[-1]
            vectors.append(value)

    gram = lax.all_to_all(gram, AXES, 0, 0)

    def finish(ins, outs, scratch):
        finish_kernel(*ins, *outs)

    solution, hessenberg = call(
        "finish",
        finish,
        [in_vmem([gram, *vectors])],
        [vector_shape, shape_of((KRYLOV + 1, KRYLOV), f32)],
    )
    return solution.reshape(first, second, local_modes), hessenberg


def solution(mesh):
    return jax.shard_map(
        per_device,
        mesh=mesh,
        in_specs=(
            P("gx", "gy", "mode"),
            P("mode", None),
            P("mode", None, None, None),
            P("mode"),
            P(None, "mode"),
            P(None, "mode"),
            P("gx", "gy"),
        ),
        out_specs=(P("gx", "gy", "mode"), P()),
        check_vma=False,
    )
```

```python
import functools

import jax
import jax.numpy as jnp
from jax import lax
from jax.experimental import pallas as pl
from jax.experimental.pallas import tpu as pltpu
from jax.sharding import PartitionSpec as P

KRYLOV = 3
SHIFT = 4.05
AXES = ("mode", "gx", "gy")

epsilon = 1e-12


def moves_of(count):
    moves = []
    for first in (0, 1)[: count - 1]:
        partner = list(range(count))
        for low in range(first, count - 1, 2):
            partner[low], partner[low + 1] = low + 1, low
        moves.append(partner)
    return moves


def move_faces(faces):
    received = []
    shards = lax.axis_size("mode")
    for axis in ("gy", "gx"):
        count = lax.axis_size(axis)
        arrived = []
        for face, partner in zip(faces[axis], moves_of(count)):
            pairs = []
            for shard in range(shards):
                for at in range(count):
                    alone = partner[at] == at
                    other = (shard ^ 1 if alone and shards > 1 else shard) * count + partner[at]
                    pairs.append((shard * count + at, other))
            arrived.append(lax.ppermute(face, ("mode", axis), pairs))
        received.append(arrived)
    return received


def exchange(array, bit):
    count = lax.axis_size("mode")
    return lax.ppermute(array, "mode", [(i, i ^ bit) for i in range(count)])


def gather_far(packed):
    held = {0: packed}
    bit = lax.axis_size("mode") // 2
    while bit > 1:
        for key in list(held):
            held[key ^ bit] = exchange(held[key], bit)
        bit //= 2
    del held[0]
    return held


def store_packed(refs, lanes, value):
    refs[0][:, lanes] = value.astype(jnp.bfloat16)
    at = 0
    for ref in refs[1:]:
        rows = ref.shape[0]
        ref[:, lanes] = value[at : at + rows].astype(jnp.bfloat16)
        at += rows


def hand_on(arrays, after):
    count = len(arrays)
    if not count:
        return []
    return pl.pallas_call(
        lambda *refs: None,
        out_shape=[jax.ShapeDtypeStruct(array.shape, array.dtype) for array in arrays],
        in_specs=[ANY] * (count + len(after)),
        out_specs=[ANY] * count,
        input_output_aliases={at: at for at in range(count)},
        compiler_params=pltpu.CompilerParams(vmem_limit_bytes=SCOPED),
        name="hand_on",
    )(*arrays, *after)


def store_faces(refs, axis, lanes, low, high):
    even = lax.rem(lax.axis_index(axis), 2) == 0
    for ref, take_high in zip(refs, (even, jnp.logical_not(even))):
        ref[:, lanes] = jnp.where(take_high, high, low)


def write_faces(masked, lanes, first, second, x_refs, y_refs):
    store_faces(x_refs, "gx", lanes, masked[0], masked[first - 1])
    store_faces(y_refs, "gy", lanes, masked[:, 0, :], masked[:, second - 1, :])


def halos(refs, axis, lanes, shape):
    zero = jnp.zeros(shape, jnp.float32)
    if not refs:
        return zero, zero
    at = lax.axis_index(axis)
    odd = lax.rem(at, 2) == 1
    one, two = refs[0][:, lanes], refs[-1][:, lanes]
    low, high = jnp.where(odd, one, two), jnp.where(odd, two, one)
    return jnp.where(at == 0, zero, low), jnp.where(at == lax.axis_size(axis) - 1, zero, high)


def prepare_kernel(sizes, rhs_ref, wall_ref, x_refs, y_refs, open_ref):
    first, second, local_blocks, block = sizes
    wall = wall_ref[...].astype(jnp.float32)
    eye = (
        lax.broadcasted_iota(jnp.int32, (second, second), 0)
        == lax.broadcasted_iota(jnp.int32, (second, second), 1)
    ).astype(jnp.float32)
    for row in range(first):
        column = jnp.sum(eye * (1.0 - wall[row : row + 1, :]), axis=1, keepdims=True)
        open_ref[row * second : (row + 1) * second, :] = jnp.broadcast_to(column, (second, block))
    for b in range(local_blocks):
        lanes = slice(b * block, (b + 1) * block)
        masked = (rhs_ref[:, lanes] * open_ref[...]).reshape(first, second, block)
        write_faces(masked, lanes, first, second, x_refs, y_refs)


def scatter(sizes, per_owner, b, places, cols_ref, sources, blocks_ref):
    first, second, local_blocks, block = sizes
    mine = lax.axis_index("mode")
    picks, weights = [], []
    for place, source in zip(places, sources):
        owner = mine ^ place
        for p in range(per_owner):
            slot = owner * per_owner + p
            column = cols_ref[slot, b] - owner * local_blocks
            lanes = pl.ds(pl.multiple_of(column * block, block), block)
            picks.append(jnp.concatenate([part[:, lanes] for part in source], axis=0))
            weights.append(blocks_ref[b, slot])
    return lax.dot_general(
        jnp.concatenate(picks, axis=1),
        jnp.concatenate(weights, axis=1),
        (((1,), (1,)), ((), ())),
        preferred_element_type=jnp.float32,
    )


def add_product(sums, key, left, right):
    cells, block = left.shape
    term = jnp.sum((left * right).reshape(cells // 8, 8, block), axis=0)
    sums[key] = sums[key] + term if key in sums else term


def lane_sum(value):
    return jnp.sum(jnp.sum(value, axis=0, keepdims=True), axis=1, keepdims=True)


def early_products(sizes, vectors, early_ref):
    first, second, local_blocks, block = sizes
    sums = {}
    for b in range(local_blocks):
        lanes = slice(b * block, (b + 1) * block)
        values = [ref[:, lanes] for ref in vectors]
        for i in range(len(values)):
            for j in range(i, len(values)):
                add_product(sums, (i, j), values[i], values[j])
    at = 0
    for i in range(len(vectors) + 1):
        for j in range(i, len(vectors) + 1):
            if j < len(vectors):
                early_ref[at : at + 1, :] = jnp.broadcast_to(lane_sum(sums[i, j]), (1, block))
            at += 1


def split_speeds(speed_ref, sign_ref, lanes):
    parts = []
    for axis in range(2):
        speed, sign = speed_ref[axis : axis + 1, lanes], sign_ref[axis : axis + 1, lanes]
        parts += [jnp.where(sign == 1, speed, 0.0), jnp.where(sign == 1, 0.0, speed)]
    return parts


def near_kernel(sizes, per_owner, places, cols_ref, sources, blocks_ref, current_ref, params, open_ref, out_ref, finer_ref=None):
    first, second, local_blocks, block = sizes
    cells = first * second
    open_cells = open_ref[...]
    row_at = lax.broadcasted_iota(jnp.int32, (first, second, block), 1)
    zero = jnp.zeros((1, second, block), jnp.float32)
    if finer_ref is not None:
        for b in range(local_blocks):
            lanes = slice(b * block, (b + 1) * block)
            rounded = sources[0][0][:, lanes].astype(jnp.float32)
            finer_ref[:, lanes] = (current_ref[:, lanes] - rounded).astype(jnp.bfloat16)
        places, sources = places + [0], sources + [[finer_ref]]
    for b in range(local_blocks):
        lanes = slice(b * block, (b + 1) * block)
        scattered = scatter(sizes, per_owner, b, places, cols_ref, sources, blocks_ref)
        current = current_ref[:, lanes]
        masked = (current * open_cells).reshape(first, second, block)
        relax_ref, speed_ref, sign_ref = params
        west, east, south, north = split_speeds(speed_ref, sign_ref, lanes)
        diagonal = relax_ref[lanes].reshape(1, block) + (west + east) + (south + north) - SHIFT
        from_west = jnp.concatenate([zero, masked[:-1]], axis=0)
        from_east = jnp.concatenate([masked[1:], zero], axis=0)
        from_south = jnp.where(row_at == 0, 0.0, pltpu.roll(masked, 1, axis=1))
        from_north = jnp.where(row_at == second - 1, 0.0, pltpu.roll(masked, second - 1, axis=1))
        drift = (
            west.reshape(1, 1, block) * from_west
            + east.reshape(1, 1, block) * from_east
            + south.reshape(1, 1, block) * from_south
            + north.reshape(1, 1, block) * from_north
        ).reshape(cells, block)
        out_ref[:, lanes] = diagonal * current - drift - scattered


def middle_kernel(sizes, per_owner, places, cols_ref, sources, blocks_ref, partial_ref, speed_ref, sign_ref, x_in, y_in, out_ref):
    first, second, local_blocks, block = sizes
    cells = first * second
    row_at = lax.broadcasted_iota(jnp.int32, (first, second, block), 1)
    for b in range(local_blocks):
        lanes = slice(b * block, (b + 1) * block)
        value = partial_ref[:, lanes]
        if places:
            value = value - scatter(sizes, per_owner, b, places, cols_ref, sources, blocks_ref)
        west, east, south, north = split_speeds(speed_ref, sign_ref, lanes)
        west_in, east_in = halos(x_in, "gx", lanes, (second, block))
        south_in, north_in = halos(y_in, "gy", lanes, (first, block))
        value = value.reshape(first, second, block)
        value = value - jnp.where(
            row_at == 0,
            (south * south_in)[:, None, :],
            jnp.where(row_at == second - 1, (north * north_in)[:, None, :], 0.0),
        )
        value = jnp.concatenate(
            [value[:1] - (west * west_in)[None], value[1:-1], value[-1:] - (east * east_in)[None]],
            axis=0,
        )
        out_ref[:, lanes] = value.reshape(cells, block)


def last_kernel(sizes, per_owner, places, cols_ref, sources, blocks_ref, partial_ref, earlier, open_ref, outs, early_ref=None):
    first, second, local_blocks, block = sizes
    cells = first * second
    sums = {}
    for b in range(local_blocks):
        lanes = slice(b * block, (b + 1) * block)
        scattered = scatter(sizes, per_owner, b, places, cols_ref, sources, blocks_ref)
        result = partial_ref[:, lanes] - scattered
        if outs.gram is None:
            outs.value[:, lanes] = result
            store_packed(outs.packed, lanes, result)
            write_faces(
                (result * open_ref[...]).reshape(first, second, block),
                lanes, first, second, outs.x, outs.y,
            )
        else:
            vectors = [ref[:, lanes] for ref in earlier] + [result]
            for i, vector in enumerate(vectors):
                add_product(sums, (i, len(earlier)), vector, result)
    if outs.gram is not None:
        devices = outs.gram.shape[0]
        lane = lax.broadcasted_iota(jnp.int32, (1, block), 1)
        row = jnp.zeros((1, block), jnp.float32)
        size = len(earlier) + 1
        at = 0
        for i in range(size):
            for j in range(i, size):
                if j < size - 1:
                    total = early_ref[at : at + 1, :]
                else:
                    total = lane_sum(sums[i, j])
                row = jnp.where(lane == at, total, row)
                at += 1
        outs.gram[...] = jnp.broadcast_to(row[None], (devices, 1, block))


class Outs:
    value = gram = None
    x = y = packed = ()


def least_squares(hessenberg, initial):
    upper = [list(row) for row in hessenberg]
    target = [initial] + [jnp.zeros_like(initial) for row_index in range(KRYLOV)]
    cosines = []
    sines = []
    for col_index in range(KRYLOV):
        for row_index in range(col_index):
            first = upper[row_index][col_index]
            second = upper[row_index + 1][col_index]
            upper[row_index][col_index] = cosines[row_index] * first + sines[row_index] * second
            upper[row_index + 1][col_index] = cosines[row_index] * second - sines[row_index] * first
        first = upper[col_index][col_index]
        second = upper[col_index + 1][col_index]
        radius = jnp.sqrt(first * first + second * second)
        cosine = first / radius
        sine_value = second / radius
        upper[col_index][col_index] = radius
        target[col_index + 1] = -sine_value * target[col_index]
        target[col_index] = cosine * target[col_index]
        cosines.append(cosine)
        sines.append(sine_value)
    combo = [None] * KRYLOV
    for row_index in reversed(range(KRYLOV)):
        running = target[row_index]
        for col_index in range(row_index + 1, KRYLOV):
            running = running - upper[row_index][col_index] * combo[col_index]
        combo[row_index] = running / upper[row_index][row_index]
    return combo


def arnoldi(gram):
    size = KRYLOV + 1

    def inner(left, right):
        total = None
        for i in range(size):
            for j in range(size):
                if left[i] is None or right[j] is None:
                    continue
                term = left[i] * right[j] * gram[min(i, j)][max(i, j)]
                total = term if total is None else total + term
        return total

    initial = jnp.sqrt(gram[0][0] + epsilon)
    basis = [[1.0 / initial] + [None] * KRYLOV]
    zero = jnp.zeros_like(initial)
    hessenberg = [[zero] * KRYLOV for row_index in range(size)]
    for section in range(KRYLOV):
        vector = basis[section]
        image = [None] * size
        for k in range(section + 2):
            parts = []
            if k > 0 and vector[k - 1] is not None:
                parts.append(vector[k - 1])
            if vector[k] is not None:
                parts.append(SHIFT * vector[k])
            image[k] = sum(parts[1:], parts[0])
        rest = list(image)
        for earlier in range(section + 1):
            coefficient = inner(basis[earlier], image)
            hessenberg[earlier][section] = coefficient
            for k in range(earlier + 1):
                rest[k] = rest[k] - coefficient * basis[earlier][k]
        length = jnp.sqrt(jnp.maximum(inner(rest, rest), 0.0) + epsilon)
        hessenberg[section + 1][section] = length
        basis.append([None if part is None else part / length for part in rest])
    combo = least_squares(hessenberg, initial)
    weights = []
    for k in range(KRYLOV):
        total = zero
        for j in range(k, KRYLOV):
            total = total + combo[j] * basis[j][k]
        weights.append(total)
    return hessenberg, weights


def finish_kernel(gram_ref, *refs):
    vectors, (solution_ref, hessenberg_ref) = refs[:KRYLOV], refs[KRYLOV:]
    block = gram_ref.shape[2]
    total = jnp.sum(gram_ref[...], axis=0)
    lane = lax.broadcasted_iota(jnp.int32, (1, block), 1)
    gram = [[None] * (KRYLOV + 1) for i in range(KRYLOV + 1)]
    at = 0
    for i in range(KRYLOV + 1):
        for j in range(i, KRYLOV + 1):
            entry = jnp.sum(jnp.where(lane == at, total, 0.0), axis=1, keepdims=True)
            gram[i][j] = jnp.broadcast_to(entry, (1, block))
            at += 1
    hessenberg, weights = arnoldi(gram)
    rows = lax.broadcasted_iota(jnp.int32, (KRYLOV + 1, KRYLOV), 0)
    cols = lax.broadcasted_iota(jnp.int32, (KRYLOV + 1, KRYLOV), 1)
    table = jnp.zeros((KRYLOV + 1, KRYLOV), jnp.float32)
    for i in range(KRYLOV + 1):
        for j in range(KRYLOV):
            table = jnp.where((rows == i) & (cols == j), hessenberg[i][j][:, :KRYLOV], table)
    hessenberg_ref[...] = table
    for b in range(solution_ref.shape[1] // block):
        lanes = slice(b * block, (b + 1) * block)
        solution_ref[:, lanes] = sum(
            weight * ref[:, lanes] for weight, ref in zip(weights, vectors)
        )


VMEM = pl.BlockSpec(memory_space=pltpu.VMEM)
ANY = pl.BlockSpec(memory_space=pl.ANY)
SCOPED = 16 * 1024 * 1024


def call(name, kernel, groups, shapes, scratch=(), flops=0):
    flat = [pair for group in groups for pair in group]

    def body(*refs):
        refs = list(refs)
        lists = []
        for group in groups:
            lists.append(refs[: len(group)])
            del refs[: len(group)]
        kernel(*lists, refs[: len(shapes)], refs[len(shapes) :])

    size = sum(operand.size * operand.dtype.itemsize for spec, operand in flat)
    size += sum(shape.size * shape.dtype.itemsize for shape in shapes)
    return pl.pallas_call(
        body,
        out_shape=list(shapes),
        in_specs=[spec for spec, operand in flat],
        out_specs=[VMEM] * len(shapes),
        scratch_shapes=list(scratch),
        compiler_params=pltpu.CompilerParams(vmem_limit_bytes=SCOPED),
        cost_estimate=pl.CostEstimate(flops=flops, bytes_accessed=size, transcendentals=0),
        name=name,
    )(*[operand for spec, operand in flat])


def in_vmem(operands):
    return [(VMEM, operand) for operand in operands]


def per_device(right_side, col_block, blocks, relax_rate, drift_speed, upwind_sign, wall_mask):
    first, second, local_modes = right_side.shape
    local_blocks, slots, block = blocks.shape[:3]
    cells = first * second
    count = lax.axis_size("mode")
    devices = count * lax.axis_size("gx") * lax.axis_size("gy")
    per_owner = slots // count
    sizes = (first, second, local_blocks, block)
    x_moves, y_moves = len(moves_of(lax.axis_size("gx"))), len(moves_of(lax.axis_size("gy")))
    n_faces = x_moves + y_moves
    f32 = jnp.float32
    shape_of = jax.ShapeDtypeStruct
    face_shapes = [shape_of((second, local_modes), f32)] * x_moves + [
        shape_of((first, local_modes), f32)
    ] * y_moves
    parts = 2 if cells % 32 == 0 else 1
    packed_shapes = [shape_of((cells, local_modes), jnp.bfloat16)]
    packed_shapes += [shape_of((cells // parts, local_modes), jnp.bfloat16)] * parts
    vector_shape = shape_of((cells, local_modes), f32)
    near = [place for place in (0, 1) if place < count]
    final = [place for place in range(3, count) if place % 2 == 1]
    middle = [place for place in range(2, count) if place not in final]

    start = right_side.reshape(cells, local_modes)

    def pack(ins, outs, scratch):
        store_packed(outs, slice(None), ins[0][...])

    packed = call("pack", pack, [in_vmem([start])], packed_shapes, flops=8 * 10**9)

    def prepare(ins, outs, scratch):
        faces, (open_ref,) = outs[:n_faces], outs[n_faces:]
        prepare_kernel(sizes, *ins, faces[:x_moves], faces[x_moves:], open_ref)

    *faces, open_cells = call(
        "prepare",
        prepare,
        [in_vmem([start, wall_mask])],
        face_shapes + [shape_of((cells, block), f32)],
        flops=1 * 10**9,
    )
    columns = col_block.T

    work = 2 * cells * local_modes * per_owner * block
    vectors = [start]
    for section in range(KRYLOV):
        sources = {0: packed[0]}
        held = gather_far(packed[0])
        neighbour = [exchange(part, 1) for part in packed[1:]] if count > 1 else []
        y_in, x_in = move_faces({"gx": faces[:x_moves], "gy": faces[x_moves:]})

        last = section == KRYLOV - 1

        def near_step(cols, sources, rest, params, known, outs, scratch, section=section, last=last):
            sources = [sources[:1], sources[1:]][: len(near)]
            blocks_ref, current_ref, open_ref = rest
            near_kernel(
                sizes, per_owner, near, cols[0], sources, blocks_ref, current_ref, params,
                open_ref, outs[0], scratch[0] if section == 0 else None,
            )
            if last:
                early_products(sizes, known, outs[1])

        partial, *early = call(
            "near_%d" % section,
            near_step,
            [
                in_vmem([columns]),
                in_vmem([packed[0], *neighbour]),
                in_vmem([blocks, vectors[-1], open_cells]),
                in_vmem([relax_rate, drift_speed, upwind_sign]),
                in_vmem(vectors if last else []),
            ],
            [vector_shape] + [shape_of((16, block), f32)] * last,
            [pltpu.VMEM((cells, local_modes), jnp.bfloat16)] * (section == 0),
            flops=work * len(near),
        )

        held = dict(zip(held, hand_on(list(held.values()), [partial, *x_in, *y_in])))
        for place, array in held.items():
            sources[place] = array
            sources[place ^ 1] = exchange(array, 1)

        def middle_step(cols, sources, rest, x_in, y_in, outs, scratch):
            middle_kernel(
                sizes, per_owner, middle, cols[0], [[ref] for ref in sources], *rest, x_in, y_in, outs[0]
            )

        (partial,) = call(
            "middle_%d" % section,
            middle_step,
            [
                in_vmem([columns]),
                in_vmem([sources[place] for place in middle]),
                in_vmem([blocks, partial, drift_speed, upwind_sign]),
                in_vmem(x_in),
                in_vmem(y_in),
            ],
            [vector_shape],
            flops=work * len(middle),
        )

        def last_step(cols, sources, rest, earlier, early, outs, scratch, last=last):
            blocks_ref, partial_ref, open_ref = rest
            named = Outs()
            if last:
                named.gram = outs[0]
            else:
                named.x, named.y = outs[:x_moves], outs[x_moves:n_faces]
                *named.packed, named.value = outs[n_faces:]
            last_kernel(
                sizes, per_owner, final, cols[0], [[ref] for ref in sources], blocks_ref, partial_ref,
                earlier, open_ref, named, early[0] if last else None,
            )

        if last:
            shapes = [shape_of((devices, 1, block), f32)]
        else:
            shapes = face_shapes + packed_shapes + [vector_shape]
        results = call(
            "last_%d" % section,
            last_step,
            [
                in_vmem([columns]),
                in_vmem([sources[place] for place in final]),
                in_vmem([blocks, partial, open_cells]),
                in_vmem(vectors if last else []),
                in_vmem(early),
            ],
            shapes,
            flops=work * len(final),
        )
        if last:
            (gram,) = results
        else:
            faces, packed, value = results[:n_faces], results[n_faces:-1], results[-1]
            vectors.append(value)

    gram = lax.all_to_all(gram, AXES, 0, 0)

    def finish(ins, outs, scratch):
        finish_kernel(*ins, *outs)

    solution, hessenberg = call(
        "finish",
        finish,
        [in_vmem([gram, *vectors])],
        [vector_shape, shape_of((KRYLOV + 1, KRYLOV), f32)],
    )
    return solution.reshape(first, second, local_modes), hessenberg


def solution(mesh):
    return jax.shard_map(
        per_device,
        mesh=mesh,
        in_specs=(
            P("gx", "gy", "mode"),
            P("mode", None),
            P("mode", None, None, None),
            P("mode"),
            P(None, "mode"),
            P(None, "mode"),
            P("gx", "gy"),
        ),
        out_specs=(P("gx", "gy", "mode"), P()),
        check_vma=False,
    )
```

```python
import functools

import jax
import jax.numpy as jnp
from jax import lax
from jax.experimental import pallas as pl
from jax.experimental.pallas import tpu as pltpu
from jax.sharding import PartitionSpec as P

KRYLOV = 3
SHIFT = 4.05
AXES = ("mode", "gx", "gy")

epsilon = 1e-12


def moves_of(count):
    moves = []
    for first in (0, 1)[: count - 1]:
        partner = list(range(count))
        for low in range(first, count - 1, 2):
            partner[low], partner[low + 1] = low + 1, low
        moves.append(partner)
    return moves


def move_faces(faces):
    received = []
    shards = lax.axis_size("mode")
    for axis in ("gy", "gx"):
        count = lax.axis_size(axis)
        arrived = []
        for face, partner in zip(faces[axis], moves_of(count)):
            pairs = []
            for shard in range(shards):
                for at in range(count):
                    alone = partner[at] == at
                    other = (shard ^ 1 if alone and shards > 1 else shard) * count + partner[at]
                    pairs.append((shard * count + at, other))
            arrived.append(lax.ppermute(face, ("mode", axis), pairs))
        received.append(arrived)
    return received


def exchange(array, bit):
    count = lax.axis_size("mode")
    return lax.ppermute(array, "mode", [(i, i ^ bit) for i in range(count)])


def gather_far(packed):
    held = {0: packed}
    bit = lax.axis_size("mode") // 2
    while bit > 1:
        for key in list(held):
            held[key ^ bit] = exchange(held[key], bit)
        bit //= 2
    del held[0]
    return held


def store_packed(refs, lanes, value):
    refs[0][:, lanes] = value.astype(jnp.bfloat16)
    at = 0
    for ref in refs[1:]:
        rows = ref.shape[0]
        ref[:, lanes] = value[at : at + rows].astype(jnp.bfloat16)
        at += rows


def hand_on(arrays, after):
    count = len(arrays)
    if not count:
        return []
    return pl.pallas_call(
        lambda *refs: None,
        out_shape=[jax.ShapeDtypeStruct(array.shape, array.dtype) for array in arrays],
        in_specs=[ANY] * (count + len(after)),
        out_specs=[ANY] * count,
        input_output_aliases={at: at for at in range(count)},
        compiler_params=pltpu.CompilerParams(vmem_limit_bytes=SCOPED),
        name="hand_on",
    )(*arrays, *after)


def store_faces(refs, axis, lanes, low, high):
    even = lax.rem(lax.axis_index(axis), 2) == 0
    for ref, take_high in zip(refs, (even, jnp.logical_not(even))):
        ref[:, lanes] = jnp.where(take_high, high, low)


def write_faces(masked, lanes, first, second, x_refs, y_refs):
    store_faces(x_refs, "gx", lanes, masked[0], masked[first - 1])
    store_faces(y_refs, "gy", lanes, masked[:, 0, :], masked[:, second - 1, :])


def halos(refs, axis, lanes, shape):
    zero = jnp.zeros(shape, jnp.float32)
    if not refs:
        return zero, zero
    at = lax.axis_index(axis)
    odd = lax.rem(at, 2) == 1
    one, two = refs[0][:, lanes], refs[-1][:, lanes]
    low, high = jnp.where(odd, one, two), jnp.where(odd, two, one)
    return jnp.where(at == 0, zero, low), jnp.where(at == lax.axis_size(axis) - 1, zero, high)


def prepare_kernel(sizes, rhs_ref, wall_ref, x_refs, y_refs, open_ref):
    first, second, local_blocks, block = sizes
    wall = wall_ref[...].astype(jnp.float32)
    eye = (
        lax.broadcasted_iota(jnp.int32, (second, second), 0)
        == lax.broadcasted_iota(jnp.int32, (second, second), 1)
    ).astype(jnp.float32)
    for row in range(first):
        column = jnp.sum(eye * (1.0 - wall[row : row + 1, :]), axis=1, keepdims=True)
        open_ref[row * second : (row + 1) * second, :] = jnp.broadcast_to(column, (second, block))
    for b in range(local_blocks):
        lanes = slice(b * block, (b + 1) * block)
        masked = (rhs_ref[:, lanes] * open_ref[...]).reshape(first, second, block)
        write_faces(masked, lanes, first, second, x_refs, y_refs)


def scatter(sizes, per_owner, b, places, cols_ref, sources, blocks_ref, turned=False):
    first, second, local_blocks, block = sizes
    mine = lax.axis_index("mode")
    picks, weights = [], []
    for place, source in zip(places, sources):
        owner = mine ^ place
        for p in range(per_owner):
            slot = owner * per_owner + p
            column = cols_ref[slot, b] - owner * local_blocks
            lanes = pl.ds(pl.multiple_of(column * block, block), block)
            picks.append(jnp.concatenate([part[:, lanes] for part in source], axis=0))
            if not turned:
                weights.append(blocks_ref[b, slot])
    picks = jnp.concatenate(picks, axis=1)
    if turned:
        return jnp.dot(picks, blocks_ref[b], preferred_element_type=jnp.float32)
    return lax.dot_general(
        picks,
        jnp.concatenate(weights, axis=1),
        (((1,), (1,)), ((), ())),
        preferred_element_type=jnp.float32,
    )


def turn_blocks(per_owner, places, blocks_ref, turned_ref):
    block = blocks_ref.shape[2]
    mine = lax.axis_index("mode")
    for b in range(blocks_ref.shape[0]):
        at = 0
        for place in places:
            for p in range(per_owner):
                turned_ref[b, at : at + block, :] = blocks_ref[b, (mine ^ place) * per_owner + p].T
                at += block


def add_product(sums, key, left, right):
    cells, block = left.shape
    term = jnp.sum((left * right).reshape(cells // 8, 8, block), axis=0)
    sums[key] = sums[key] + term if key in sums else term


def lane_sum(value):
    return jnp.sum(jnp.sum(value, axis=0, keepdims=True), axis=1, keepdims=True)


def early_products(sizes, vectors, early_ref):
    first, second, local_blocks, block = sizes
    sums = {}
    for b in range(local_blocks):
        lanes = slice(b * block, (b + 1) * block)
        values = [ref[:, lanes] for ref in vectors]
        for i in range(len(values)):
            for j in range(i, len(values)):
                add_product(sums, (i, j), values[i], values[j])
    at = 0
    for i in range(len(vectors) + 1):
        for j in range(i, len(vectors) + 1):
            if j < len(vectors):
                early_ref[at : at + 1, :] = jnp.broadcast_to(lane_sum(sums[i, j]), (1, block))
            at += 1


def split_speeds(speed_ref, sign_ref, lanes):
    parts = []
    for axis in range(2):
        speed, sign = speed_ref[axis : axis + 1, lanes], sign_ref[axis : axis + 1, lanes]
        parts += [jnp.where(sign == 1, speed, 0.0), jnp.where(sign == 1, 0.0, speed)]
    return parts


def near_kernel(sizes, per_owner, places, cols_ref, sources, blocks_ref, current_ref, params, open_ref, out_ref, finer_ref=None):
    first, second, local_blocks, block = sizes
    cells = first * second
    open_cells = open_ref[...]
    row_at = lax.broadcasted_iota(jnp.int32, (first, second, block), 1)
    zero = jnp.zeros((1, second, block), jnp.float32)
    if finer_ref is not None:
        for b in range(local_blocks):
            lanes = slice(b * block, (b + 1) * block)
            rounded = sources[0][0][:, lanes].astype(jnp.float32)
            finer_ref[:, lanes] = (current_ref[:, lanes] - rounded).astype(jnp.bfloat16)
        places, sources = places + [0], sources + [[finer_ref]]
    for b in range(local_blocks):
        lanes = slice(b * block, (b + 1) * block)
        scattered = scatter(sizes, per_owner, b, places, cols_ref, sources, blocks_ref)
        current = current_ref[:, lanes]
        masked = (current * open_cells).reshape(first, second, block)
        relax_ref, speed_ref, sign_ref = params
        west, east, south, north = split_speeds(speed_ref, sign_ref, lanes)
        diagonal = relax_ref[lanes].reshape(1, block) + (west + east) + (south + north) - SHIFT
        from_west = jnp.concatenate([zero, masked[:-1]], axis=0)
        from_east = jnp.concatenate([masked[1:], zero], axis=0)
        from_south = jnp.where(row_at == 0, 0.0, pltpu.roll(masked, 1, axis=1))
        from_north = jnp.where(row_at == second - 1, 0.0, pltpu.roll(masked, second - 1, axis=1))
        drift = (
            west.reshape(1, 1, block) * from_west
            + east.reshape(1, 1, block) * from_east
            + south.reshape(1, 1, block) * from_south
            + north.reshape(1, 1, block) * from_north
        ).reshape(cells, block)
        out_ref[:, lanes] = diagonal * current - drift - scattered


def middle_kernel(sizes, per_owner, places, cols_ref, sources, blocks_ref, partial_ref, speed_ref, sign_ref, x_in, y_in, out_ref):
    first, second, local_blocks, block = sizes
    cells = first * second
    row_at = lax.broadcasted_iota(jnp.int32, (first, second, block), 1)
    for b in range(local_blocks):
        lanes = slice(b * block, (b + 1) * block)
        value = partial_ref[:, lanes]
        if places:
            value = value - scatter(sizes, per_owner, b, places, cols_ref, sources, blocks_ref)
        west, east, south, north = split_speeds(speed_ref, sign_ref, lanes)
        west_in, east_in = halos(x_in, "gx", lanes, (second, block))
        south_in, north_in = halos(y_in, "gy", lanes, (first, block))
        value = value.reshape(first, second, block)
        value = value - jnp.where(
            row_at == 0,
            (south * south_in)[:, None, :],
            jnp.where(row_at == second - 1, (north * north_in)[:, None, :], 0.0),
        )
        value = jnp.concatenate(
            [value[:1] - (west * west_in)[None], value[1:-1], value[-1:] - (east * east_in)[None]],
            axis=0,
        )
        out_ref[:, lanes] = value.reshape(cells, block)


def last_kernel(sizes, per_owner, places, cols_ref, sources, blocks_ref, partial_ref, earlier, open_ref, outs, early_ref=None):
    first, second, local_blocks, block = sizes
    cells = first * second
    sums = {}
    for b in range(local_blocks):
        lanes = slice(b * block, (b + 1) * block)
        scattered = scatter(sizes, per_owner, b, places, cols_ref, sources, blocks_ref, True)
        result = partial_ref[:, lanes] - scattered
        if outs.gram is None:
            outs.value[:, lanes] = result
            store_packed(outs.packed, lanes, result)
            write_faces(
                (result * open_ref[...]).reshape(first, second, block),
                lanes, first, second, outs.x, outs.y,
            )
        else:
            vectors = [ref[:, lanes] for ref in earlier] + [result]
            for i, vector in enumerate(vectors):
                add_product(sums, (i, len(earlier)), vector, result)
    if outs.gram is not None:
        devices = outs.gram.shape[0]
        lane = lax.broadcasted_iota(jnp.int32, (1, block), 1)
        row = jnp.zeros((1, block), jnp.float32)
        size = len(earlier) + 1
        at = 0
        for i in range(size):
            for j in range(i, size):
                if j < size - 1:
                    total = early_ref[at : at + 1, :]
                else:
                    total = lane_sum(sums[i, j])
                row = jnp.where(lane == at, total, row)
                at += 1
        outs.gram[...] = jnp.broadcast_to(row[None], (devices, 1, block))


class Outs:
    value = gram = None
    x = y = packed = ()


def least_squares(hessenberg, initial):
    upper = [list(row) for row in hessenberg]
    target = [initial] + [jnp.zeros_like(initial) for row_index in range(KRYLOV)]
    cosines = []
    sines = []
    for col_index in range(KRYLOV):
        for row_index in range(col_index):
            first = upper[row_index][col_index]
            second = upper[row_index + 1][col_index]
            upper[row_index][col_index] = cosines[row_index] * first + sines[row_index] * second
            upper[row_index + 1][col_index] = cosines[row_index] * second - sines[row_index] * first
        first = upper[col_index][col_index]
        second = upper[col_index + 1][col_index]
        radius = jnp.sqrt(first * first + second * second)
        cosine = first / radius
        sine_value = second / radius
        upper[col_index][col_index] = radius
        target[col_index + 1] = -sine_value * target[col_index]
        target[col_index] = cosine * target[col_index]
        cosines.append(cosine)
        sines.append(sine_value)
    combo = [None] * KRYLOV
    for row_index in reversed(range(KRYLOV)):
        running = target[row_index]
        for col_index in range(row_index + 1, KRYLOV):
            running = running - upper[row_index][col_index] * combo[col_index]
        combo[row_index] = running / upper[row_index][row_index]
    return combo


def arnoldi(gram):
    size = KRYLOV + 1

    def inner(left, right):
        total = None
        for i in range(size):
            for j in range(size):
                if left[i] is None or right[j] is None:
                    continue
                term = left[i] * right[j] * gram[min(i, j)][max(i, j)]
                total = term if total is None else total + term
        return total

    initial = jnp.sqrt(gram[0][0] + epsilon)
    basis = [[1.0 / initial] + [None] * KRYLOV]
    zero = jnp.zeros_like(initial)
    hessenberg = [[zero] * KRYLOV for row_index in range(size)]
    for section in range(KRYLOV):
        vector = basis[section]
        image = [None] * size
        for k in range(section + 2):
            parts = []
            if k > 0 and vector[k - 1] is not None:
                parts.append(vector[k - 1])
            if vector[k] is not None:
                parts.append(SHIFT * vector[k])
            image[k] = sum(parts[1:], parts[0])
        rest = list(image)
        for earlier in range(section + 1):
            coefficient = inner(basis[earlier], image)
            hessenberg[earlier][section] = coefficient
            for k in range(earlier + 1):
                rest[k] = rest[k] - coefficient * basis[earlier][k]
        length = jnp.sqrt(jnp.maximum(inner(rest, rest), 0.0) + epsilon)
        hessenberg[section + 1][section] = length
        basis.append([None if part is None else part / length for part in rest])
    combo = least_squares(hessenberg, initial)
    weights = []
    for k in range(KRYLOV):
        total = zero
        for j in range(k, KRYLOV):
            total = total + combo[j] * basis[j][k]
        weights.append(total)
    return hessenberg, weights


def finish_kernel(gram_ref, *refs):
    vectors, (solution_ref, hessenberg_ref) = refs[:KRYLOV], refs[KRYLOV:]
    block = gram_ref.shape[2]
    total = jnp.sum(gram_ref[...], axis=0)
    lane = lax.broadcasted_iota(jnp.int32, (1, block), 1)
    gram = [[None] * (KRYLOV + 1) for i in range(KRYLOV + 1)]
    at = 0
    for i in range(KRYLOV + 1):
        for j in range(i, KRYLOV + 1):
            entry = jnp.sum(jnp.where(lane == at, total, 0.0), axis=1, keepdims=True)
            gram[i][j] = jnp.broadcast_to(entry, (1, block))
            at += 1
    hessenberg, weights = arnoldi(gram)
    rows = lax.broadcasted_iota(jnp.int32, (KRYLOV + 1, KRYLOV), 0)
    cols = lax.broadcasted_iota(jnp.int32, (KRYLOV + 1, KRYLOV), 1)
    table = jnp.zeros((KRYLOV + 1, KRYLOV), jnp.float32)
    for i in range(KRYLOV + 1):
        for j in range(KRYLOV):
            table = jnp.where((rows == i) & (cols == j), hessenberg[i][j][:, :KRYLOV], table)
    hessenberg_ref[...] = table
    for b in range(solution_ref.shape[1] // block):
        lanes = slice(b * block, (b + 1) * block)
        solution_ref[:, lanes] = sum(
            weight * ref[:, lanes] for weight, ref in zip(weights, vectors)
        )


VMEM = pl.BlockSpec(memory_space=pltpu.VMEM)
ANY = pl.BlockSpec(memory_space=pl.ANY)
SCOPED = 16 * 1024 * 1024


def call(name, kernel, groups, shapes, scratch=(), flops=0):
    flat = [pair for group in groups for pair in group]

    def body(*refs):
        refs = list(refs)
        lists = []
        for group in groups:
            lists.append(refs[: len(group)])
            del refs[: len(group)]
        kernel(*lists, refs[: len(shapes)], refs[len(shapes) :])

    size = sum(operand.size * operand.dtype.itemsize for spec, operand in flat)
    size += sum(shape.size * shape.dtype.itemsize for shape in shapes)
    return pl.pallas_call(
        body,
        out_shape=list(shapes),
        in_specs=[spec for spec, operand in flat],
        out_specs=[VMEM] * len(shapes),
        scratch_shapes=list(scratch),
        compiler_params=pltpu.CompilerParams(vmem_limit_bytes=SCOPED),
        cost_estimate=pl.CostEstimate(flops=flops, bytes_accessed=size, transcendentals=0),
        name=name,
    )(*[operand for spec, operand in flat])


def in_vmem(operands):
    return [(VMEM, operand) for operand in operands]


def per_device(right_side, col_block, blocks, relax_rate, drift_speed, upwind_sign, wall_mask):
    first, second, local_modes = right_side.shape
    local_blocks, slots, block = blocks.shape[:3]
    cells = first * second
    count = lax.axis_size("mode")
    devices = count * lax.axis_size("gx") * lax.axis_size("gy")
    per_owner = slots // count
    sizes = (first, second, local_blocks, block)
    x_moves, y_moves = len(moves_of(lax.axis_size("gx"))), len(moves_of(lax.axis_size("gy")))
    n_faces = x_moves + y_moves
    f32 = jnp.float32
    shape_of = jax.ShapeDtypeStruct
    face_shapes = [shape_of((second, local_modes), f32)] * x_moves + [
        shape_of((first, local_modes), f32)
    ] * y_moves
    parts = 2 if cells % 32 == 0 else 1
    packed_shapes = [shape_of((cells, local_modes), jnp.bfloat16)]
    packed_shapes += [shape_of((cells // parts, local_modes), jnp.bfloat16)] * parts
    vector_shape = shape_of((cells, local_modes), f32)
    near = [place for place in (0, 1) if place < count]
    final = [place for place in range(3, count) if place % 2 == 1]
    middle = [place for place in range(2, count) if place not in final]

    start = right_side.reshape(cells, local_modes)

    def pack(ins, outs, scratch):
        store_packed(outs, slice(None), ins[0][...])

    packed = call("pack", pack, [in_vmem([start])], packed_shapes, flops=8 * 10**9)

    def prepare(ins, outs, scratch):
        faces, (open_ref,) = outs[:n_faces], outs[n_faces:]
        prepare_kernel(sizes, *ins, faces[:x_moves], faces[x_moves:], open_ref)

    *faces, open_cells = call(
        "prepare",
        prepare,
        [in_vmem([start, wall_mask])],
        face_shapes + [shape_of((cells, block), f32)],
        flops=1 * 10**9,
    )
    columns = col_block.T

    turned_shape = shape_of((local_blocks, len(final) * per_owner * block, block), blocks.dtype)
    work = 2 * cells * local_modes * per_owner * block
    vectors = [start]
    for section in range(KRYLOV):
        sources = {0: packed[0]}
        held = gather_far(packed[0])
        neighbour = [exchange(part, 1) for part in packed[1:]] if count > 1 else []
        y_in, x_in = move_faces({"gx": faces[:x_moves], "gy": faces[x_moves:]})

        last = section == KRYLOV - 1

        def near_step(cols, sources, rest, params, known, outs, scratch, section=section, last=last):
            sources = [sources[:1], sources[1:]][: len(near)]
            blocks_ref, current_ref, open_ref = rest
            near_kernel(
                sizes, per_owner, near, cols[0], sources, blocks_ref, current_ref, params,
                open_ref, outs[0], scratch[0] if section == 0 else None,
            )
            if section == 0:
                turn_blocks(per_owner, final, blocks_ref, outs[1])
            if last:
                early_products(sizes, known, outs[1])

        partial, *early = call(
            "near_%d" % section,
            near_step,
            [
                in_vmem([columns]),
                in_vmem([packed[0], *neighbour]),
                in_vmem([blocks, vectors[-1], open_cells]),
                in_vmem([relax_rate, drift_speed, upwind_sign]),
                in_vmem(vectors if last else []),
            ],
            [vector_shape] + [turned_shape] * (section == 0) + [shape_of((16, block), f32)] * last,
            [pltpu.VMEM((cells, local_modes), jnp.bfloat16)] * (section == 0),
            flops=work * len(near),
        )

        if section == 0:
            turned, *early = early
        held = dict(zip(held, hand_on(list(held.values()), [partial, *x_in, *y_in])))
        for place, array in held.items():
            sources[place] = array
            sources[place ^ 1] = exchange(array, 1)

        def middle_step(cols, sources, rest, x_in, y_in, outs, scratch):
            middle_kernel(
                sizes, per_owner, middle, cols[0], [[ref] for ref in sources], *rest, x_in, y_in, outs[0]
            )

        (partial,) = call(
            "middle_%d" % section,
            middle_step,
            [
                in_vmem([columns]),
                in_vmem([sources[place] for place in middle]),
                in_vmem([blocks, partial, drift_speed, upwind_sign]),
                in_vmem(x_in),
                in_vmem(y_in),
            ],
            [vector_shape],
            flops=work * len(middle),
        )

        def last_step(cols, sources, rest, earlier, early, outs, scratch, last=last):
            blocks_ref, partial_ref, open_ref = rest
            named = Outs()
            if last:
                named.gram = outs[0]
            else:
                named.x, named.y = outs[:x_moves], outs[x_moves:n_faces]
                *named.packed, named.value = outs[n_faces:]
            last_kernel(
                sizes, per_owner, final, cols[0], [[ref] for ref in sources], blocks_ref, partial_ref,
                earlier, open_ref, named, early[0] if last else None,
            )

        if last:
            shapes = [shape_of((devices, 1, block), f32)]
        else:
            shapes = face_shapes + packed_shapes + [vector_shape]
        results = call(
            "last_%d" % section,
            last_step,
            [
                in_vmem([columns]),
                in_vmem([sources[place] for place in final]),
                in_vmem([turned, partial, open_cells]),
                in_vmem(vectors if last else []),
                in_vmem(early),
            ],
            shapes,
            flops=work * len(final),
        )
        if last:
            (gram,) = results
        else:
            faces, packed, value = results[:n_faces], results[n_faces:-1], results[-1]
            vectors.append(value)

    gram = lax.all_to_all(gram, AXES, 0, 0)

    def finish(ins, outs, scratch):
        finish_kernel(*ins, *outs)

    solution, hessenberg = call(
        "finish",
        finish,
        [in_vmem([gram, *vectors])],
        [vector_shape, shape_of((KRYLOV + 1, KRYLOV), f32)],
    )
    return solution.reshape(first, second, local_modes), hessenberg


def solution(mesh):
    return jax.shard_map(
        per_device,
        mesh=mesh,
        in_specs=(
            P("gx", "gy", "mode"),
            P("mode", None),
            P("mode", None, None, None),
            P("mode"),
            P(None, "mode"),
            P(None, "mode"),
            P("gx", "gy"),
        ),
        out_specs=(P("gx", "gy", "mode"), P()),
        check_vma=False,
    )
```

```python
import functools

import jax
import jax.numpy as jnp
from jax import lax
from jax.experimental import pallas as pl
from jax.experimental.pallas import tpu as pltpu
from jax.sharding import PartitionSpec as P

KRYLOV = 3
SHIFT = 4.05
AXES = ("mode", "gx", "gy")

epsilon = 1e-12


def moves_of(count):
    moves = []
    for first in (0, 1)[: count - 1]:
        partner = list(range(count))
        for low in range(first, count - 1, 2):
            partner[low], partner[low + 1] = low + 1, low
        moves.append(partner)
    return moves


def move_faces(faces):
    received = []
    shards = lax.axis_size("mode")
    for axis in ("gy", "gx"):
        count = lax.axis_size(axis)
        arrived = []
        for face, partner in zip(faces[axis], moves_of(count)):
            pairs = []
            for shard in range(shards):
                for at in range(count):
                    alone = partner[at] == at
                    other = (shard ^ 1 if alone and shards > 1 else shard) * count + partner[at]
                    pairs.append((shard * count + at, other))
            arrived.append(lax.ppermute(face, ("mode", axis), pairs))
        received.append(arrived)
    return received


def exchange(array, bit):
    count = lax.axis_size("mode")
    return lax.ppermute(array, "mode", [(i, i ^ bit) for i in range(count)])


def gather_far(packed):
    held = {0: packed}
    bit = lax.axis_size("mode") // 2
    while bit > 1:
        for key in list(held):
            held[key ^ bit] = exchange(held[key], bit)
        bit //= 2
    del held[0]
    return held


def store_packed(refs, lanes, value):
    refs[0][:, lanes] = value.astype(jnp.bfloat16)
    at = 0
    for ref in refs[1:]:
        rows = ref.shape[0]
        ref[:, lanes] = value[at : at + rows].astype(jnp.bfloat16)
        at += rows


def hand_on(arrays, after):
    count = len(arrays)
    if not count:
        return []
    return pl.pallas_call(
        lambda *refs: None,
        out_shape=[jax.ShapeDtypeStruct(array.shape, array.dtype) for array in arrays],
        in_specs=[ANY] * (count + len(after)),
        out_specs=[ANY] * count,
        input_output_aliases={at: at for at in range(count)},
        compiler_params=pltpu.CompilerParams(vmem_limit_bytes=SCOPED),
        name="hand_on",
    )(*arrays, *after)


def store_faces(refs, axis, lanes, low, high):
    even = lax.rem(lax.axis_index(axis), 2) == 0
    for ref, take_high in zip(refs, (even, jnp.logical_not(even))):
        ref[:, lanes] = jnp.where(take_high, high, low)


def write_faces(masked, lanes, first, second, x_refs, y_refs):
    store_faces(x_refs, "gx", lanes, masked[0], masked[first - 1])
    store_faces(y_refs, "gy", lanes, masked[:, 0, :], masked[:, second - 1, :])


def halos(refs, axis, lanes, shape):
    zero = jnp.zeros(shape, jnp.float32)
    if not refs:
        return zero, zero
    at = lax.axis_index(axis)
    odd = lax.rem(at, 2) == 1
    one, two = refs[0][:, lanes], refs[-1][:, lanes]
    low, high = jnp.where(odd, one, two), jnp.where(odd, two, one)
    return jnp.where(at == 0, zero, low), jnp.where(at == lax.axis_size(axis) - 1, zero, high)


def prepare_kernel(sizes, rhs_ref, wall_ref, x_refs, y_refs, open_ref):
    first, second, local_blocks, block = sizes
    wall = wall_ref[...].astype(jnp.float32)
    eye = (
        lax.broadcasted_iota(jnp.int32, (second, second), 0)
        == lax.broadcasted_iota(jnp.int32, (second, second), 1)
    ).astype(jnp.float32)
    for row in range(first):
        column = jnp.sum(eye * (1.0 - wall[row : row + 1, :]), axis=1, keepdims=True)
        open_ref[row * second : (row + 1) * second, :] = jnp.broadcast_to(column, (second, block))
    for b in range(local_blocks):
        lanes = slice(b * block, (b + 1) * block)
        masked = (rhs_ref[:, lanes] * open_ref[...]).reshape(first, second, block)
        write_faces(masked, lanes, first, second, x_refs, y_refs)


def scatter(sizes, per_owner, b, places, cols_ref, sources, blocks_ref, turned=False):
    first, second, local_blocks, block = sizes
    mine = lax.axis_index("mode")
    picks, weights = [], []
    for place, source in zip(places, sources):
        owner = mine ^ place
        for p in range(per_owner):
            slot = owner * per_owner + p
            column = cols_ref[slot, b] - owner * local_blocks
            lanes = pl.ds(pl.multiple_of(column * block, block), block)
            picks.append(jnp.concatenate([part[:, lanes] for part in source], axis=0))
            if not turned:
                weights.append(blocks_ref[b, slot])
    picks = jnp.concatenate(picks, axis=1)
    if turned:
        return jnp.dot(picks, blocks_ref[b], preferred_element_type=jnp.float32)
    return lax.dot_general(
        picks,
        jnp.concatenate(weights, axis=1),
        (((1,), (1,)), ((), ())),
        preferred_element_type=jnp.float32,
    )


def turn_blocks(per_owner, places, blocks_ref, turned_ref):
    block = blocks_ref.shape[2]
    mine = lax.axis_index("mode")
    for b in range(blocks_ref.shape[0]):
        at = 0
        for place in places:
            for p in range(per_owner):
                turned_ref[b, at : at + block, :] = blocks_ref[b, (mine ^ place) * per_owner + p].T
                at += block


def add_product(sums, key, left, right):
    cells, block = left.shape
    term = jnp.sum((left * right).reshape(cells // 8, 8, block), axis=0)
    sums[key] = sums[key] + term if key in sums else term


def lane_sum(value):
    return jnp.sum(jnp.sum(value, axis=0, keepdims=True), axis=1, keepdims=True)


def early_products(sizes, vectors, early_ref):
    first, second, local_blocks, block = sizes
    sums = {}
    for b in range(local_blocks):
        lanes = slice(b * block, (b + 1) * block)
        values = [ref[:, lanes] for ref in vectors]
        for i in range(len(values)):
            for j in range(i, len(values)):
                add_product(sums, (i, j), values[i], values[j])
    at = 0
    for i in range(len(vectors) + 1):
        for j in range(i, len(vectors) + 1):
            if j < len(vectors):
                early_ref[at : at + 1, :] = jnp.broadcast_to(lane_sum(sums[i, j]), (1, block))
            at += 1


def split_speeds(speed_ref, sign_ref, lanes):
    parts = []
    for axis in range(2):
        speed, sign = speed_ref[axis : axis + 1, lanes], sign_ref[axis : axis + 1, lanes]
        parts += [jnp.where(sign == 1, speed, 0.0), jnp.where(sign == 1, 0.0, speed)]
    return parts


def near_kernel(sizes, per_owner, places, cols_ref, sources, blocks_ref, current_ref, params, open_ref, out_ref, finer_ref=None):
    first, second, local_blocks, block = sizes
    cells = first * second
    open_cells = open_ref[...]
    row_at = lax.broadcasted_iota(jnp.int32, (first, second, block), 1)
    zero = jnp.zeros((1, second, block), jnp.float32)
    if finer_ref is not None:
        for b in range(local_blocks):
            lanes = slice(b * block, (b + 1) * block)
            rounded = sources[0][0][:, lanes].astype(jnp.float32)
            finer_ref[:, lanes] = (current_ref[:, lanes] - rounded).astype(jnp.bfloat16)
        places, sources = places + [0], sources + [[finer_ref]]
    for b in range(local_blocks):
        lanes = slice(b * block, (b + 1) * block)
        scattered = scatter(sizes, per_owner, b, places, cols_ref, sources, blocks_ref)
        current = current_ref[:, lanes]
        masked = (current * open_cells).reshape(first, second, block)
        relax_ref, speed_ref, sign_ref = params
        west, east, south, north = split_speeds(speed_ref, sign_ref, lanes)
        diagonal = relax_ref[lanes].reshape(1, block) + (west + east) + (south + north) - SHIFT
        from_west = jnp.concatenate([zero, masked[:-1]], axis=0)
        from_east = jnp.concatenate([masked[1:], zero], axis=0)
        from_south = jnp.where(row_at == 0, 0.0, pltpu.roll(masked, 1, axis=1))
        from_north = jnp.where(row_at == second - 1, 0.0, pltpu.roll(masked, second - 1, axis=1))
        drift = (
            west.reshape(1, 1, block) * from_west
            + east.reshape(1, 1, block) * from_east
            + south.reshape(1, 1, block) * from_south
            + north.reshape(1, 1, block) * from_north
        ).reshape(cells, block)
        out_ref[:, lanes] = diagonal * current - drift - scattered


def middle_kernel(sizes, per_owner, places, cols_ref, sources, blocks_ref, partial_ref, speed_ref, sign_ref, x_in, y_in, out_ref):
    first, second, local_blocks, block = sizes
    cells = first * second
    row_at = lax.broadcasted_iota(jnp.int32, (first, second, block), 1)
    for b in range(local_blocks):
        lanes = slice(b * block, (b + 1) * block)
        value = partial_ref[:, lanes]
        if places:
            value = value - scatter(sizes, per_owner, b, places, cols_ref, sources, blocks_ref)
        west, east, south, north = split_speeds(speed_ref, sign_ref, lanes)
        west_in, east_in = halos(x_in, "gx", lanes, (second, block))
        south_in, north_in = halos(y_in, "gy", lanes, (first, block))
        value = value.reshape(first, second, block)
        value = value - jnp.where(
            row_at == 0,
            (south * south_in)[:, None, :],
            jnp.where(row_at == second - 1, (north * north_in)[:, None, :], 0.0),
        )
        value = jnp.concatenate(
            [value[:1] - (west * west_in)[None], value[1:-1], value[-1:] - (east * east_in)[None]],
            axis=0,
        )
        out_ref[:, lanes] = value.reshape(cells, block)


def last_kernel(sizes, per_owner, places, cols_ref, sources, blocks_ref, partial_ref, earlier, open_ref, outs, early_ref=None):
    first, second, local_blocks, block = sizes
    cells = first * second
    sums = {}
    for b in range(local_blocks):
        lanes = slice(b * block, (b + 1) * block)
        scattered = scatter(sizes, per_owner, b, places, cols_ref, sources, blocks_ref, True)
        result = partial_ref[:, lanes] - scattered
        if outs.gram is None:
            outs.value[:, lanes] = result
            store_packed(outs.packed, lanes, result)
            write_faces(
                (result * open_ref[...]).reshape(first, second, block),
                lanes, first, second, outs.x, outs.y,
            )
        else:
            vectors = [ref[:, lanes] for ref in earlier] + [result]
            for i, vector in enumerate(vectors):
                add_product(sums, (i, len(earlier)), vector, result)
    if outs.gram is not None:
        devices = outs.gram.shape[0]
        lane = lax.broadcasted_iota(jnp.int32, (1, block), 1)
        row = jnp.zeros((1, block), jnp.float32)
        size = len(earlier) + 1
        at = 0
        for i in range(size):
            for j in range(i, size):
                if j < size - 1:
                    total = early_ref[at : at + 1, :]
                else:
                    total = lane_sum(sums[i, j])
                row = jnp.where(lane == at, total, row)
                at += 1
        outs.gram[...] = jnp.broadcast_to(row[None], (devices, 1, block))


class Outs:
    value = gram = None
    x = y = packed = ()


def least_squares(hessenberg, initial):
    upper = [list(row) for row in hessenberg]
    target = [initial] + [jnp.zeros_like(initial) for row_index in range(KRYLOV)]
    cosines = []
    sines = []
    for col_index in range(KRYLOV):
        for row_index in range(col_index):
            first = upper[row_index][col_index]
            second = upper[row_index + 1][col_index]
            upper[row_index][col_index] = cosines[row_index] * first + sines[row_index] * second
            upper[row_index + 1][col_index] = cosines[row_index] * second - sines[row_index] * first
        first = upper[col_index][col_index]
        second = upper[col_index + 1][col_index]
        radius = jnp.sqrt(first * first + second * second)
        cosine = first / radius
        sine_value = second / radius
        upper[col_index][col_index] = radius
        target[col_index + 1] = -sine_value * target[col_index]
        target[col_index] = cosine * target[col_index]
        cosines.append(cosine)
        sines.append(sine_value)
    combo = [None] * KRYLOV
    for row_index in reversed(range(KRYLOV)):
        running = target[row_index]
        for col_index in range(row_index + 1, KRYLOV):
            running = running - upper[row_index][col_index] * combo[col_index]
        combo[row_index] = running / upper[row_index][row_index]
    return combo


def arnoldi(gram):
    size = KRYLOV + 1

    def inner(left, right):
        total = None
        for i in range(size):
            for j in range(size):
                if left[i] is None or right[j] is None:
                    continue
                term = left[i] * gram[min(i, j)][max(i, j)] * right[j]
                total = term if total is None else total + term
        return total

    initial = jnp.sqrt(gram[0][0] + epsilon)
    basis = [[1.0 / initial] + [None] * KRYLOV]
    zero = jnp.zeros_like(initial)
    hessenberg = [[zero] * KRYLOV for row_index in range(size)]
    for section in range(KRYLOV):
        vector = basis[section]
        image = [None] * size
        for k in range(section + 2):
            parts = []
            if k > 0 and vector[k - 1] is not None:
                parts.append(vector[k - 1])
            if vector[k] is not None:
                parts.append(SHIFT * vector[k])
            image[k] = sum(parts[1:], parts[0])
        rest = list(image)
        for earlier in range(section + 1):
            coefficient = inner(basis[earlier], image)
            hessenberg[earlier][section] = coefficient
            for k in range(earlier + 1):
                rest[k] = rest[k] - coefficient * basis[earlier][k]
        length = jnp.sqrt(jnp.maximum(inner(rest, rest), 0.0) + epsilon)
        hessenberg[section + 1][section] = length
        basis.append([None if part is None else part / length for part in rest])
    combo = least_squares(hessenberg, initial)
    weights = []
    for k in range(KRYLOV):
        total = zero
        for j in range(k, KRYLOV):
            total = total + combo[j] * basis[j][k]
        weights.append(total)
    return hessenberg, weights


def finish_kernel(gram_ref, *refs):
    vectors, (solution_ref, hessenberg_ref) = refs[:KRYLOV], refs[KRYLOV:]
    block = gram_ref.shape[2]
    total = jnp.sum(gram_ref[...], axis=0)
    lane = lax.broadcasted_iota(jnp.int32, (1, block), 1)
    gram = [[None] * (KRYLOV + 1) for i in range(KRYLOV + 1)]
    at = 0
    for i in range(KRYLOV + 1):
        for j in range(i, KRYLOV + 1):
            entry = jnp.sum(jnp.where(lane == at, total, 0.0), axis=1, keepdims=True)
            gram[i][j] = jnp.broadcast_to(entry, (1, block))
            at += 1
    hessenberg, weights = arnoldi(gram)
    rows = lax.broadcasted_iota(jnp.int32, (KRYLOV + 1, KRYLOV), 0)
    cols = lax.broadcasted_iota(jnp.int32, (KRYLOV + 1, KRYLOV), 1)
    table = jnp.zeros((KRYLOV + 1, KRYLOV), jnp.float32)
    for i in range(KRYLOV + 1):
        for j in range(KRYLOV):
            table = jnp.where((rows == i) & (cols == j), hessenberg[i][j][:, :KRYLOV], table)
    hessenberg_ref[...] = table
    for b in range(solution_ref.shape[1] // block):
        lanes = slice(b * block, (b + 1) * block)
        solution_ref[:, lanes] = sum(
            weight * ref[:, lanes] for weight, ref in zip(weights, vectors)
        )


VMEM = pl.BlockSpec(memory_space=pltpu.VMEM)
ANY = pl.BlockSpec(memory_space=pl.ANY)
SCOPED = 16 * 1024 * 1024


def call(name, kernel, groups, shapes, scratch=(), flops=0):
    flat = [pair for group in groups for pair in group]

    def body(*refs):
        refs = list(refs)
        lists = []
        for group in groups:
            lists.append(refs[: len(group)])
            del refs[: len(group)]
        kernel(*lists, refs[: len(shapes)], refs[len(shapes) :])

    size = sum(operand.size * operand.dtype.itemsize for spec, operand in flat)
    size += sum(shape.size * shape.dtype.itemsize for shape in shapes)
    return pl.pallas_call(
        body,
        out_shape=list(shapes),
        in_specs=[spec for spec, operand in flat],
        out_specs=[VMEM] * len(shapes),
        scratch_shapes=list(scratch),
        compiler_params=pltpu.CompilerParams(vmem_limit_bytes=SCOPED),
        cost_estimate=pl.CostEstimate(flops=flops, bytes_accessed=size, transcendentals=0),
        name=name,
    )(*[operand for spec, operand in flat])


def in_vmem(operands):
    return [(VMEM, operand) for operand in operands]


def per_device(right_side, col_block, blocks, relax_rate, drift_speed, upwind_sign, wall_mask):
    first, second, local_modes = right_side.shape
    local_blocks, slots, block = blocks.shape[:3]
    cells = first * second
    count = lax.axis_size("mode")
    devices = count * lax.axis_size("gx") * lax.axis_size("gy")
    per_owner = slots // count
    sizes = (first, second, local_blocks, block)
    x_moves, y_moves = len(moves_of(lax.axis_size("gx"))), len(moves_of(lax.axis_size("gy")))
    n_faces = x_moves + y_moves
    f32 = jnp.float32
    shape_of = jax.ShapeDtypeStruct
    face_shapes = [shape_of((second, local_modes), f32)] * x_moves + [
        shape_of((first, local_modes), f32)
    ] * y_moves
    parts = 2 if cells % 32 == 0 else 1
    packed_shapes = [shape_of((cells, local_modes), jnp.bfloat16)]
    packed_shapes += [shape_of((cells // parts, local_modes), jnp.bfloat16)] * parts
    vector_shape = shape_of((cells, local_modes), f32)
    near = [place for place in (0, 1) if place < count]
    final = [place for place in range(3, count) if place % 2 == 1]
    middle = [place for place in range(2, count) if place not in final]

    start = right_side.reshape(cells, local_modes)

    def pack(ins, outs, scratch):
        store_packed(outs, slice(None), ins[0][...])

    packed = call("pack", pack, [in_vmem([start])], packed_shapes, flops=8 * 10**9)

    def prepare(ins, outs, scratch):
        faces, (open_ref,) = outs[:n_faces], outs[n_faces:]
        prepare_kernel(sizes, *ins, faces[:x_moves], faces[x_moves:], open_ref)

    *faces, open_cells = call(
        "prepare",
        prepare,
        [in_vmem([start, wall_mask])],
        face_shapes + [shape_of((cells, block), f32)],
        flops=1 * 10**9,
    )
    columns = col_block.T

    turned_shape = shape_of((local_blocks, len(final) * per_owner * block, block), blocks.dtype)
    work = 2 * cells * local_modes * per_owner * block
    vectors = [start]
    for section in range(KRYLOV):
        sources = {0: packed[0]}
        held = gather_far(packed[0])
        neighbour = [exchange(part, 1) for part in packed[1:]] if count > 1 else []
        y_in, x_in = move_faces({"gx": faces[:x_moves], "gy": faces[x_moves:]})

        last = section == KRYLOV - 1

        def near_step(cols, sources, rest, params, known, outs, scratch, section=section, last=last):
            sources = [sources[:1], sources[1:]][: len(near)]
            blocks_ref, current_ref, open_ref = rest
            near_kernel(
                sizes, per_owner, near, cols[0], sources, blocks_ref, current_ref, params,
                open_ref, outs[0], scratch[0] if section == 0 else None,
            )
            if section == 0:
                turn_blocks(per_owner, final, blocks_ref, outs[1])
            if last:
                early_products(sizes, known, outs[1])

        partial, *early = call(
            "near_%d" % section,
            near_step,
            [
                in_vmem([columns]),
                in_vmem([packed[0], *neighbour]),
                in_vmem([blocks, vectors[-1], open_cells]),
                in_vmem([relax_rate, drift_speed, upwind_sign]),
                in_vmem(vectors if last else []),
            ],
            [vector_shape] + [turned_shape] * (section == 0) + [shape_of((16, block), f32)] * last,
            [pltpu.VMEM((cells, local_modes), jnp.bfloat16)] * (section == 0),
            flops=work * len(near),
        )

        if section == 0:
            turned, *early = early
        held = dict(zip(held, hand_on(list(held.values()), [partial, *x_in, *y_in])))
        for place, array in held.items():
            sources[place] = array
            sources[place ^ 1] = exchange(array, 1)

        def middle_step(cols, sources, rest, x_in, y_in, outs, scratch):
            middle_kernel(
                sizes, per_owner, middle, cols[0], [[ref] for ref in sources], *rest, x_in, y_in, outs[0]
            )

        (partial,) = call(
            "middle_%d" % section,
            middle_step,
            [
                in_vmem([columns]),
                in_vmem([sources[place] for place in middle]),
                in_vmem([blocks, partial, drift_speed, upwind_sign]),
                in_vmem(x_in),
                in_vmem(y_in),
            ],
            [vector_shape],
            flops=work * len(middle),
        )

        def last_step(cols, sources, rest, earlier, early, outs, scratch, last=last):
            blocks_ref, partial_ref, open_ref = rest
            named = Outs()
            if last:
                named.gram = outs[0]
            else:
                named.x, named.y = outs[:x_moves], outs[x_moves:n_faces]
                *named.packed, named.value = outs[n_faces:]
            last_kernel(
                sizes, per_owner, final, cols[0], [[ref] for ref in sources], blocks_ref, partial_ref,
                earlier, open_ref, named, early[0] if last else None,
            )

        if last:
            shapes = [shape_of((devices, 1, block), f32)]
        else:
            shapes = face_shapes + packed_shapes + [vector_shape]
        results = call(
            "last_%d" % section,
            last_step,
            [
                in_vmem([columns]),
                in_vmem([sources[place] for place in final]),
                in_vmem([turned, partial, open_cells]),
                in_vmem(vectors if last else []),
                in_vmem(early),
            ],
            shapes,
            flops=work * len(final),
        )
        if last:
            (gram,) = results
        else:
            faces, packed, value = results[:n_faces], results[n_faces:-1], results[-1]
            vectors.append(value)

    gram = lax.all_to_all(gram, AXES, 0, 0)

    def finish(ins, outs, scratch):
        finish_kernel(*ins, *outs)

    solution, hessenberg = call(
        "finish",
        finish,
        [in_vmem([gram, *vectors])],
        [vector_shape, shape_of((KRYLOV + 1, KRYLOV), f32)],
    )
    return solution.reshape(first, second, local_modes), hessenberg


def solution(mesh):
    return jax.shard_map(
        per_device,
        mesh=mesh,
        in_specs=(
            P("gx", "gy", "mode"),
            P("mode", None),
            P("mode", None, None, None),
            P("mode"),
            P(None, "mode"),
            P(None, "mode"),
            P("gx", "gy"),
        ),
        out_specs=(P("gx", "gy", "mode"), P()),
        check_vma=False,
    )
```

```python
import jax
import jax.numpy as jnp
from jax import lax
from jax.experimental import pallas as pl
from jax.experimental.pallas import tpu as pltpu
from jax.sharding import PartitionSpec as P

KRYLOV = 3
SHIFT = 4.05
AXES = ("mode", "gx", "gy")

epsilon = 1e-12


def moves_of(count):
    moves = []
    for first in (0, 1)[: count - 1]:
        partner = list(range(count))
        for low in range(first, count - 1, 2):
            partner[low], partner[low + 1] = low + 1, low
        moves.append(partner)
    return moves


def move_faces(faces):
    received = []
    shards = lax.axis_size("mode")
    for axis in ("gy", "gx"):
        count = lax.axis_size(axis)
        arrived = []
        for face, partner in zip(faces[axis], moves_of(count)):
            pairs = []
            for shard in range(shards):
                for at in range(count):
                    alone = partner[at] == at
                    other = (shard ^ 1 if alone and shards > 1 else shard) * count + partner[at]
                    pairs.append((shard * count + at, other))
            arrived.append(lax.ppermute(face, ("mode", axis), pairs))
        received.append(arrived)
    return received


def exchange(array, bit):
    count = lax.axis_size("mode")
    return lax.ppermute(array, "mode", [(i, i ^ bit) for i in range(count)])


def gather_far(packed):
    held = {0: packed}
    bit = lax.axis_size("mode") // 2
    while bit > 1:
        for key in list(held):
            held[key ^ bit] = exchange(held[key], bit)
        bit //= 2
    del held[0]
    return held


def spread_kernel(sizes, value_ref, open_ref, part_refs, x_refs, y_refs):
    first, second, local_blocks, block = sizes
    at = 0
    for ref in part_refs:
        rows = ref.shape[0]
        ref[...] = value_ref[at : at + rows, :].astype(jnp.bfloat16)
        at += rows
    for b in range(local_blocks):
        lanes = slice(b * block, (b + 1) * block)
        masked = (value_ref[:, lanes] * open_ref[...]).reshape(first, second, block)
        write_faces(masked, lanes, first, second, x_refs, y_refs)


def hand_on(arrays, after):
    count = len(arrays)
    if not count:
        return []
    return pl.pallas_call(
        lambda *refs: None,
        out_shape=[jax.ShapeDtypeStruct(array.shape, array.dtype) for array in arrays],
        in_specs=[ANY] * (count + len(after)),
        out_specs=[ANY] * count,
        input_output_aliases={at: at for at in range(count)},
        compiler_params=pltpu.CompilerParams(vmem_limit_bytes=SCOPED),
        name="hand_on",
    )(*arrays, *after)


def store_faces(refs, axis, lanes, low, high):
    even = lax.rem(lax.axis_index(axis), 2) == 0
    for ref, take_high in zip(refs, (even, jnp.logical_not(even))):
        ref[:, lanes] = jnp.where(take_high, high, low)


def write_faces(masked, lanes, first, second, x_refs, y_refs):
    store_faces(x_refs, "gx", lanes, masked[0], masked[first - 1])
    store_faces(y_refs, "gy", lanes, masked[:, 0, :], masked[:, second - 1, :])


def halos(refs, axis, lanes, shape):
    zero = jnp.zeros(shape, jnp.float32)
    if not refs:
        return zero, zero
    at = lax.axis_index(axis)
    odd = lax.rem(at, 2) == 1
    one, two = refs[0][:, lanes], refs[-1][:, lanes]
    low, high = jnp.where(odd, one, two), jnp.where(odd, two, one)
    return jnp.where(at == 0, zero, low), jnp.where(at == lax.axis_size(axis) - 1, zero, high)


def prepare_kernel(sizes, rhs_ref, wall_ref, part_refs, x_refs, y_refs, open_ref):
    first, second, local_blocks, block = sizes
    wall = wall_ref[...].astype(jnp.float32)
    eye = (
        lax.broadcasted_iota(jnp.int32, (second, second), 0)
        == lax.broadcasted_iota(jnp.int32, (second, second), 1)
    ).astype(jnp.float32)
    for row in range(first):
        column = jnp.sum(eye * (1.0 - wall[row : row + 1, :]), axis=1, keepdims=True)
        open_ref[row * second : (row + 1) * second, :] = jnp.broadcast_to(column, (second, block))
    spread_kernel(sizes, rhs_ref, open_ref, part_refs, x_refs, y_refs)


def scatter(sizes, per_owner, b, places, cols_ref, sources, blocks_ref, turned=False):
    first, second, local_blocks, block = sizes
    mine = lax.axis_index("mode")
    picks, weights = [], []
    for place, source in zip(places, sources):
        owner = mine ^ place
        for p in range(per_owner):
            slot = owner * per_owner + p
            column = cols_ref[slot, b] - owner * local_blocks
            lanes = pl.ds(pl.multiple_of(column * block, block), block)
            picks.append(jnp.concatenate([part[:, lanes] for part in source], axis=0))
            if not turned:
                weights.append(blocks_ref[b, slot])
    picks = jnp.concatenate(picks, axis=1)
    if turned:
        return jnp.dot(picks, blocks_ref[b], preferred_element_type=jnp.float32)
    return lax.dot_general(
        picks,
        jnp.concatenate(weights, axis=1),
        (((1,), (1,)), ((), ())),
        preferred_element_type=jnp.float32,
    )


def turn_blocks(per_owner, places, blocks_ref, turned_ref):
    block = blocks_ref.shape[2]
    mine = lax.axis_index("mode")
    for b in range(blocks_ref.shape[0]):
        at = 0
        for place in places:
            for p in range(per_owner):
                turned_ref[b, at : at + block, :] = blocks_ref[b, (mine ^ place) * per_owner + p].T
                at += block


def add_product(sums, key, left, right):
    cells, block = left.shape
    term = jnp.sum((left * right).reshape(cells // 8, 8, block), axis=0)
    sums[key] = sums[key] + term if key in sums else term


def lane_sum(value):
    return jnp.sum(jnp.sum(value, axis=0, keepdims=True), axis=1, keepdims=True)


def early_products(sizes, vectors, early_ref):
    first, second, local_blocks, block = sizes
    sums = {}
    for b in range(local_blocks):
        lanes = slice(b * block, (b + 1) * block)
        values = [ref[:, lanes] for ref in vectors]
        for i in range(len(values)):
            for j in range(i, len(values)):
                add_product(sums, (i, j), values[i], values[j])
    at = 0
    for i in range(len(vectors) + 1):
        for j in range(i, len(vectors) + 1):
            if j < len(vectors):
                early_ref[at : at + 1, :] = jnp.broadcast_to(lane_sum(sums[i, j]), (1, block))
            at += 1


def split_speeds(speed_ref, sign_ref, lanes):
    parts = []
    for axis in range(2):
        speed, sign = speed_ref[axis : axis + 1, lanes], sign_ref[axis : axis + 1, lanes]
        parts += [jnp.where(sign == 1, speed, 0.0), jnp.where(sign == 1, 0.0, speed)]
    return parts


def near_kernel(sizes, per_owner, places, cols_ref, sources, blocks_ref, current_ref, params, open_ref, out_ref, finer_ref=None):
    first, second, local_blocks, block = sizes
    cells = first * second
    open_cells = open_ref[...]
    row_at = lax.broadcasted_iota(jnp.int32, (first, second, block), 1)
    zero = jnp.zeros((1, second, block), jnp.float32)
    if finer_ref is not None:
        for b in range(local_blocks):
            lanes = slice(b * block, (b + 1) * block)
            rounded = sources[0][0][:, lanes].astype(jnp.float32)
            finer_ref[:, lanes] = (current_ref[:, lanes] - rounded).astype(jnp.bfloat16)
        places, sources = places + [0], sources + [[finer_ref]]
    for b in range(local_blocks):
        lanes = slice(b * block, (b + 1) * block)
        scattered = scatter(sizes, per_owner, b, places, cols_ref, sources, blocks_ref)
        current = current_ref[:, lanes]
        masked = (current * open_cells).reshape(first, second, block)
        relax_ref, speed_ref, sign_ref = params
        west, east, south, north = split_speeds(speed_ref, sign_ref, lanes)
        diagonal = relax_ref[lanes].reshape(1, block) + (west + east) + (south + north) - SHIFT
        from_west = jnp.concatenate([zero, masked[:-1]], axis=0)
        from_east = jnp.concatenate([masked[1:], zero], axis=0)
        from_south = jnp.where(row_at == 0, 0.0, pltpu.roll(masked, 1, axis=1))
        from_north = jnp.where(row_at == second - 1, 0.0, pltpu.roll(masked, second - 1, axis=1))
        drift = (
            west.reshape(1, 1, block) * from_west
            + east.reshape(1, 1, block) * from_east
            + south.reshape(1, 1, block) * from_south
            + north.reshape(1, 1, block) * from_north
        ).reshape(cells, block)
        out_ref[:, lanes] = diagonal * current - drift - scattered


def middle_kernel(sizes, per_owner, places, cols_ref, sources, blocks_ref, partial_ref, speed_ref, sign_ref, x_in, y_in, out_ref):
    first, second, local_blocks, block = sizes
    cells = first * second
    row_at = lax.broadcasted_iota(jnp.int32, (first, second, block), 1)
    for b in range(local_blocks):
        lanes = slice(b * block, (b + 1) * block)
        value = partial_ref[:, lanes]
        if places:
            value = value - scatter(sizes, per_owner, b, places, cols_ref, sources, blocks_ref)
        west, east, south, north = split_speeds(speed_ref, sign_ref, lanes)
        west_in, east_in = halos(x_in, "gx", lanes, (second, block))
        south_in, north_in = halos(y_in, "gy", lanes, (first, block))
        value = value.reshape(first, second, block)
        value = value - jnp.where(
            row_at == 0,
            (south * south_in)[:, None, :],
            jnp.where(row_at == second - 1, (north * north_in)[:, None, :], 0.0),
        )
        value = jnp.concatenate(
            [value[:1] - (west * west_in)[None], value[1:-1], value[-1:] - (east * east_in)[None]],
            axis=0,
        )
        out_ref[:, lanes] = value.reshape(cells, block)


def last_kernel(sizes, per_owner, places, cols_ref, sources, blocks_ref, partial_ref, earlier, outs, early_ref=None):
    first, second, local_blocks, block = sizes
    cells = first * second
    sums = {}
    for b in range(local_blocks):
        lanes = slice(b * block, (b + 1) * block)
        scattered = scatter(sizes, per_owner, b, places, cols_ref, sources, blocks_ref, True)
        result = partial_ref[:, lanes] - scattered
        if outs.gram is None:
            outs.value[:, lanes] = result
            outs.packed[:, lanes] = result.astype(jnp.bfloat16)
        else:
            vectors = [ref[:, lanes] for ref in earlier] + [result]
            for i, vector in enumerate(vectors):
                add_product(sums, (i, len(earlier)), vector, result)
    if outs.gram is not None:
        devices = outs.gram.shape[0]
        lane = lax.broadcasted_iota(jnp.int32, (1, block), 1)
        row = jnp.zeros((1, block), jnp.float32)
        size = len(earlier) + 1
        at = 0
        for i in range(size):
            for j in range(i, size):
                if j < size - 1:
                    total = early_ref[at : at + 1, :]
                else:
                    total = lane_sum(sums[i, j])
                row = jnp.where(lane == at, total, row)
                at += 1
        outs.gram[...] = jnp.broadcast_to(row[None], (devices, 1, block))


class Outs:
    value = packed = gram = None


def least_squares(hessenberg, initial):
    upper = [list(row) for row in hessenberg]
    target = [initial] + [jnp.zeros_like(initial) for row_index in range(KRYLOV)]
    cosines = []
    sines = []
    for col_index in range(KRYLOV):
        for row_index in range(col_index):
            first = upper[row_index][col_index]
            second = upper[row_index + 1][col_index]
            upper[row_index][col_index] = cosines[row_index] * first + sines[row_index] * second
            upper[row_index + 1][col_index] = cosines[row_index] * second - sines[row_index] * first
        first = upper[col_index][col_index]
        second = upper[col_index + 1][col_index]
        radius = jnp.sqrt(first * first + second * second)
        cosine = first / radius
        sine_value = second / radius
        upper[col_index][col_index] = radius
        target[col_index + 1] = -sine_value * target[col_index]
        target[col_index] = cosine * target[col_index]
        cosines.append(cosine)
        sines.append(sine_value)
    combo = [None] * KRYLOV
    for row_index in reversed(range(KRYLOV)):
        running = target[row_index]
        for col_index in range(row_index + 1, KRYLOV):
            running = running - upper[row_index][col_index] * combo[col_index]
        combo[row_index] = running / upper[row_index][row_index]
    return combo


def arnoldi(gram):
    size = KRYLOV + 1

    def dot(left, right):
        terms = [a * b for a, b in zip(left, right) if a is not None and b is not None]
        while len(terms) > 1:
            terms = [sum(terms[at + 1 : at + 2], terms[at]) for at in range(0, len(terms), 2)]
        return terms[0]

    def times_gram(vector):
        return [dot([gram[min(i, j)][max(i, j)] for j in range(size)], vector) for i in range(size)]

    initial = jnp.sqrt(gram[0][0] + epsilon)
    basis = [[1.0 / initial] + [None] * KRYLOV]
    zero = jnp.zeros_like(initial)
    hessenberg = [[zero] * KRYLOV for row_index in range(size)]
    for section in range(KRYLOV):
        vector = basis[section]
        image = [None] * size
        for k in range(section + 2):
            parts = []
            if k > 0 and vector[k - 1] is not None:
                parts.append(vector[k - 1])
            if vector[k] is not None:
                parts.append(SHIFT * vector[k])
            image[k] = sum(parts[1:], parts[0])
        rest = list(image)
        products = times_gram(image)
        for earlier in range(section + 1):
            coefficient = dot(basis[earlier], products)
            hessenberg[earlier][section] = coefficient
            for k in range(earlier + 1):
                rest[k] = rest[k] - coefficient * basis[earlier][k]
        length = jnp.sqrt(jnp.maximum(dot(rest, times_gram(rest)), 0.0) + epsilon)
        hessenberg[section + 1][section] = length
        basis.append([None if part is None else part / length for part in rest])
    combo = least_squares(hessenberg, initial)
    weights = []
    for k in range(KRYLOV):
        total = zero
        for j in range(k, KRYLOV):
            total = total + combo[j] * basis[j][k]
        weights.append(total)
    return hessenberg, weights


def finish_kernel(gram_ref, *refs):
    vectors, (solution_ref, hessenberg_ref) = refs[:KRYLOV], refs[KRYLOV:]
    block = gram_ref.shape[2]
    total = jnp.sum(gram_ref[...], axis=0)
    lane = lax.broadcasted_iota(jnp.int32, (1, block), 1)
    gram = [[None] * (KRYLOV + 1) for i in range(KRYLOV + 1)]
    at = 0
    for i in range(KRYLOV + 1):
        for j in range(i, KRYLOV + 1):
            entry = jnp.sum(jnp.where(lane == at, total, 0.0), axis=1, keepdims=True)
            gram[i][j] = jnp.broadcast_to(entry, (1, block))
            at += 1
    hessenberg, weights = arnoldi(gram)
    rows = lax.broadcasted_iota(jnp.int32, (KRYLOV + 1, KRYLOV), 0)
    cols = lax.broadcasted_iota(jnp.int32, (KRYLOV + 1, KRYLOV), 1)
    table = jnp.zeros((KRYLOV + 1, KRYLOV), jnp.float32)
    for i in range(KRYLOV + 1):
        for j in range(KRYLOV):
            table = jnp.where((rows == i) & (cols == j), hessenberg[i][j][:, :KRYLOV], table)
    hessenberg_ref[...] = table
    for b in range(solution_ref.shape[1] // block):
        lanes = slice(b * block, (b + 1) * block)
        solution_ref[:, lanes] = sum(
            weight * ref[:, lanes] for weight, ref in zip(weights, vectors)
        )


VMEM = pl.BlockSpec(memory_space=pltpu.VMEM)
ANY = pl.BlockSpec(memory_space=pl.ANY)
SCOPED = 16 * 1024 * 1024


def call(name, kernel, groups, shapes, scratch=(), flops=0):
    flat = [pair for group in groups for pair in group]

    def body(*refs):
        refs = list(refs)
        lists = []
        for group in groups:
            lists.append(refs[: len(group)])
            del refs[: len(group)]
        kernel(*lists, refs[: len(shapes)], refs[len(shapes) :])

    size = sum(operand.size * operand.dtype.itemsize for spec, operand in flat)
    size += sum(shape.size * shape.dtype.itemsize for shape in shapes)
    return pl.pallas_call(
        body,
        out_shape=list(shapes),
        in_specs=[spec for spec, operand in flat],
        out_specs=[VMEM] * len(shapes),
        scratch_shapes=list(scratch),
        compiler_params=pltpu.CompilerParams(vmem_limit_bytes=SCOPED),
        cost_estimate=pl.CostEstimate(flops=flops, bytes_accessed=size, transcendentals=0),
        name=name,
    )(*[operand for spec, operand in flat])


def in_vmem(operands):
    return [(VMEM, operand) for operand in operands]


def per_device(right_side, col_block, blocks, relax_rate, drift_speed, upwind_sign, wall_mask):
    first, second, local_modes = right_side.shape
    local_blocks, slots, block = blocks.shape[:3]
    cells = first * second
    count = lax.axis_size("mode")
    devices = count * lax.axis_size("gx") * lax.axis_size("gy")
    per_owner = slots // count
    sizes = (first, second, local_blocks, block)
    x_moves, y_moves = len(moves_of(lax.axis_size("gx"))), len(moves_of(lax.axis_size("gy")))
    n_faces = x_moves + y_moves
    f32 = jnp.float32
    shape_of = jax.ShapeDtypeStruct
    face_shapes = [shape_of((second, local_modes), f32)] * x_moves + [
        shape_of((first, local_modes), f32)
    ] * y_moves
    parts = 2 if cells % 32 == 0 else 1
    packed_shape = shape_of((cells, local_modes), jnp.bfloat16)
    spread_shapes = [shape_of((cells // parts, local_modes), jnp.bfloat16)] * parts + face_shapes
    vector_shape = shape_of((cells, local_modes), f32)
    near = [place for place in (0, 1) if place < count]
    final = [place for place in range(3, count) if place % 2 == 1]
    middle = [place for place in range(2, count) if place not in final]

    start = right_side.reshape(cells, local_modes)

    def pack(ins, outs, scratch):
        outs[0][...] = ins[0][...].astype(jnp.bfloat16)

    (packed,) = call("pack", pack, [in_vmem([start])], [packed_shape], flops=8 * 10**9)

    def split(outs):
        faces = outs[parts:]
        return outs[:parts], faces[:x_moves], faces[x_moves:n_faces]

    def prepare(ins, outs, scratch):
        prepare_kernel(sizes, *ins, *split(outs), outs[-1])

    *spread, open_cells = call(
        "prepare",
        prepare,
        [in_vmem([start, wall_mask])],
        spread_shapes + [shape_of((cells, block), f32)],
        flops=1 * 10**9,
    )
    columns = col_block.T

    turned_shape = shape_of((local_blocks, len(final) * per_owner * block, block), blocks.dtype)
    work = 2 * cells * local_modes * per_owner * block
    vectors = [start]
    for section in range(KRYLOV):
        sources = {0: packed}
        held = gather_far(packed)
        halves, x_faces, y_faces = split(spread)
        neighbour = [exchange(part, 1) for part in halves] if count > 1 else []
        y_in, x_in = move_faces({"gx": x_faces, "gy": y_faces})

        last = section == KRYLOV - 1

        def near_step(cols, sources, rest, params, known, outs, scratch, section=section, last=last):
            sources = [sources[:1], sources[1:]][: len(near)]
            blocks_ref, current_ref, open_ref = rest
            near_kernel(
                sizes, per_owner, near, cols[0], sources, blocks_ref, current_ref, params,
                open_ref, outs[0], scratch[0] if section == 0 else None,
            )
            if section == 0:
                turn_blocks(per_owner, final, blocks_ref, outs[1])
            if last:
                early_products(sizes, known, outs[1])

        partial, *early = call(
            "near_%d" % section,
            near_step,
            [
                in_vmem([columns]),
                in_vmem([packed, *neighbour]),
                in_vmem([blocks, vectors[-1], open_cells]),
                in_vmem([relax_rate, drift_speed, upwind_sign]),
                in_vmem(vectors if last else []),
            ],
            [vector_shape] + [turned_shape] * (section == 0) + [shape_of((16, block), f32)] * last,
            [pltpu.VMEM((cells, local_modes), jnp.bfloat16)] * (section == 0),
            flops=work * len(near),
        )

        if section == 0:
            turned, *early = early
        held = dict(zip(held, hand_on(list(held.values()), [partial, *x_in, *y_in])))
        for place, array in held.items():
            sources[place] = array
            sources[place ^ 1] = exchange(array, 1)

        def middle_step(cols, sources, rest, x_in, y_in, outs, scratch):
            middle_kernel(
                sizes, per_owner, middle, cols[0], [[ref] for ref in sources], *rest, x_in, y_in, outs[0]
            )

        (partial,) = call(
            "middle_%d" % section,
            middle_step,
            [
                in_vmem([columns]),
                in_vmem([sources[place] for place in middle]),
                in_vmem([blocks, partial, drift_speed, upwind_sign]),
                in_vmem(x_in),
                in_vmem(y_in),
            ],
            [vector_shape],
            flops=work * len(middle),
        )

        def last_step(cols, sources, rest, earlier, early, outs, scratch, last=last):
            blocks_ref, partial_ref = rest
            named = Outs()
            if last:
                named.gram = outs[0]
            else:
                named.packed, named.value = outs
            last_kernel(
                sizes, per_owner, final, cols[0], [[ref] for ref in sources], blocks_ref, partial_ref,
                earlier, named, early[0] if last else None,
            )

        if last:
            shapes = [shape_of((devices, 1, block), f32)]
        else:
            shapes = [packed_shape, vector_shape]
        results = call(
            "last_%d" % section,
            last_step,
            [
                in_vmem([columns]),
                in_vmem([sources[place] for place in final]),
                in_vmem([turned, partial]),
                in_vmem(vectors if last else []),
                in_vmem(early),
            ],
            shapes,
            flops=work * len(final),
        )
        if last:
            (gram,) = results
        else:
            packed, value = results
            vectors.append(value)
            spread = call(
                "spread_%d" % section,
                lambda ins, outs, scratch: spread_kernel(sizes, *ins, *split(outs)),
                [in_vmem([value, open_cells])],
                spread_shapes,
            )

    gram = lax.all_to_all(gram, AXES, 0, 0)

    def finish(ins, outs, scratch):
        finish_kernel(*ins, *outs)

    solution, hessenberg = call(
        "finish",
        finish,
        [in_vmem([gram, *vectors])],
        [vector_shape, shape_of((KRYLOV + 1, KRYLOV), f32)],
    )
    return solution.reshape(first, second, local_modes), hessenberg


def solution(mesh):
    return jax.shard_map(
        per_device,
        mesh=mesh,
        in_specs=(
            P("gx", "gy", "mode"),
            P("mode", None),
            P("mode", None, None, None),
            P("mode"),
            P(None, "mode"),
            P(None, "mode"),
            P("gx", "gy"),
        ),
        out_specs=(P("gx", "gy", "mode"), P()),
        check_vma=False,
    )
```

```python
import jax
import jax.numpy as jnp
from jax import lax
from jax.experimental import pallas as pl
from jax.experimental.pallas import tpu as pltpu
from jax.sharding import PartitionSpec as P

KRYLOV = 3
SHIFT = 4.05
AXES = ("mode", "gx", "gy")

epsilon = 1e-12


def moves_of(count):
    moves = []
    for first in (0, 1)[: count - 1]:
        partner = list(range(count))
        for low in range(first, count - 1, 2):
            partner[low], partner[low + 1] = low + 1, low
        moves.append(partner)
    return moves


def move_faces(faces):
    received = []
    shards = lax.axis_size("mode")
    for axis in ("gy", "gx"):
        count = lax.axis_size(axis)
        arrived = []
        for face, partner in zip(faces[axis], moves_of(count)):
            pairs = []
            for shard in range(shards):
                for at in range(count):
                    alone = partner[at] == at
                    other = (shard ^ 1 if alone and shards > 1 else shard) * count + partner[at]
                    pairs.append((shard * count + at, other))
            arrived.append(lax.ppermute(face, ("mode", axis), pairs))
        received.append(arrived)
    return received


def exchange(array, bit):
    count = lax.axis_size("mode")
    return lax.ppermute(array, "mode", [(i, i ^ bit) for i in range(count)])


def gather_far(packed):
    held = {0: packed}
    bit = lax.axis_size("mode") // 2
    while bit > 1:
        for key in list(held):
            held[key ^ bit] = exchange(held[key], bit)
        bit //= 2
    del held[0]
    return held


def spread_kernel(sizes, value_ref, open_ref, part_refs, x_refs, y_refs):
    first, second, local_blocks, block = sizes
    at = 0
    for ref in part_refs:
        rows = ref.shape[0]
        ref[...] = value_ref[at : at + rows, :].astype(jnp.bfloat16)
        at += rows
    for b in range(local_blocks):
        lanes = slice(b * block, (b + 1) * block)
        masked = (value_ref[:, lanes] * open_ref[...]).reshape(first, second, block)
        write_faces(masked, lanes, first, second, x_refs, y_refs)


def hand_on(arrays, after):
    count = len(arrays)
    if not count:
        return []
    return pl.pallas_call(
        lambda *refs: None,
        out_shape=[jax.ShapeDtypeStruct(array.shape, array.dtype) for array in arrays],
        in_specs=[ANY] * (count + len(after)),
        out_specs=[ANY] * count,
        input_output_aliases={at: at for at in range(count)},
        compiler_params=pltpu.CompilerParams(vmem_limit_bytes=SCOPED),
        name="hand_on",
    )(*arrays, *after)


def store_faces(refs, axis, lanes, low, high):
    even = lax.rem(lax.axis_index(axis), 2) == 0
    for ref, take_high in zip(refs, (even, jnp.logical_not(even))):
        ref[:, lanes] = jnp.where(take_high, high, low)


def write_faces(masked, lanes, first, second, x_refs, y_refs):
    store_faces(x_refs, "gx", lanes, masked[0], masked[first - 1])
    store_faces(y_refs, "gy", lanes, masked[:, 0, :], masked[:, second - 1, :])


def halos(refs, axis, lanes, shape):
    zero = jnp.zeros(shape, jnp.float32)
    if not refs:
        return zero, zero
    at = lax.axis_index(axis)
    odd = lax.rem(at, 2) == 1
    one, two = refs[0][:, lanes], refs[-1][:, lanes]
    low, high = jnp.where(odd, one, two), jnp.where(odd, two, one)
    return jnp.where(at == 0, zero, low), jnp.where(at == lax.axis_size(axis) - 1, zero, high)


def prepare_kernel(sizes, rhs_ref, wall_ref, part_refs, x_refs, y_refs, open_ref):
    first, second, local_blocks, block = sizes
    wall = wall_ref[...].astype(jnp.float32)
    eye = (
        lax.broadcasted_iota(jnp.int32, (second, second), 0)
        == lax.broadcasted_iota(jnp.int32, (second, second), 1)
    ).astype(jnp.float32)
    for row in range(first):
        column = jnp.sum(eye * (1.0 - wall[row : row + 1, :]), axis=1, keepdims=True)
        open_ref[row * second : (row + 1) * second, :] = jnp.broadcast_to(column, (second, block))
    spread_kernel(sizes, rhs_ref, open_ref, part_refs, x_refs, y_refs)


def scatter(sizes, per_owner, b, places, cols_ref, sources, blocks_ref, turned=False):
    first, second, local_blocks, block = sizes
    mine = lax.axis_index("mode")
    picks, weights = [], []
    for place, source in zip(places, sources):
        owner = mine ^ place
        for p in range(per_owner):
            slot = owner * per_owner + p
            column = cols_ref[slot, b] - owner * local_blocks
            lanes = pl.ds(pl.multiple_of(column * block, block), block)
            picks.append(jnp.concatenate([part[:, lanes] for part in source], axis=0))
            if not turned:
                weights.append(blocks_ref[b, slot])
    picks = jnp.concatenate(picks, axis=1)
    if turned:
        return jnp.dot(picks, blocks_ref[b], preferred_element_type=jnp.float32)
    return lax.dot_general(
        picks,
        jnp.concatenate(weights, axis=1),
        (((1,), (1,)), ((), ())),
        preferred_element_type=jnp.float32,
    )


def turn_blocks(per_owner, places, blocks_ref, turned_ref):
    block = blocks_ref.shape[2]
    mine = lax.axis_index("mode")
    for b in range(blocks_ref.shape[0]):
        at = 0
        for place in places:
            for p in range(per_owner):
                turned_ref[b, at : at + block, :] = blocks_ref[b, (mine ^ place) * per_owner + p].T
                at += block


def add_product(sums, key, left, right):
    cells, block = left.shape
    term = jnp.sum((left * right).reshape(cells // 8, 8, block), axis=0)
    sums[key] = sums[key] + term if key in sums else term


def lane_sum(value):
    return jnp.sum(jnp.sum(value, axis=0, keepdims=True), axis=1, keepdims=True)


def early_products(sizes, vectors, early_ref):
    first, second, local_blocks, block = sizes
    sums = {}
    for b in range(local_blocks):
        lanes = slice(b * block, (b + 1) * block)
        values = [ref[:, lanes] for ref in vectors]
        for i in range(len(values)):
            for j in range(i, len(values)):
                add_product(sums, (i, j), values[i], values[j])
    at = 0
    for i in range(len(vectors) + 1):
        for j in range(i, len(vectors) + 1):
            if j < len(vectors):
                early_ref[at : at + 1, :] = jnp.broadcast_to(lane_sum(sums[i, j]), (1, block))
            at += 1


def split_speeds(speed_ref, sign_ref, lanes):
    parts = []
    for axis in range(2):
        speed, sign = speed_ref[axis : axis + 1, lanes], sign_ref[axis : axis + 1, lanes]
        parts += [jnp.where(sign == 1, speed, 0.0), jnp.where(sign == 1, 0.0, speed)]
    return parts


def near_kernel(sizes, per_owner, places, cols_ref, sources, blocks_ref, current_ref, params, open_ref, out_ref, finer_ref=None):
    first, second, local_blocks, block = sizes
    cells = first * second
    open_cells = open_ref[...]
    row_at = lax.broadcasted_iota(jnp.int32, (first, second, block), 1)
    zero = jnp.zeros((1, second, block), jnp.float32)
    if finer_ref is not None:
        for b in range(local_blocks):
            lanes = slice(b * block, (b + 1) * block)
            rounded = sources[0][0][:, lanes].astype(jnp.float32)
            finer_ref[:, lanes] = (current_ref[:, lanes] - rounded).astype(jnp.bfloat16)
        places, sources = places + [0], sources + [[finer_ref]]
    for b in range(local_blocks):
        lanes = slice(b * block, (b + 1) * block)
        scattered = scatter(sizes, per_owner, b, places, cols_ref, sources, blocks_ref)
        current = current_ref[:, lanes]
        masked = (current * open_cells).reshape(first, second, block)
        relax_ref, speed_ref, sign_ref = params
        west, east, south, north = split_speeds(speed_ref, sign_ref, lanes)
        diagonal = relax_ref[lanes].reshape(1, block) + (west + east) + (south + north) - SHIFT
        from_west = jnp.concatenate([zero, masked[:-1]], axis=0)
        from_east = jnp.concatenate([masked[1:], zero], axis=0)
        from_south = jnp.where(row_at == 0, 0.0, pltpu.roll(masked, 1, axis=1))
        from_north = jnp.where(row_at == second - 1, 0.0, pltpu.roll(masked, second - 1, axis=1))
        drift = (
            west.reshape(1, 1, block) * from_west
            + east.reshape(1, 1, block) * from_east
            + south.reshape(1, 1, block) * from_south
            + north.reshape(1, 1, block) * from_north
        ).reshape(cells, block)
        out_ref[:, lanes] = diagonal * current - drift - scattered


def middle_kernel(sizes, per_owner, places, cols_ref, sources, blocks_ref, partial_ref, speed_ref, sign_ref, x_in, y_in, out_ref):
    first, second, local_blocks, block = sizes
    cells = first * second
    row_at = lax.broadcasted_iota(jnp.int32, (first, second, block), 1)
    for b in range(local_blocks):
        lanes = slice(b * block, (b + 1) * block)
        value = partial_ref[:, lanes]
        if places:
            value = value - scatter(sizes, per_owner, b, places, cols_ref, sources, blocks_ref)
        west, east, south, north = split_speeds(speed_ref, sign_ref, lanes)
        west_in, east_in = halos(x_in, "gx", lanes, (second, block))
        south_in, north_in = halos(y_in, "gy", lanes, (first, block))
        value = value.reshape(first, second, block)
        value = value - jnp.where(
            row_at == 0,
            (south * south_in)[:, None, :],
            jnp.where(row_at == second - 1, (north * north_in)[:, None, :], 0.0),
        )
        value = jnp.concatenate(
            [value[:1] - (west * west_in)[None], value[1:-1], value[-1:] - (east * east_in)[None]],
            axis=0,
        )
        out_ref[:, lanes] = value.reshape(cells, block)


def last_kernel(sizes, per_owner, places, cols_ref, sources, blocks_ref, partial_ref, earlier, outs, early_ref=None):
    first, second, local_blocks, block = sizes
    cells = first * second
    sums = {}
    for b in range(local_blocks):
        lanes = slice(b * block, (b + 1) * block)
        scattered = scatter(sizes, per_owner, b, places, cols_ref, sources, blocks_ref, True)
        result = partial_ref[:, lanes] - scattered
        if outs.gram is None:
            outs.value[:, lanes] = result
            outs.packed[:, lanes] = result.astype(jnp.bfloat16)
        else:
            vectors = [ref[:, lanes] for ref in earlier] + [result]
            for i, vector in enumerate(vectors):
                add_product(sums, (i, len(earlier)), vector, result)
    if outs.gram is not None:
        devices = outs.gram.shape[0]
        lane = lax.broadcasted_iota(jnp.int32, (1, block), 1)
        row = jnp.zeros((1, block), jnp.float32)
        size = len(earlier) + 1
        at = 0
        for i in range(size):
            for j in range(i, size):
                if j < size - 1:
                    total = early_ref[at : at + 1, :]
                else:
                    total = lane_sum(sums[i, j])
                row = jnp.where(lane == at, total, row)
                at += 1
        outs.gram[...] = jnp.broadcast_to(row[None], (devices, 1, block))


class Outs:
    value = packed = gram = None


def least_squares(hessenberg, initial):
    upper = [list(row) for row in hessenberg]
    target = [initial] + [jnp.zeros_like(initial) for row_index in range(KRYLOV)]
    cosines = []
    sines = []
    for col_index in range(KRYLOV):
        for row_index in range(col_index):
            first = upper[row_index][col_index]
            second = upper[row_index + 1][col_index]
            upper[row_index][col_index] = cosines[row_index] * first + sines[row_index] * second
            upper[row_index + 1][col_index] = cosines[row_index] * second - sines[row_index] * first
        first = upper[col_index][col_index]
        second = upper[col_index + 1][col_index]
        radius = jnp.sqrt(first * first + second * second)
        cosine = first / radius
        sine_value = second / radius
        upper[col_index][col_index] = radius
        target[col_index + 1] = -sine_value * target[col_index]
        target[col_index] = cosine * target[col_index]
        cosines.append(cosine)
        sines.append(sine_value)
    combo = [None] * KRYLOV
    for row_index in reversed(range(KRYLOV)):
        running = target[row_index]
        for col_index in range(row_index + 1, KRYLOV):
            running = running - upper[row_index][col_index] * combo[col_index]
        combo[row_index] = running / upper[row_index][row_index]
    return combo


def dot(left, right):
    terms = [a * b for a, b in zip(left, right)]
    while len(terms) > 1:
        terms = [sum(terms[at + 1 : at + 2], terms[at]) for at in range(0, len(terms), 2)]
    return terms[0]


def factor(gram):
    size = len(gram)
    rows = [[] for k in range(size)]
    for j in range(size):
        pivot = gram[j][j] - dot(rows[j], rows[j]) if j else gram[j][j]
        edge = jnp.sqrt(jnp.maximum(pivot, 0.0))
        inverse = jnp.where(edge > 1e-18, 1.0 / jnp.maximum(edge, 1e-18), 0.0)
        for k in range(j + 1, size):
            value = gram[j][k] - dot(rows[k], rows[j]) if j else gram[j][k]
            rows[k].append(value * inverse)
        rows[j].append(edge)
    return rows


def arnoldi(gram):
    rows = factor(gram)

    def coordinates(vector):
        return [
            dot(vector[i:], [rows[k][i] for k in range(i, len(vector))]) for i in range(len(vector))
        ]

    initial = jnp.sqrt(gram[0][0] + epsilon)
    basis = [[1.0 / initial]]
    places = [coordinates(basis[0])]
    zero = jnp.zeros_like(initial)
    hessenberg = [[zero] * KRYLOV for row_index in range(KRYLOV + 1)]
    for section in range(KRYLOV):
        vector = basis[section]
        shifted = [SHIFT * part for part in vector] + [zero]
        image = [shifted[0]] + [a + b for a, b in zip(vector, shifted[1:])]
        spot = coordinates(image)
        rest, rest_spot = list(image), list(spot)
        for earlier in range(section + 1):
            coefficient = dot(places[earlier], spot)
            hessenberg[earlier][section] = coefficient
            for k in range(earlier + 1):
                rest[k] = rest[k] - coefficient * basis[earlier][k]
                rest_spot[k] = rest_spot[k] - coefficient * places[earlier][k]
        length = jnp.sqrt(dot(rest_spot, rest_spot) + epsilon)
        hessenberg[section + 1][section] = length
        basis.append([part / length for part in rest])
        places.append([part / length for part in rest_spot])
    combo = least_squares(hessenberg, initial)
    weights = []
    for k in range(KRYLOV):
        total = zero
        for j in range(k, KRYLOV):
            total = total + combo[j] * basis[j][k]
        weights.append(total)
    return hessenberg, weights


def finish_kernel(gram_ref, *refs):
    vectors, (solution_ref, hessenberg_ref) = refs[:KRYLOV], refs[KRYLOV:]
    block = gram_ref.shape[2]
    total = jnp.sum(gram_ref[...], axis=0)
    lane = lax.broadcasted_iota(jnp.int32, (1, block), 1)
    gram = [[None] * (KRYLOV + 1) for i in range(KRYLOV + 1)]
    at = 0
    for i in range(KRYLOV + 1):
        for j in range(i, KRYLOV + 1):
            entry = jnp.sum(jnp.where(lane == at, total, 0.0), axis=1, keepdims=True)
            gram[i][j] = jnp.broadcast_to(entry, (1, block))
            at += 1
    hessenberg, weights = arnoldi(gram)
    rows = lax.broadcasted_iota(jnp.int32, (KRYLOV + 1, KRYLOV), 0)
    cols = lax.broadcasted_iota(jnp.int32, (KRYLOV + 1, KRYLOV), 1)
    table = jnp.zeros((KRYLOV + 1, KRYLOV), jnp.float32)
    for i in range(KRYLOV + 1):
        for j in range(KRYLOV):
            table = jnp.where((rows == i) & (cols == j), hessenberg[i][j][:, :KRYLOV], table)
    hessenberg_ref[...] = table
    for b in range(solution_ref.shape[1] // block):
        lanes = slice(b * block, (b + 1) * block)
        solution_ref[:, lanes] = sum(
            weight * ref[:, lanes] for weight, ref in zip(weights, vectors)
        )


VMEM = pl.BlockSpec(memory_space=pltpu.VMEM)
ANY = pl.BlockSpec(memory_space=pl.ANY)
SCOPED = 16 * 1024 * 1024


def call(name, kernel, groups, shapes, scratch=(), flops=0):
    flat = [pair for group in groups for pair in group]

    def body(*refs):
        refs = list(refs)
        lists = []
        for group in groups:
            lists.append(refs[: len(group)])
            del refs[: len(group)]
        kernel(*lists, refs[: len(shapes)], refs[len(shapes) :])

    size = sum(operand.size * operand.dtype.itemsize for spec, operand in flat)
    size += sum(shape.size * shape.dtype.itemsize for shape in shapes)
    return pl.pallas_call(
        body,
        out_shape=list(shapes),
        in_specs=[spec for spec, operand in flat],
        out_specs=[VMEM] * len(shapes),
        scratch_shapes=list(scratch),
        compiler_params=pltpu.CompilerParams(vmem_limit_bytes=SCOPED),
        cost_estimate=pl.CostEstimate(flops=flops, bytes_accessed=size, transcendentals=0),
        name=name,
    )(*[operand for spec, operand in flat])


def in_vmem(operands):
    return [(VMEM, operand) for operand in operands]


def per_device(right_side, col_block, blocks, relax_rate, drift_speed, upwind_sign, wall_mask):
    first, second, local_modes = right_side.shape
    local_blocks, slots, block = blocks.shape[:3]
    cells = first * second
    count = lax.axis_size("mode")
    devices = count * lax.axis_size("gx") * lax.axis_size("gy")
    per_owner = slots // count
    sizes = (first, second, local_blocks, block)
    x_moves, y_moves = len(moves_of(lax.axis_size("gx"))), len(moves_of(lax.axis_size("gy")))
    n_faces = x_moves + y_moves
    f32 = jnp.float32
    shape_of = jax.ShapeDtypeStruct
    face_shapes = [shape_of((second, local_modes), f32)] * x_moves + [
        shape_of((first, local_modes), f32)
    ] * y_moves
    parts = 2 if cells % 32 == 0 else 1
    packed_shape = shape_of((cells, local_modes), jnp.bfloat16)
    spread_shapes = [shape_of((cells // parts, local_modes), jnp.bfloat16)] * parts + face_shapes
    vector_shape = shape_of((cells, local_modes), f32)
    near = [place for place in (0, 1) if place < count]
    final = [place for place in range(3, count) if place % 2 == 1]
    middle = [place for place in range(2, count) if place not in final]

    start = right_side.reshape(cells, local_modes)

    def pack(ins, outs, scratch):
        outs[0][...] = ins[0][...].astype(jnp.bfloat16)

    (packed,) = call("pack", pack, [in_vmem([start])], [packed_shape], flops=8 * 10**9)

    def split(outs):
        faces = outs[parts:]
        return outs[:parts], faces[:x_moves], faces[x_moves:n_faces]

    def prepare(ins, outs, scratch):
        prepare_kernel(sizes, *ins, *split(outs), outs[-1])

    *spread, open_cells = call(
        "prepare",
        prepare,
        [in_vmem([start, wall_mask])],
        spread_shapes + [shape_of((cells, block), f32)],
        flops=1 * 10**9,
    )
    columns = col_block.T

    turned_shape = shape_of((local_blocks, len(final) * per_owner * block, block), blocks.dtype)
    work = 2 * cells * local_modes * per_owner * block
    vectors = [start]
    for section in range(KRYLOV):
        sources = {0: packed}
        held = gather_far(packed)
        halves, x_faces, y_faces = split(spread)
        neighbour = [exchange(part, 1) for part in halves] if count > 1 else []
        y_in, x_in = move_faces({"gx": x_faces, "gy": y_faces})

        last = section == KRYLOV - 1

        def near_step(cols, sources, rest, params, known, outs, scratch, section=section, last=last):
            sources = [sources[:1], sources[1:]][: len(near)]
            blocks_ref, current_ref, open_ref = rest
            near_kernel(
                sizes, per_owner, near, cols[0], sources, blocks_ref, current_ref, params,
                open_ref, outs[0], scratch[0] if section == 0 else None,
            )
            if section == 0:
                turn_blocks(per_owner, final, blocks_ref, outs[1])
            if last:
                early_products(sizes, known, outs[1])

        partial, *early = call(
            "near_%d" % section,
            near_step,
            [
                in_vmem([columns]),
                in_vmem([packed, *neighbour]),
                in_vmem([blocks, vectors[-1], open_cells]),
                in_vmem([relax_rate, drift_speed, upwind_sign]),
                in_vmem(vectors if last else []),
            ],
            [vector_shape] + [turned_shape] * (section == 0) + [shape_of((16, block), f32)] * last,
            [pltpu.VMEM((cells, local_modes), jnp.bfloat16)] * (section == 0),
            flops=work * len(near),
        )

        if section == 0:
            turned, *early = early
        held = dict(zip(held, hand_on(list(held.values()), [partial, *x_in, *y_in])))
        for place, array in held.items():
            sources[place] = array
            sources[place ^ 1] = exchange(array, 1)

        def middle_step(cols, sources, rest, x_in, y_in, outs, scratch):
            middle_kernel(
                sizes, per_owner, middle, cols[0], [[ref] for ref in sources], *rest, x_in, y_in, outs[0]
            )

        (partial,) = call(
            "middle_%d" % section,
            middle_step,
            [
                in_vmem([columns]),
                in_vmem([sources[place] for place in middle]),
                in_vmem([blocks, partial, drift_speed, upwind_sign]),
                in_vmem(x_in),
                in_vmem(y_in),
            ],
            [vector_shape],
            flops=work * len(middle),
        )

        def last_step(cols, sources, rest, earlier, early, outs, scratch, last=last):
            blocks_ref, partial_ref = rest
            named = Outs()
            if last:
                named.gram = outs[0]
            else:
                named.packed, named.value = outs
            last_kernel(
                sizes, per_owner, final, cols[0], [[ref] for ref in sources], blocks_ref, partial_ref,
                earlier, named, early[0] if last else None,
            )

        if last:
            shapes = [shape_of((devices, 1, block), f32)]
        else:
            shapes = [packed_shape, vector_shape]
        results = call(
            "last_%d" % section,
            last_step,
            [
                in_vmem([columns]),
                in_vmem([sources[place] for place in final]),
                in_vmem([turned, partial]),
                in_vmem(vectors if last else []),
                in_vmem(early),
            ],
            shapes,
            flops=work * len(final),
        )
        if last:
            (gram,) = results
        else:
            packed, value = results
            vectors.append(value)
            spread = call(
                "spread_%d" % section,
                lambda ins, outs, scratch: spread_kernel(sizes, *ins, *split(outs)),
                [in_vmem([value, open_cells])],
                spread_shapes,
            )

    gram = lax.all_to_all(gram, AXES, 0, 0)

    def finish(ins, outs, scratch):
        finish_kernel(*ins, *outs)

    solution, hessenberg = call(
        "finish",
        finish,
        [in_vmem([gram, *vectors])],
        [vector_shape, shape_of((KRYLOV + 1, KRYLOV), f32)],
    )
    return solution.reshape(first, second, local_modes), hessenberg


def solution(mesh):
    return jax.shard_map(
        per_device,
        mesh=mesh,
        in_specs=(
            P("gx", "gy", "mode"),
            P("mode", None),
            P("mode", None, None, None),
            P("mode"),
            P(None, "mode"),
            P(None, "mode"),
            P("gx", "gy"),
        ),
        out_specs=(P("gx", "gy", "mode"), P()),
        check_vma=False,
    )
```

```python
import jax
import jax.numpy as jnp
from jax import lax
from jax.experimental import pallas as pl
from jax.experimental.pallas import tpu as pltpu
from jax.sharding import PartitionSpec as P

KRYLOV = 3
SHIFT = 4.05
AXES = ("mode", "gx", "gy")

epsilon = 1e-12


def moves_of(count):
    moves = []
    for first in (0, 1)[: count - 1]:
        partner = list(range(count))
        for low in range(first, count - 1, 2):
            partner[low], partner[low + 1] = low + 1, low
        moves.append(partner)
    return moves


def move_faces(faces):
    received = []
    shards = lax.axis_size("mode")
    for axis in ("gy", "gx"):
        count = lax.axis_size(axis)
        arrived = []
        for face, partner in zip(faces[axis], moves_of(count)):
            pairs = []
            for shard in range(shards):
                for at in range(count):
                    alone = partner[at] == at
                    other = (shard ^ 1 if alone and shards > 1 else shard) * count + partner[at]
                    pairs.append((shard * count + at, other))
            arrived.append(lax.ppermute(face, ("mode", axis), pairs))
        received.append(arrived)
    return received


def exchange(array, bit):
    count = lax.axis_size("mode")
    return lax.ppermute(array, "mode", [(i, i ^ bit) for i in range(count)])


def gather_far(packed):
    held = {0: packed}
    bit = lax.axis_size("mode") // 2
    while bit > 1:
        for key in list(held):
            held[key ^ bit] = exchange(held[key], bit)
        bit //= 2
    del held[0]
    return held


def spread_kernel(sizes, value_ref, open_ref, part_refs, x_refs, y_refs):
    first, second, local_blocks, block = sizes
    at = 0
    for ref in part_refs:
        rows = ref.shape[0]
        ref[...] = value_ref[at : at + rows, :].astype(jnp.bfloat16)
        at += rows
    for b in range(local_blocks):
        lanes = slice(b * block, (b + 1) * block)
        masked = (value_ref[:, lanes] * open_ref[...]).reshape(first, second, block)
        write_faces(masked, lanes, first, second, x_refs, y_refs)


def hand_on(arrays, after):
    count = len(arrays)
    if not count:
        return []
    return pl.pallas_call(
        lambda *refs: None,
        out_shape=[jax.ShapeDtypeStruct(array.shape, array.dtype) for array in arrays],
        in_specs=[ANY] * (count + len(after)),
        out_specs=[ANY] * count,
        input_output_aliases={at: at for at in range(count)},
        compiler_params=pltpu.CompilerParams(vmem_limit_bytes=SCOPED),
        name="hand_on",
    )(*arrays, *after)


def store_faces(refs, axis, lanes, low, high):
    even = lax.rem(lax.axis_index(axis), 2) == 0
    for ref, take_high in zip(refs, (even, jnp.logical_not(even))):
        ref[:, lanes] = jnp.where(take_high, high, low)


def write_faces(masked, lanes, first, second, x_refs, y_refs):
    store_faces(x_refs, "gx", lanes, masked[0], masked[first - 1])
    store_faces(y_refs, "gy", lanes, masked[:, 0, :], masked[:, second - 1, :])


def halos(refs, axis, lanes, shape):
    zero = jnp.zeros(shape, jnp.float32)
    if not refs:
        return zero, zero
    at = lax.axis_index(axis)
    odd = lax.rem(at, 2) == 1
    one, two = refs[0][:, lanes], refs[-1][:, lanes]
    low, high = jnp.where(odd, one, two), jnp.where(odd, two, one)
    return jnp.where(at == 0, zero, low), jnp.where(at == lax.axis_size(axis) - 1, zero, high)


def prepare_kernel(sizes, rhs_ref, wall_ref, part_refs, x_refs, y_refs, open_ref):
    first, second, local_blocks, block = sizes
    wall = wall_ref[...].astype(jnp.float32)
    eye = (
        lax.broadcasted_iota(jnp.int32, (second, second), 0)
        == lax.broadcasted_iota(jnp.int32, (second, second), 1)
    ).astype(jnp.float32)
    for row in range(first):
        column = jnp.sum(eye * (1.0 - wall[row : row + 1, :]), axis=1, keepdims=True)
        open_ref[row * second : (row + 1) * second, :] = jnp.broadcast_to(column, (second, block))
    spread_kernel(sizes, rhs_ref, open_ref, part_refs, x_refs, y_refs)


def scatter(sizes, per_owner, b, places, cols_ref, sources, blocks_ref, turned=False):
    first, second, local_blocks, block = sizes
    mine = lax.axis_index("mode")
    picks, weights = [], []
    for place, source in zip(places, sources):
        owner = mine ^ place
        for p in range(per_owner):
            slot = owner * per_owner + p
            column = cols_ref[slot, b] - owner * local_blocks
            lanes = pl.ds(pl.multiple_of(column * block, block), block)
            picks.append(jnp.concatenate([part[:, lanes] for part in source], axis=0))
            if not turned:
                weights.append(blocks_ref[b, slot])
    picks = jnp.concatenate(picks, axis=1)
    if turned:
        return jnp.dot(picks, blocks_ref[b], preferred_element_type=jnp.float32)
    return lax.dot_general(
        picks,
        jnp.concatenate(weights, axis=1),
        (((1,), (1,)), ((), ())),
        preferred_element_type=jnp.float32,
    )


def turn_blocks(per_owner, places, blocks_ref, turned_ref):
    block = blocks_ref.shape[2]
    mine = lax.axis_index("mode")
    for b in range(blocks_ref.shape[0]):
        at = 0
        for place in places:
            for p in range(per_owner):
                turned_ref[b, at : at + block, :] = blocks_ref[b, (mine ^ place) * per_owner + p].T
                at += block


def add_product(sums, key, left, right):
    cells, block = left.shape
    term = jnp.sum((left * right).reshape(cells // 8, 8, block), axis=0)
    sums[key] = sums[key] + term if key in sums else term


def lane_sum(value):
    return jnp.sum(jnp.sum(value, axis=0, keepdims=True), axis=1, keepdims=True)


def early_products(sizes, vectors, early_ref):
    first, second, local_blocks, block = sizes
    sums = {}
    for b in range(local_blocks):
        lanes = slice(b * block, (b + 1) * block)
        values = [ref[:, lanes] for ref in vectors]
        for i in range(len(values)):
            for j in range(i, len(values)):
                add_product(sums, (i, j), values[i], values[j])
    at = 0
    for i in range(len(vectors) + 1):
        for j in range(i, len(vectors) + 1):
            if j < len(vectors):
                early_ref[at : at + 1, :] = jnp.broadcast_to(lane_sum(sums[i, j]), (1, block))
            at += 1


def split_speeds(speed_ref, sign_ref, lanes):
    parts = []
    for axis in range(2):
        speed, sign = speed_ref[axis : axis + 1, lanes], sign_ref[axis : axis + 1, lanes]
        parts += [jnp.where(sign == 1, speed, 0.0), jnp.where(sign == 1, 0.0, speed)]
    return parts


def near_kernel(sizes, per_owner, places, cols_ref, sources, blocks_ref, current_ref, params, open_ref, out_ref, finer_ref=None):
    first, second, local_blocks, block = sizes
    cells = first * second
    open_cells = open_ref[...]
    row_at = lax.broadcasted_iota(jnp.int32, (first, second, block), 1)
    zero = jnp.zeros((1, second, block), jnp.float32)
    if finer_ref is not None:
        for b in range(local_blocks):
            lanes = slice(b * block, (b + 1) * block)
            rounded = sources[0][0][:, lanes].astype(jnp.float32)
            finer_ref[:, lanes] = (current_ref[:, lanes] - rounded).astype(jnp.bfloat16)
        places, sources = places + [0], sources + [[finer_ref]]
    for b in range(local_blocks):
        lanes = slice(b * block, (b + 1) * block)
        scattered = scatter(sizes, per_owner, b, places, cols_ref, sources, blocks_ref)
        current = current_ref[:, lanes]
        masked = (current * open_cells).reshape(first, second, block)
        relax_ref, speed_ref, sign_ref = params
        west, east, south, north = split_speeds(speed_ref, sign_ref, lanes)
        diagonal = relax_ref[lanes].reshape(1, block) + (west + east) + (south + north) - SHIFT
        from_west = jnp.concatenate([zero, masked[:-1]], axis=0)
        from_east = jnp.concatenate([masked[1:], zero], axis=0)
        from_south = jnp.where(row_at == 0, 0.0, pltpu.roll(masked, 1, axis=1))
        from_north = jnp.where(row_at == second - 1, 0.0, pltpu.roll(masked, second - 1, axis=1))
        drift = (
            west.reshape(1, 1, block) * from_west
            + east.reshape(1, 1, block) * from_east
            + south.reshape(1, 1, block) * from_south
            + north.reshape(1, 1, block) * from_north
        ).reshape(cells, block)
        out_ref[:, lanes] = diagonal * current - drift - scattered


def middle_kernel(sizes, per_owner, places, cols_ref, sources, blocks_ref, partial_ref, speed_ref, sign_ref, x_in, y_in, out_ref):
    first, second, local_blocks, block = sizes
    cells = first * second
    row_at = lax.broadcasted_iota(jnp.int32, (first, second, block), 1)
    for b in range(local_blocks):
        lanes = slice(b * block, (b + 1) * block)
        value = partial_ref[:, lanes]
        if places:
            value = value - scatter(sizes, per_owner, b, places, cols_ref, sources, blocks_ref)
        west, east, south, north = split_speeds(speed_ref, sign_ref, lanes)
        west_in, east_in = halos(x_in, "gx", lanes, (second, block))
        south_in, north_in = halos(y_in, "gy", lanes, (first, block))
        value = value.reshape(first, second, block)
        value = value - jnp.where(
            row_at == 0,
            (south * south_in)[:, None, :],
            jnp.where(row_at == second - 1, (north * north_in)[:, None, :], 0.0),
        )
        value = jnp.concatenate(
            [value[:1] - (west * west_in)[None], value[1:-1], value[-1:] - (east * east_in)[None]],
            axis=0,
        )
        out_ref[:, lanes] = value.reshape(cells, block)


def last_kernel(sizes, per_owner, places, cols_ref, sources, blocks_ref, partial_ref, earlier, outs, early_ref=None):
    first, second, local_blocks, block = sizes
    cells = first * second
    sums = {}
    for b in range(local_blocks):
        lanes = slice(b * block, (b + 1) * block)
        scattered = scatter(sizes, per_owner, b, places, cols_ref, sources, blocks_ref, True)
        result = partial_ref[:, lanes] - scattered
        if outs.gram is None:
            outs.value[:, lanes] = result
            outs.packed[:, lanes] = result.astype(jnp.bfloat16)
        else:
            vectors = [ref[:, lanes] for ref in earlier] + [result]
            for i, vector in enumerate(vectors):
                add_product(sums, (i, len(earlier)), vector, result)
    if outs.gram is not None:
        devices = outs.gram.shape[0]
        lane = lax.broadcasted_iota(jnp.int32, (1, block), 1)
        row = jnp.zeros((1, block), jnp.float32)
        size = len(earlier) + 1
        at = 0
        for i in range(size):
            for j in range(i, size):
                if j < size - 1:
                    total = early_ref[at : at + 1, :]
                else:
                    total = lane_sum(sums[i, j])
                row = jnp.where(lane == at, total, row)
                at += 1
        outs.gram[...] = jnp.broadcast_to(row[None], (devices, 1, block))


class Outs:
    value = packed = gram = None


def least_squares(hessenberg, initial):
    upper = [list(row) for row in hessenberg]
    target = [initial] + [jnp.zeros_like(initial) for row_index in range(KRYLOV)]
    cosines = []
    sines = []
    for col_index in range(KRYLOV):
        for row_index in range(col_index):
            first = upper[row_index][col_index]
            second = upper[row_index + 1][col_index]
            upper[row_index][col_index] = cosines[row_index] * first + sines[row_index] * second
            upper[row_index + 1][col_index] = cosines[row_index] * second - sines[row_index] * first
        first = upper[col_index][col_index]
        second = upper[col_index + 1][col_index]
        radius = jnp.sqrt(first * first + second * second)
        cosine = first / radius
        sine_value = second / radius
        upper[col_index][col_index] = radius
        target[col_index + 1] = -sine_value * target[col_index]
        target[col_index] = cosine * target[col_index]
        cosines.append(cosine)
        sines.append(sine_value)
    combo = [None] * KRYLOV
    for row_index in reversed(range(KRYLOV)):
        running = target[row_index]
        for col_index in range(row_index + 1, KRYLOV):
            running = running - upper[row_index][col_index] * combo[col_index]
        combo[row_index] = running / upper[row_index][row_index]
    return combo


def arnoldi(gram):
    size = KRYLOV + 1

    def dot(left, right):
        terms = [a * b for a, b in zip(left, right) if a is not None and b is not None]
        while len(terms) > 1:
            terms = [sum(terms[at + 1 : at + 2], terms[at]) for at in range(0, len(terms), 2)]
        return terms[0]

    def times_gram(vector):
        return [dot([gram[min(i, j)][max(i, j)] for j in range(size)], vector) for i in range(size)]

    initial = jnp.sqrt(gram[0][0] + epsilon)
    basis = [[1.0 / initial] + [None] * KRYLOV]
    zero = jnp.zeros_like(initial)
    hessenberg = [[zero] * KRYLOV for row_index in range(size)]
    for section in range(KRYLOV):
        vector = basis[section]
        image = [None] * size
        for k in range(section + 2):
            parts = []
            if k > 0 and vector[k - 1] is not None:
                parts.append(vector[k - 1])
            if vector[k] is not None:
                parts.append(SHIFT * vector[k])
            image[k] = sum(parts[1:], parts[0])
        rest = list(image)
        products = times_gram(image)
        for earlier in range(section + 1):
            coefficient = dot(basis[earlier], products)
            hessenberg[earlier][section] = coefficient
            for k in range(earlier + 1):
                rest[k] = rest[k] - coefficient * basis[earlier][k]
        length = jnp.sqrt(jnp.maximum(dot(rest, times_gram(rest)), 0.0) + epsilon)
        hessenberg[section + 1][section] = length
        basis.append([None if part is None else part / length for part in rest])
    combo = least_squares(hessenberg, initial)
    weights = []
    for k in range(KRYLOV):
        total = zero
        for j in range(k, KRYLOV):
            total = total + combo[j] * basis[j][k]
        weights.append(total)
    return hessenberg, weights


def finish_kernel(gram_ref, *refs):
    vectors, (solution_ref, hessenberg_ref) = refs[:KRYLOV], refs[KRYLOV:]
    block = gram_ref.shape[2]
    total = gram_ref[...]
    while total.shape[0] % 2 == 0:
        middle = total.shape[0] // 2
        total = total[:middle] + total[middle:]
    total = jnp.sum(total, axis=0)
    lane = lax.broadcasted_iota(jnp.int32, (1, block), 1)
    gram = [[None] * (KRYLOV + 1) for i in range(KRYLOV + 1)]
    at = 0
    for i in range(KRYLOV + 1):
        for j in range(i, KRYLOV + 1):
            entry = jnp.sum(jnp.where(lane == at, total, 0.0), axis=1, keepdims=True)
            gram[i][j] = jnp.broadcast_to(entry, (1, block))
            at += 1
    hessenberg, weights = arnoldi(gram)
    rows = lax.broadcasted_iota(jnp.int32, (KRYLOV + 1, KRYLOV), 0)
    cols = lax.broadcasted_iota(jnp.int32, (KRYLOV + 1, KRYLOV), 1)
    table = jnp.zeros((KRYLOV + 1, KRYLOV), jnp.float32)
    for i in range(KRYLOV + 1):
        for j in range(KRYLOV):
            table = jnp.where((rows == i) & (cols == j), hessenberg[i][j][:, :KRYLOV], table)
    hessenberg_ref[...] = table
    for b in range(solution_ref.shape[1] // block):
        lanes = slice(b * block, (b + 1) * block)
        solution_ref[:, lanes] = sum(
            weight * ref[:, lanes] for weight, ref in zip(weights, vectors)
        )


VMEM = pl.BlockSpec(memory_space=pltpu.VMEM)
ANY = pl.BlockSpec(memory_space=pl.ANY)
SCOPED = 16 * 1024 * 1024


def call(name, kernel, groups, shapes, scratch=(), flops=0):
    flat = [pair for group in groups for pair in group]

    def body(*refs):
        refs = list(refs)
        lists = []
        for group in groups:
            lists.append(refs[: len(group)])
            del refs[: len(group)]
        kernel(*lists, refs[: len(shapes)], refs[len(shapes) :])

    size = sum(operand.size * operand.dtype.itemsize for spec, operand in flat)
    size += sum(shape.size * shape.dtype.itemsize for shape in shapes)
    return pl.pallas_call(
        body,
        out_shape=list(shapes),
        in_specs=[spec for spec, operand in flat],
        out_specs=[VMEM] * len(shapes),
        scratch_shapes=list(scratch),
        compiler_params=pltpu.CompilerParams(vmem_limit_bytes=SCOPED),
        cost_estimate=pl.CostEstimate(flops=flops, bytes_accessed=size, transcendentals=0),
        name=name,
    )(*[operand for spec, operand in flat])


def in_vmem(operands):
    return [(VMEM, operand) for operand in operands]


def per_device(right_side, col_block, blocks, relax_rate, drift_speed, upwind_sign, wall_mask):
    first, second, local_modes = right_side.shape
    local_blocks, slots, block = blocks.shape[:3]
    cells = first * second
    count = lax.axis_size("mode")
    devices = count * lax.axis_size("gx") * lax.axis_size("gy")
    per_owner = slots // count
    sizes = (first, second, local_blocks, block)
    x_moves, y_moves = len(moves_of(lax.axis_size("gx"))), len(moves_of(lax.axis_size("gy")))
    n_faces = x_moves + y_moves
    f32 = jnp.float32
    shape_of = jax.ShapeDtypeStruct
    face_shapes = [shape_of((second, local_modes), f32)] * x_moves + [
        shape_of((first, local_modes), f32)
    ] * y_moves
    parts = 2 if cells % 32 == 0 else 1
    packed_shape = shape_of((cells, local_modes), jnp.bfloat16)
    spread_shapes = [shape_of((cells // parts, local_modes), jnp.bfloat16)] * parts + face_shapes
    vector_shape = shape_of((cells, local_modes), f32)
    near = [place for place in (0, 1) if place < count]
    final = [place for place in range(3, count) if place % 2 == 1]
    middle = [place for place in range(2, count) if place not in final]

    start = right_side.reshape(cells, local_modes)

    def pack(ins, outs, scratch):
        outs[0][...] = ins[0][...].astype(jnp.bfloat16)

    (packed,) = call("pack", pack, [in_vmem([start])], [packed_shape], flops=8 * 10**9)

    def split(outs):
        faces = outs[parts:]
        return outs[:parts], faces[:x_moves], faces[x_moves:n_faces]

    def prepare(ins, outs, scratch):
        prepare_kernel(sizes, *ins, *split(outs), outs[-1])

    *spread, open_cells = call(
        "prepare",
        prepare,
        [in_vmem([start, wall_mask])],
        spread_shapes + [shape_of((cells, block), f32)],
        flops=1 * 10**9,
    )
    columns = col_block.T

    turned_shape = shape_of((local_blocks, len(final) * per_owner * block, block), blocks.dtype)
    work = 2 * cells * local_modes * per_owner * block
    vectors = [start]
    for section in range(KRYLOV):
        sources = {0: packed}
        held = gather_far(packed)
        halves, x_faces, y_faces = split(spread)
        neighbour = [exchange(part, 1) for part in halves] if count > 1 else []
        y_in, x_in = move_faces({"gx": x_faces, "gy": y_faces})

        last = section == KRYLOV - 1

        def near_step(cols, sources, rest, params, known, outs, scratch, section=section, last=last):
            sources = [sources[:1], sources[1:]][: len(near)]
            blocks_ref, current_ref, open_ref = rest
            near_kernel(
                sizes, per_owner, near, cols[0], sources, blocks_ref, current_ref, params,
                open_ref, outs[0], scratch[0] if section == 0 else None,
            )
            if section == 0:
                turn_blocks(per_owner, final, blocks_ref, outs[1])
            if last:
                early_products(sizes, known, outs[1])

        partial, *early = call(
            "near_%d" % section,
            near_step,
            [
                in_vmem([columns]),
                in_vmem([packed, *neighbour]),
                in_vmem([blocks, vectors[-1], open_cells]),
                in_vmem([relax_rate, drift_speed, upwind_sign]),
                in_vmem(vectors if last else []),
            ],
            [vector_shape] + [turned_shape] * (section == 0) + [shape_of((16, block), f32)] * last,
            [pltpu.VMEM((cells, local_modes), jnp.bfloat16)] * (section == 0),
            flops=work * len(near),
        )

        if section == 0:
            turned, *early = early
        held = dict(zip(held, hand_on(list(held.values()), [partial, *x_in, *y_in])))
        for place, array in held.items():
            sources[place] = array
            sources[place ^ 1] = exchange(array, 1)

        def middle_step(cols, sources, rest, x_in, y_in, outs, scratch):
            middle_kernel(
                sizes, per_owner, middle, cols[0], [[ref] for ref in sources], *rest, x_in, y_in, outs[0]
            )

        (partial,) = call(
            "middle_%d" % section,
            middle_step,
            [
                in_vmem([columns]),
                in_vmem([sources[place] for place in middle]),
                in_vmem([blocks, partial, drift_speed, upwind_sign]),
                in_vmem(x_in),
                in_vmem(y_in),
            ],
            [vector_shape],
            flops=work * len(middle),
        )

        def last_step(cols, sources, rest, earlier, early, outs, scratch, last=last):
            blocks_ref, partial_ref = rest
            named = Outs()
            if last:
                named.gram = outs[0]
            else:
                named.packed, named.value = outs
            last_kernel(
                sizes, per_owner, final, cols[0], [[ref] for ref in sources], blocks_ref, partial_ref,
                earlier, named, early[0] if last else None,
            )

        if last:
            shapes = [shape_of((devices, 1, block), f32)]
        else:
            shapes = [packed_shape, vector_shape]
        results = call(
            "last_%d" % section,
            last_step,
            [
                in_vmem([columns]),
                in_vmem([sources[place] for place in final]),
                in_vmem([turned, partial]),
                in_vmem(vectors if last else []),
                in_vmem(early),
            ],
            shapes,
            flops=work * len(final),
        )
        if last:
            (gram,) = results
        else:
            packed, value = results
            vectors.append(value)
            spread = call(
                "spread_%d" % section,
                lambda ins, outs, scratch: spread_kernel(sizes, *ins, *split(outs)),
                [in_vmem([value, open_cells])],
                spread_shapes,
            )

    gram = lax.all_to_all(gram, AXES, 0, 0)

    def finish(ins, outs, scratch):
        finish_kernel(*ins, *outs)

    solution, hessenberg = call(
        "finish",
        finish,
        [in_vmem([gram, *vectors])],
        [vector_shape, shape_of((KRYLOV + 1, KRYLOV), f32)],
    )
    return solution.reshape(first, second, local_modes), hessenberg


def solution(mesh):
    return jax.shard_map(
        per_device,
        mesh=mesh,
        in_specs=(
            P("gx", "gy", "mode"),
            P("mode", None),
            P("mode", None, None, None),
            P("mode"),
            P(None, "mode"),
            P(None, "mode"),
            P("gx", "gy"),
        ),
        out_specs=(P("gx", "gy", "mode"), P()),
        check_vma=False,
    )
```
